32 devices in a mesh: dp: 8 (over z, x), tensor: 4 (over y, core).
Axes of the slice: x: 2, y: 2, z: 4, core: 2. Of those that a mesh axis runs over, the one named last changes fastest.
Arguments:
- tokens: bfloat16 [4096, 2048], P(('dp', 'tensor')), may hold values from -6 to 6
- norm_gain1: float32 [2048], P(('dp', 'tensor')), may hold values from 0.5 to 1.5
- norm_gain2: float32 [2048], P(('dp', 'tensor')), may hold values from 0.5 to 1.5
- att_router: float32 [2048, 4], P(('dp', 'tensor')), may hold values from -0.09375 to 0.09375
- query_maps: float32 [4, 2048, 2048], P(None, 'dp', 'tensor'), may hold values from -0.125 to 0.125
- kv_maps: float32 [2, 2048, 2048], P(None, 'dp', 'tensor'), may hold values from -0.125 to 0.125
- out_maps: float32 [4, 2048, 2048], P(None, 'dp', 'tensor'), may hold values from -0.5 to 0.5
- ffn_router: float32 [2048, 4], P(('dp', 'tensor')), may hold values from -0.09375 to 0.09375
- ffn_maps: float32 [12, 2048, 5632], P(None, 'dp', 'tensor'), may hold values from -0.125 to 0.125
- att_route: int32 [4096, 2], P('dp'), may hold values from 0 to 3, all different within a row; in each aligned block of 512 rows (0 to 511, 512 to 1023, ...) at most 352 rows name the same one
- ffn_route: int32 [4096, 2], P('dp'), may hold values from 0 to 3, all different within a row; in each aligned block of 512 rows (0 to 511, 512 to 1023, ...) at most 352 rows name the same one
- parents: int32 [32], P('dp'), may hold values from 0 to 2, as said below
- cotangent: bfloat16 [4096, 2048], P(('dp', 'tensor')), may hold values from -6 to 6
Outputs:
- mixed: bfloat16 [4096, 2048], P(('dp', 'tensor'))
- input_grad: bfloat16 [4096, 2048], P(('dp', 'tensor'))
- gain1_grad: float32 [2048], P(('dp', 'tensor'))
- gain2_grad: float32 [2048], P(('dp', 'tensor'))
- att_router_grad: float32 [2048, 4], P(('dp', 'tensor'))
- query_grad: float32 [4, 2048, 2048], P(None, 'dp', 'tensor')
- kv_grad: float32 [2, 2048, 2048], P(None, 'dp', 'tensor')
- out_grad: float32 [4, 2048, 2048], P(None, 'dp', 'tensor')
- ffn_router_grad: float32 [2048, 4], P(('dp', 'tensor'))
- ffn_grad: float32 [12, 2048, 5632], P(None, 'dp', 'tensor')
The draws below stay inside these ranges and needn't reach their ends.
Inputs may be any that keep to these rules, and one draw needn't show every extreme that they name: `parents`: within each tree segment 0 has entry 0; every other segment's parent is an earlier segment of the same tree, and the last segment's parent is the one just before it. `att_route`: each row names two different experts; among the 512 rows of one tree no expert is named by more than 352 rows, a bound that some block reaches. `ffn_route`: each row names two different experts; among the 512 rows of one tree no expert is named by more than 352 rows, a bound that some block reaches.
All inputs are finite; a program needn't handle non-finite values.
Results may differ from the reference program's by a relative error of at most 0.02.
Values may be sent and summed in bfloat16 or wider, within the bound.
No kernel may reach another device: no remote copies, remote signals or barrier semaphores. Data moves between devices by JAX's collectives and lax.ppermute only.
A program may use at most 576 MiB of HBM per device.

```python
import math
import jax
import jax.numpy as jnp
import numpy as np
from jax import lax

D = 2048
KVH = 16
HS = 128
FF = 5632
EA = 4
EF = 4
TOPK = 2
SEG = 128
HD = 2048
GROUP = 512
TREES = 8
TOKENS = 4096
NSEG = 4
CAP_A = 352
CAP_F = 352


def draw_parents(key, part):
    key = jax.random.fold_in(key, 11)
    segment = jnp.arange(NSEG, dtype=jnp.int32)
    random_bits = jax.random.randint(key, (TREES, NSEG), 0, 1 << 20, dtype=jnp.int32)
    parent_pick = random_bits % jnp.maximum(segment, 1)[None, :]
    parent_pick = jnp.where(segment[None, :] == NSEG - 1, NSEG - 2, parent_pick)
    return parent_pick.reshape(-1).astype(jnp.int32)


def raised(values, stream_key, source, target, blocks, factor):
    owner, partner = [(jnp.arange(values.shape[dim]) // (values.shape[dim] // blocks)).reshape([-1 if axis == dim else 1 for axis in range(values.ndim)]) for dim in (source, target)]
    chosen = jax.random.permutation(stream_key, blocks)[partner]
    strong = (owner == chosen) | (owner == (partner + blocks // 2) % blocks)
    return jnp.where(strong, factor * values, values)


def steps_of(rng, dims, cuts, smallest, largest):
    def one(dim, shards_of):
        steps = jax.random.uniform(jax.random.fold_in(jax.random.fold_in(rng, 6), dim), (shards_of,), jnp.float32, smallest / len(cuts), largest / len(cuts))
        return jnp.repeat(jnp.exp(steps), dims[dim] // shards_of).reshape((-1,) + (1,) * (len(dims) - dim - 1))

    loudness = one(*cuts[0])
    for cut in cuts[1:]:
        loudness = loudness * one(*cut)
    return loudness


def deal_out(stream_key, own, number, rows, count, top, limit, skew):
    ranking = jax.random.permutation(stream_key, count)
    crowded, common = shares(count, rows * top, limit, skew, True), shares(count, rows * top, limit, skew, False)
    places = jnp.arange(count)

    def named(sizes, rotation):
        used = int((sizes > 0).sum())
        fixed = max(1, used // 4)
        shifted = fixed + (places - fixed + rotation * (used - fixed)) % max(1, count - fixed)
        return jnp.zeros((count,), jnp.int32).at[ranking[jnp.where(places < fixed, places, shifted)]].set(jnp.asarray(sizes, jnp.int32))

    sizes = jnp.where(number % 4 == 0, named(crowded, number // 4), named(common, number - number // 4 - 1))
    mixed = jax.random.permutation(jax.random.fold_in(own, 3), count)
    giver, receiver = mixed[0:count // 2 * 2:2], mixed[1:count // 2 * 2:2]
    slack = jnp.minimum(sizes[giver] - 1, limit - sizes[receiver]) // 2
    slack = jnp.where((giver == ranking[0]) | (receiver == ranking[0]) | (sizes[receiver] == 0), 0, jnp.maximum(slack, 0))
    shifted = jax.random.randint(jax.random.fold_in(own, 4), (count // 2,), 0, 1 << 20) % (slack + 1)
    sizes = sizes.at[giver].add(-shifted).at[receiver].add(shifted)
    labels = jnp.searchsorted(jnp.cumsum(sizes), jnp.arange(rows * top), side="right").astype(jnp.int32)
    listing = labels.reshape(top, rows).T
    listing = listing[jax.random.permutation(jax.random.fold_in(own, 1), rows)]
    rotation = jax.random.randint(jax.random.fold_in(own, 2), (rows, 1), 0, top)
    return jnp.take_along_axis(listing, (jnp.arange(top)[None, :] + rotation) % top, axis=1)


def shares(number_of, total, reach, skew, full):
    weights = [(1 << 20) // math.isqrt(grade ** skew) + 1 for grade in range(1, number_of + 1)]
    largest = reach if full else min(reach, max(-(-total // number_of), total * weights[0] // sum(weights)))
    least = 1 if total - largest >= number_of - 1 else 0
    given, rest = [largest] + [least] * (number_of - 1), total - largest - least * (number_of - 1)
    while rest > 0:
        movable = [i for i in range(1, number_of) if given[i] < largest] or [i for i in range(1, number_of) if given[i] < reach]
        mass, left = sum([weights[i] for i in movable]), rest
        for i in movable:
            extra = min(reach - given[i], max(1, left * weights[i] // mass), rest)
            given[i] = given[i] + extra
            rest = rest - extra
    return np.array(given)


def gaussian(rng, shape, spread, reach, shards=(), kind=jnp.bfloat16):
    loudness = steps_of(rng, shape, shards, -0.22, 0.18) if shards else 1.0
    entries = jax.random.normal(rng, shape, jnp.float32) * spread * loudness
    return jnp.minimum(jnp.maximum(entries, -reach), reach).astype(kind)


def heavy_noise(rng, extent, width, bound, cuts, heavy, kind=jnp.bfloat16):
    array = width * jax.random.normal(rng, extent, jnp.float32)
    if cuts:
        array = array * steps_of(rng, extent, cuts, -0.22, 0.18)
    return jnp.clip(raised(array, jax.random.fold_in(rng, 3), *heavy), -bound, bound).astype(kind)


def setup_inputs(seed: int = 0) -> dict:
    streams_of = jax.random.split(jax.random.key(seed), 14)
    tokens = gaussian(streams_of[0], (TOKENS, D), 1.0, 6.0, ((0, 32),))
    norm_gain1 = jnp.clip(1.0 + 0.1 * jax.random.normal(streams_of[1], (D,), jnp.float32), 0.5, 1.5)
    norm_gain2 = jnp.clip(1.0 + 0.1 * jax.random.normal(streams_of[2], (D,), jnp.float32), 0.5, 1.5)
    att_router = gaussian(streams_of[3], (D, EA), (2 * D) ** -0.5, 0.09375, ((0, 32),), jnp.float32)
    query_maps = gaussian(streams_of[4], (EA, D, HD), D ** -0.5, 0.125, ((1, 8), (2, 4)), jnp.float32)
    kv_maps = gaussian(streams_of[5], (2, D, HD), D ** -0.5, 0.125, ((1, 8), (2, 4)), jnp.float32)
    out_maps = gaussian(streams_of[6], (EA, D, HD), HS ** -0.5, 0.5, ((1, 8), (2, 4)), jnp.float32)
    ffn_router = gaussian(streams_of[7], (D, EF), (2 * D) ** -0.5, 0.09375, ((0, 32),), jnp.float32)
    ffn_maps = gaussian(streams_of[8], (3 * EF, D, FF), D ** -0.5, 0.125, ((1, 8), (2, 4)), jnp.float32)
    att_route_keys = jax.random.split(jax.random.fold_in(streams_of[9], 1), TOKENS // GROUP)
    att_route_turns = jax.random.permutation(jax.random.fold_in(streams_of[9], 3), TOKENS // GROUP)
    att_route = jax.vmap(lambda own, number: deal_out(jax.random.fold_in(streams_of[9], 2), own, number, GROUP, EA, TOPK, CAP_A, 1))(att_route_keys, att_route_turns).reshape((TOKENS, TOPK))
    ffn_route_keys = jax.random.split(jax.random.fold_in(streams_of[10], 1), TOKENS // GROUP)
    ffn_route_turns = jax.random.permutation(jax.random.fold_in(streams_of[10], 3), TOKENS // GROUP)
    ffn_route = jax.vmap(lambda own, number: deal_out(jax.random.fold_in(streams_of[10], 2), own, number, GROUP, EF, TOPK, CAP_F, 1))(ffn_route_keys, ffn_route_turns).reshape((TOKENS, TOPK))
    parents = draw_parents(jax.random.fold_in(streams_of[13], 71), 0)
    cotangent = heavy_noise(streams_of[12], (TOKENS, D), 1.0, 6.0, ((0, 32),), (0, 1, 32, 2.75))
    return {"tokens": tokens, "norm_gain1": norm_gain1, "norm_gain2": norm_gain2, "att_router": att_router, "query_maps": query_maps, "kv_maps": kv_maps, "out_maps": out_maps, "ffn_router": ffn_router, "ffn_maps": ffn_maps, "att_route": att_route, "ffn_route": ffn_route, "parents": parents, "cotangent": cotangent}


epsilon = 1e-05
rope_base = 10000.0
highest = lax.Precision.HIGHEST

@jax.custom_vjp
def low(v):
    return lax.optimization_barrier(v.astype(jnp.bfloat16)).astype(jnp.float32)

@jax.custom_vjp
def low_back(v):
    return v

def low_keep(v):
    return (low(v), None)

def low_pass(kept, grad):
    return (grad,)

def back_keep(v):
    return (v, None)

def back_low(kept, grad):
    return (low(grad),)
low.defvjp(low_keep, low_pass)
low_back.defvjp(back_keep, back_low)

def tree_tables(parent_row):
    segment = jnp.arange(NSEG, dtype=jnp.int32)
    parent_row = parent_row.astype(jnp.int32)

    def climb(depth_step, carried):
        reached, current = carried
        current = jnp.where(current > 0, parent_row[current], jnp.zeros_like(current)).astype(jnp.int32)
        return (reached | (current[:, None] == segment[None, :]), current)
    reached, current = lax.fori_loop(0, NSEG, climb, (segment[:, None] == segment[None, :], segment))
    depth_count = lax.optimization_barrier(jnp.sum(reached.astype(jnp.float32), axis=1)) - 1.0
    offsets = jnp.arange(SEG, dtype=jnp.float32)
    positions = (depth_count[:, None] * SEG + offsets[None, :]).reshape(-1)
    ancestor = jnp.repeat(jnp.repeat(reached, SEG, axis=0), SEG, axis=1)
    token_order = jnp.arange(GROUP, dtype=jnp.int32)
    return (positions, ancestor & (token_order[None, :] <= token_order[:, None]))

def rope_tables(positions):
    half_size = HS // 2
    frequency = rope_base ** (-2.0 * jnp.arange(half_size, dtype=jnp.float32) / HS)
    angles = positions[:, None] * frequency[None, :]
    cosines = jnp.cos(angles)
    sines = jnp.sin(angles)
    return (jnp.concatenate([cosines, cosines], axis=-1), jnp.concatenate([sines, sines], axis=-1))

def rotate(vectors, cosines, sines):
    half_size = vectors.shape[-1] // 2
    turned = jnp.concatenate([-vectors[..., half_size:], vectors[..., :half_size]], axis=-1)
    return vectors * cosines + turned * sines

def pick_gates(normed, router, chosen_map):
    logits = jnp.dot(normed, router, precision=highest)
    chosen = jnp.einsum('tse,te->ts', chosen_map, logits, precision=highest)
    row_max = lax.optimization_barrier(jnp.max(chosen, axis=-1, keepdims=True))
    exponent = jnp.exp(chosen - row_max)
    return exponent / lax.optimization_barrier(jnp.sum(exponent, axis=-1, keepdims=True))

def tree_attention(pieces):
    queries, keys_tree, values_tree, allowed = pieces
    scores = low_back(jnp.einsum('qshd,khd->shqk', queries, keys_tree, precision=highest) * HS ** (-0.5))
    scores = jnp.where(allowed[None, None], scores, -1e+30)
    row_max = lax.optimization_barrier(jnp.max(scores, axis=-1, keepdims=True))
    exponent = jnp.exp(scores - row_max)
    probs_low = low(exponent / lax.optimization_barrier(jnp.sum(exponent, axis=-1, keepdims=True)))
    return jnp.einsum('shqk,khd->qshd', probs_low, values_tree, precision=highest)

def layer(wide_tokens, gain_first, gain_second, router_att, query_maps, kv_maps, out_maps, router_ffn, ffn_maps, att_choice, ffn_choice, cosines, sines, allowed):
    scale_first = lax.rsqrt(lax.optimization_barrier(jnp.mean(wide_tokens * wide_tokens, axis=-1, keepdims=True)) + epsilon)
    normed_first = low(wide_tokens * scale_first * gain_first)
    att_gates = low(pick_gates(normed_first, router_att, att_choice))
    every_query = jnp.einsum('td,edf->tef', normed_first, low(query_maps), precision=highest)
    query_raw = low_back(jnp.einsum('tse,tef->tsf', att_choice, every_query, precision=highest))
    kv_raw = jnp.einsum('td,jdf->jtf', normed_first, low(kv_maps), precision=highest)
    queries = low(rotate(query_raw.reshape(TOKENS, TOPK, KVH, HS), cosines[:, None, None, :], sines[:, None, None, :]))
    keys_all = low(rotate(low_back(kv_raw[0]).reshape(TOKENS, KVH, HS), cosines[:, None, :], sines[:, None, :]))
    values_all = low(low_back(kv_raw[1])).reshape(TOKENS, KVH, HS)
    attended = lax.map(jax.checkpoint(tree_attention), (queries.reshape(TREES, GROUP, TOPK, KVH, HS), keys_all.reshape(TREES, GROUP, KVH, HS), values_all.reshape(TREES, GROUP, KVH, HS), allowed))
    heads = low(low_back(attended.reshape(TOKENS, TOPK, HD)))
    every_branch = jnp.einsum('tsf,edf->tsed', heads, low(out_maps), precision=highest)
    branch_att = low_back(jnp.einsum('tse,tsed->tsd', att_choice, every_branch, precision=highest))
    middle = wide_tokens + low_back(lax.optimization_barrier(jnp.sum(att_gates[:, :, None] * branch_att, axis=1)))
    scale_second = lax.rsqrt(lax.optimization_barrier(jnp.mean(middle * middle, axis=-1, keepdims=True)) + epsilon)
    normed_second = low(middle * scale_second * gain_second)
    ffn_gates = low(pick_gates(normed_second, router_ffn, ffn_choice))
    expert_weight = jnp.einsum('ts,tse->et', ffn_gates, ffn_choice, precision=highest)

    def expert_step(running_sum, pieces):
        gate_map, up_map, down_map, weight_row = pieces
        gate_h = low_back(jnp.dot(normed_second, low(gate_map), precision=highest))
        up_h = low_back(jnp.dot(normed_second, low(up_map), precision=highest))
        activated = low(jax.nn.silu(gate_h) * up_h)
        result = low_back(jnp.einsum('tf,df->td', activated, low(down_map), precision=highest))
        return (running_sum + weight_row[:, None] * result, None)
    ffn_sum, unused_out = lax.scan(jax.checkpoint(expert_step), jnp.zeros_like(middle), (ffn_maps[:EF], ffn_maps[EF:2 * EF], ffn_maps[2 * EF:], expert_weight))
    return middle + low_back(ffn_sum)

def reference(tokens, norm_gain1, norm_gain2, att_router, query_maps, kv_maps, out_maps, ffn_router, ffn_maps, att_route, ffn_route, parents, cotangent):
    att_choice = (att_route[:, :, None] == jnp.arange(EA, dtype=jnp.int32)[None, None, :]).astype(jnp.float32)
    ffn_choice = (ffn_route[:, :, None] == jnp.arange(EF, dtype=jnp.int32)[None, None, :]).astype(jnp.float32)
    positions, allowed = jax.vmap(tree_tables)(parents.reshape(TREES, NSEG))
    cosines, sines = rope_tables(positions.reshape(-1))

    def forward(wide_tokens, gain_first, gain_second, router_att, query_w, kv_w, out_w, router_ffn, ffn_w):
        return layer(wide_tokens, gain_first, gain_second, router_att, query_w, kv_w, out_w, router_ffn, ffn_w, att_choice, ffn_choice, cosines, sines, allowed)
    mixed_out, pullback = jax.vjp(forward, tokens.astype(jnp.float32), norm_gain1, norm_gain2, att_router, query_maps, kv_maps, out_maps, ffn_router, ffn_maps)
    gradients = pullback(cotangent.astype(jnp.float32))
    return (mixed_out.astype(jnp.bfloat16), gradients[0].astype(jnp.bfloat16), gradients[1], gradients[2], gradients[3], gradients[4], gradients[5], gradients[6], gradients[7], gradients[8])
```

```python
import functools

import jax
import jax.numpy as jnp
from jax import lax
from jax.experimental import pallas as pl
from jax.experimental.pallas import tpu as pltpu
from jax.sharding import Mesh, PartitionSpec as P

EXPERTS = 4
HS = 128
SEG = 128
SIDE = 128
epsilon = 1e-05
rope_base = 10000.0
f32 = jnp.float32
bf16 = jnp.bfloat16
ALL = ("zz", "xx", "tensor")
GROUP = ("zz", "tensor")
VMEM = 60 * 1024 * 1024


def dot(a, b):
    return lax.dot_general(a, b, (((1,), (0,)), ((), ())), preferred_element_type=f32)


def dot_nt(a, b):
    return lax.dot_general(a, b, (((1,), (1,)), ((), ())), preferred_element_type=f32)


def dot_tn(a, b):
    return lax.dot_general(a, b, (((0,), (0,)), ((), ())), preferred_element_type=f32)


def lanes(rows):
    return lax.broadcasted_iota(jnp.int32, (rows, SIDE), 1).astype(f32)


def put(columns, rows):
    lane = lanes(rows)
    out = jnp.zeros((rows, SIDE), f32)
    for place, column in columns.items():
        out = jnp.where(lane == place, column, out)
    return out


def norm_scale(rows):
    return lax.rsqrt(jnp.mean(rows * rows, axis=-1, keepdims=True) + epsilon)


def gate_probs(low, router_parts, route0, route1):
    rows = low.shape[0]
    parts = dot(low, router_parts)
    lane = lanes(rows)
    logits = (
        parts
        + pltpu.roll(parts, SIDE - EXPERTS, 1)
        + pltpu.roll(parts, SIDE - 2 * EXPERTS, 1)
    )
    c0 = jnp.sum(jnp.where(lane == route0, logits, 0.0), axis=1, keepdims=True)
    c1 = jnp.sum(jnp.where(lane == route1, logits, 0.0), axis=1, keepdims=True)
    top = jnp.maximum(c0, c1)
    e0 = jnp.exp(c0 - top)
    e1 = jnp.exp(c1 - top)
    total = e0 + e1
    return put({0: e0 / total, 1: e1 / total}, rows)


def choose(wide, route):
    out = wide[:, :HS]
    for e in range(1, EXPERTS):
        out = jnp.where(route == e, wide[:, e * HS : (e + 1) * HS], out)
    return out


def spread(slots, routes):
    blocks = []
    for e in range(EXPERTS):
        block = jnp.where(routes[0] == e, slots[0], 0.0)
        blocks.append(block + jnp.where(routes[1] == e, slots[1], 0.0))
    return blocks


def rope_rows(depth, table_ref):
    segments = table_ref.shape[0] // SEG
    out = table_ref[0:SEG, :]
    for d in range(1, segments):
        out = jnp.where(depth == d, table_ref[d * SEG : (d + 1) * SEG, :], out)
    return out


def allow_mask(side, seg):
    rows = side[seg * SEG : (seg + 1) * SEG]
    blocks = [jnp.broadcast_to(rows[:, 2 + b : 3 + b], (SEG, SEG)) for b in range(seg)]
    later = lax.broadcasted_iota(jnp.int32, (SEG, SEG), 1)
    here = lax.broadcasted_iota(jnp.int32, (SEG, SEG), 0)
    blocks.append((later <= here).astype(f32))
    mask = jnp.concatenate(blocks, axis=1) if seg else blocks[0]
    return jnp.concatenate([mask, mask], axis=0)


def weights_of(queries, keys, mask):
    scores = dot_nt(queries, keys) * (HS**-0.5)
    scores = jnp.where(mask > 0.5, scores, -1e30)
    top = jnp.max(scores, axis=-1, keepdims=True)
    exponent = jnp.exp(scores - top)
    return exponent / jnp.sum(exponent, axis=-1, keepdims=True)


def pack_kernel(where_ref, parents_ref, tok_ref, att_ref, ffn_ref, out_ref):
    rows = tok_ref.shape[0]
    dim = tok_ref.shape[1]
    out_ref[:, :dim] = tok_ref[...]
    segments = parents_ref.shape[0]
    current = where_ref[0]
    reached = [current == b for b in range(segments)]
    for step in range(segments - 1):
        parent = parents_ref[jnp.maximum(current, 0)]
        current = jnp.where(current > 0, parent, 0)
        reached = [r | (current == b) for b, r in enumerate(reached)]
    flags = [jnp.where(r, 1.0, 0.0) for r in reached]
    depth = functools.reduce(lambda a, b: a + b, flags) - 1.0
    att = att_ref[...].astype(f32)
    ffn = ffn_ref[...].astype(f32)
    columns = {0: att[:, 0:1], 1: att[:, 1:2], 6: depth, 7: ffn[:, 0:1], 8: ffn[:, 1:2]}
    for b in range(segments):
        columns[2 + b] = flags[b]
    out_ref[:, dim:] = put(columns, rows).astype(bf16)


def att_fwd_kernel(
    tok_ref, w_ref, router_ref, gain_ref, cos_ref, sin_ref, part_ref, x_ref, keep_ref, gate_ref
):
    dim = x_ref.shape[1]
    rows = x_ref.shape[0]
    side = tok_ref[:, dim:].astype(f32)
    wide = tok_ref[:, :dim].astype(f32)
    x = (wide * norm_scale(wide) * gain_ref[...]).astype(bf16)
    x_ref[...] = x
    qkv_width = (EXPERTS + 2) * HS
    qkv = dot(x, w_ref[:, :qkv_width])
    routes = (side[:, 0:1], side[:, 1:2])
    probs = gate_probs(x, router_ref[...], routes[0], routes[1])
    gate_ref[...] = probs
    gates = probs.astype(bf16).astype(f32)
    segments = rows // SEG
    cos, sin = [], []
    for a in range(segments):
        depth = side[a * SEG : (a + 1) * SEG, 6:7]
        cos.append(rope_rows(depth, cos_ref))
        sin.append(rope_rows(depth, sin_ref))
    cos = jnp.concatenate(cos, axis=0)
    sin = jnp.concatenate(sin, axis=0)

    def turn(v):
        return (v * cos + pltpu.roll(v, HS // 2, 1) * sin).astype(bf16)

    q = [turn(choose(qkv, r)) for r in routes]
    k = turn(qkv[:, EXPERTS * HS : (EXPERTS + 1) * HS])
    v = qkv[:, (EXPERTS + 1) * HS :].astype(bf16)
    heads = [[], []]
    for a in range(segments):
        here = slice(a * SEG, (a + 1) * SEG)
        upto = (a + 1) * SEG
        qa = jnp.concatenate([q[0][here], q[1][here]], axis=0)
        p = weights_of(qa, k[:upto], allow_mask(side, a))
        o = dot(p.astype(bf16), v[:upto]).astype(bf16)
        heads[0].append(o[:SEG])
        heads[1].append(o[SEG:])
    heads = [jnp.concatenate(h, axis=0) for h in heads]
    for i, piece in enumerate([q[0], q[1], k, v, heads[0], heads[1]]):
        keep_ref[:, i * HS : (i + 1) * HS] = piece
    gated = [gates[:, s : s + 1] * heads[s].astype(f32) for s in range(2)]
    z = jnp.concatenate([b.astype(bf16) for b in spread(gated, routes)], axis=1)
    part_ref[...] = dot_nt(z, w_ref[:, qkv_width:]).astype(bf16)


def att_bwd_kernel(
    c_ref, w_ref, keep_ref, gate_ref, side_ref, cos_ref, sin_ref, back_ref, grad_ref, z_ref
):
    dim = c_ref.shape[1]
    rows = c_ref.shape[0]
    qkv_width = (EXPERTS + 2) * HS
    side = side_ref[...].astype(f32)
    routes = (side[:, 0:1], side[:, 1:2])
    gates = gate_ref[...].astype(bf16).astype(f32)
    g = dot(c_ref[...], w_ref[:, qkv_width:])
    q = [keep_ref[:, :HS], keep_ref[:, HS : 2 * HS]]
    k = keep_ref[:, 2 * HS : 3 * HS]
    v = keep_ref[:, 3 * HS : 4 * HS]
    heads = [keep_ref[:, 4 * HS : 5 * HS].astype(f32), keep_ref[:, 5 * HS :].astype(f32)]
    chosen = [choose(g, r) for r in routes]
    parts = [jnp.sum(heads[s] * chosen[s], axis=1, keepdims=True) for s in range(2)]
    hg = [(gates[:, s : s + 1] * chosen[s]).astype(bf16) for s in range(2)]
    gated = [gates[:, s : s + 1] * heads[s] for s in range(2)]
    for e, block in enumerate(spread(gated, routes)):
        z_ref[:, e * HS : (e + 1) * HS] = block.astype(bf16)
    segments = rows // SEG
    dk = [jnp.zeros((SEG, HS), f32) for _ in range(segments)]
    dv = [jnp.zeros((SEG, HS), f32) for _ in range(segments)]
    dq = [[], []]
    for a in range(segments):
        here = slice(a * SEG, (a + 1) * SEG)
        upto = (a + 1) * SEG
        qa = jnp.concatenate([q[0][here], q[1][here]], axis=0)
        ha = jnp.concatenate([hg[0][here], hg[1][here]], axis=0)
        p = weights_of(qa, k[:upto], allow_mask(side, a))
        pg = dot_nt(ha, v[:upto])
        sg = (p * (pg - jnp.sum(p * pg, axis=-1, keepdims=True))).astype(bf16)
        dqa = dot(sg, k[:upto]) * (HS**-0.5)
        dq[0].append(dqa[:SEG])
        dq[1].append(dqa[SEG:])
        dka = dot_tn(sg, qa) * (HS**-0.5)
        dva = dot_tn(p.astype(bf16), ha)
        for b in range(a + 1):
            dk[b] = dk[b] + dka[b * SEG : (b + 1) * SEG]
            dv[b] = dv[b] + dva[b * SEG : (b + 1) * SEG]
    cos, sin = [], []
    for a in range(segments):
        depth = side[a * SEG : (a + 1) * SEG, 6:7]
        cos.append(rope_rows(depth, cos_ref))
        sin.append(rope_rows(depth, sin_ref))
    cos = jnp.concatenate(cos, axis=0)
    sin = jnp.concatenate(sin, axis=0)

    def unturn(v):
        return v * cos - pltpu.roll(v, HS // 2, 1) * sin

    dq = [unturn(jnp.concatenate(d, axis=0)) for d in dq]
    blocks = spread(dq, routes) + [unturn(jnp.concatenate(dk, axis=0)), jnp.concatenate(dv, axis=0)]
    grad = jnp.concatenate([b.astype(bf16) for b in blocks], axis=1)
    grad_ref[...] = grad
    back_ref[:, :dim] = dot_nt(grad, w_ref[:, :qkv_width]).astype(bf16)
    back_ref[:, dim:] = put({0: parts[0], 1: parts[1]}, rows).astype(bf16)


def mid_kernel(rs_ref, packed_ref, gain_ref, router_ref, out_ref, middle_ref, gate_ref):
    rows, dim = rs_ref.shape
    side = packed_ref[:, dim:].astype(f32)
    middle = packed_ref[:, :dim].astype(f32) + rs_ref[...].astype(f32)
    middle_ref[...] = middle
    low = (middle * norm_scale(middle) * gain_ref[...]).astype(bf16)
    out_ref[:, :dim] = low
    probs = gate_probs(low, router_ref[...], side[:, 7:8], side[:, 8:9])
    gate_ref[...] = probs
    out_ref[:, dim:] = put(
        {0: probs[:, 0:1], 1: probs[:, 1:2], 2: side[:, 7:8], 3: side[:, 8:9]}, rows
    ).astype(bf16)


def norm_back_kernel(
    route_at, where_ref, rsb_ref, rows_ref, base_ref, gain_ref, router_ref, gate_ref, side_ref,
    *out_refs
):
    count, dim = rows_ref.shape
    grad = rsb_ref[:, :dim].astype(f32)
    gp = rsb_ref[:, dim:].astype(f32)
    side = side_ref[...].astype(f32)
    p0, p1 = gate_ref[:, 0:1], gate_ref[:, 1:2]
    q0, q1 = gp[:, 0:1], gp[:, 1:2]
    inner = p0 * q0 + p1 * q1
    i0, i1 = p0 * (q0 - inner), p1 * (q1 - inner)
    rows = rows_ref[...].astype(f32)
    scale = norm_scale(rows)
    normal = rows * scale
    gain = gain_ref[...]
    low = (normal * gain).astype(bf16).astype(f32)
    route0, route1 = side[:, route_at : route_at + 1], side[:, route_at + 1 : route_at + 2]
    parts = []
    for e in range(EXPERTS):
        logit_grad = jnp.where(route0 == e, i0, 0.0) + jnp.where(route1 == e, i1, 0.0)
        grad = grad + logit_grad * router_ref[e : e + 1, :]
        parts.append(jnp.sum(logit_grad * low, axis=0, keepdims=True))
    parts.append(jnp.sum(grad * normal, axis=0, keepdims=True))
    parts.append(jnp.zeros((8 - len(parts), dim), f32))
    out_refs[0][...] = jnp.concatenate(parts, axis=0)
    weighted = grad * gain
    total = base_ref[...].astype(f32) + scale * (
        weighted - normal * jnp.mean(weighted * normal, axis=-1, keepdims=True)
    )
    for ref in out_refs[1:]:
        ref[...] = total.astype(ref.dtype)


def ffn_kernel(
    where_ref, x_ref, c_ref, wg_ref, wu_ref, wd_ref, back_ref, a_ref, gg_ref, ug_ref
):
    rows, dim = c_ref.shape
    side = x_ref[:, dim:].astype(f32)
    mine = where_ref[0].astype(f32)
    in0, in1 = side[:, 2:3] == mine, side[:, 3:4] == mine
    coef = jnp.where(in0, side[:, 0:1], 0.0) + jnp.where(in1, side[:, 1:2], 0.0)
    x = x_ref[:, :dim]
    gate = dot(x, wg_ref[...])
    up = dot(x, wu_ref[...])
    act_grad = dot(c_ref[...], wd_ref[...])
    sig = jax.nn.sigmoid(gate)
    silu = gate * sig
    act = (silu * up).astype(bf16).astype(f32)
    part = jnp.sum(act * act_grad, axis=-1, keepdims=True)
    a_ref[...] = (act * coef).astype(bf16)
    act_grad = act_grad * coef
    gg = (act_grad * up * sig * (1.0 + gate * (1.0 - sig))).astype(bf16)
    ug = (act_grad * silu).astype(bf16)
    gg_ref[...] = gg
    ug_ref[...] = ug
    back_ref[:, :dim] = (dot_nt(gg, wg_ref[...]) + dot_nt(ug, wu_ref[...])).astype(bf16)
    back_ref[:, dim:] = put(
        {0: jnp.where(in0, part, 0.0), 1: jnp.where(in1, part, 0.0)}, rows
    ).astype(bf16)


def params():
    return pltpu.CompilerParams(vmem_limit_bytes=VMEM)


def cost(flops, nbytes):
    return pl.CostEstimate(flops=int(flops), bytes_accessed=int(nbytes), transcendentals=0)


def shape(dims, dtype):
    return jax.ShapeDtypeStruct(dims, dtype)


def whole(array):
    zeros = (0,) * array.ndim
    return pl.BlockSpec(array.shape, lambda *unused: zeros)


def router_parts(router):
    high = lax.reduce_precision(router, 8, 7)
    rest = router - high
    middle = lax.reduce_precision(rest, 8, 7)
    low = rest - middle
    parts = jnp.concatenate([high, middle, low], axis=1)
    return jnp.pad(parts, ((0, 0), (0, SIDE - parts.shape[1]))).astype(bf16)


def shift(value, axis, step, size):
    return lax.ppermute(value, axis, [(i, (i + step) % size) for i in range(size)])


def local(
    tokens, norm_gain1, norm_gain2, att_router, query_maps, kv_maps, out_maps, ffn_router,
    ffn_maps, att_route, ffn_route, parents, cotangent,
):
    rows, dim = tokens.shape
    group_len = att_route.shape[0]
    zz, xx, tt = lax.axis_index("zz"), lax.axis_index("xx"), lax.axis_index("tensor")
    zs, xs, ts = lax.axis_size("zz"), lax.axis_size("xx"), lax.axis_size("tensor")
    here = jnp.stack([tt]).astype(jnp.int32)
    total = rows * zs * ts
    wide_cols = dim + SIDE

    def bring_rows(pieces):
        got = [pieces(0)] + [None] * (zs - 1)
        for k in (1, 3, 2):
            got[k] = shift(pieces(k), "zz", k, zs)
        part, width = got[0].shape
        if xs == 2:
            full = jnp.zeros((zs, xs, part, width), bf16)
            for k in (0, 1, 3, 2):
                source = (zz - k) % zs
                full = lax.dynamic_update_slice(full, got[k][None, None], (source, xx, 0, 0))
                other = shift(got[k], "xx", 1, 2)
                full = lax.dynamic_update_slice(full, other[None, None], (source, 1 - xx, 0, 0))
        else:
            half = jnp.zeros((zs, part, width), bf16)
            for k in range(zs):
                half = lax.dynamic_update_slice(half, got[k][None], ((zz - k) % zs, 0, 0))
            full = lax.all_gather(half, "xx", axis=1)
        return full.reshape(zs * xs * part, width)

    def return_rows(grad):
        width = grad.shape[1]
        grad = grad.reshape(zs, xs, -1, width)
        part = grad.shape[2]
        if xs != 2:
            summed = lax.psum_scatter(
                grad.transpose(1, 0, 2, 3), "xx", scatter_dimension=0, tiled=False
            )
        out = [None] * zs
        for k in (2, 1, 3, 0):
            target = (zz + k) % zs
            if xs == 2:
                sent = lax.dynamic_slice(grad, (target, 1 - xx, 0, 0), (1, 1, part, width))
                kept = lax.dynamic_slice(grad, (target, xx, 0, 0), (1, 1, part, width))
                piece = kept.astype(f32) + shift(sent, "xx", 1, 2).astype(f32)
                piece = piece.astype(bf16)[0, 0]
            else:
                piece = lax.dynamic_index_in_dim(summed, target, 0, keepdims=False)
            out[k] = shift(piece, "zz", k, zs) if k else piece
        return out

    packed = pl.pallas_call(
        pack_kernel,
        grid_spec=pltpu.PrefetchScalarGridSpec(
            num_scalar_prefetch=2,
            grid=(1,),
            in_specs=[
                pl.BlockSpec((rows, dim), lambda i, w, p: (0, 0)),
                pl.BlockSpec((rows, 2), lambda i, w, p: (w[0], 0)),
                pl.BlockSpec((rows, 2), lambda i, w, p: (w[0], 0)),
            ],
            out_specs=pl.BlockSpec((rows, wide_cols), lambda i, w, p: (0, 0)),
        ),
        out_shape=shape((rows, wide_cols), bf16),
        compiler_params=params(),
        name="pack",
    )(here, parents, tokens, att_route, ffn_route)
    group_tokens = lax.all_gather(packed, GROUP, axis=0, tiled=True)

    small = jnp.concatenate(
        [norm_gain1[None], norm_gain2[None], att_router.T, ffn_router.T], axis=0
    )
    small = lax.all_gather(small.reshape(1, -1), ALL, axis=0, tiled=True)
    small = small.reshape(-1, 2 + 2 * EXPERTS, norm_gain1.shape[0])
    small = small.transpose(1, 0, 2).reshape(2 + 2 * EXPERTS, dim)
    gain1, gain2 = small[0:1], small[1:2]
    router1 = jnp.pad(small[2 : 2 + EXPERTS], ((0, 8 - EXPERTS), (0, 0)))
    router2 = jnp.pad(small[2 + EXPERTS :], ((0, 8 - EXPERTS), (0, 0)))
    parts1 = router_parts(small[2 : 2 + EXPERTS].T)
    parts2 = router_parts(small[2 + EXPERTS :].T)

    maps = jnp.concatenate([query_maps, kv_maps, out_maps], axis=0).astype(bf16)
    count = maps.shape[0]
    part = maps.shape[1]
    by_head = maps.reshape(count, part, zs, HS).transpose(2, 1, 0, 3).reshape(zs, part, count * HS)
    w_att = bring_rows(
        lambda k: lax.dynamic_index_in_dim(by_head, (zz + k) % zs, 0, keepdims=False)
    )

    def expert_rows(kind):
        def piece(k):
            index = kind * EXPERTS + (zz + k) % zs
            return lax.dynamic_index_in_dim(ffn_maps, index, 0, keepdims=False).astype(bf16)

        return bring_rows(piece)

    w_gate, w_up, w_down = expert_rows(0), expert_rows(1), expert_rows(2)
    group_cot = lax.all_gather(cotangent, GROUP, axis=0, tiled=True)

    half = HS // 2
    frequency = rope_base ** (-2.0 * jnp.arange(half, dtype=f32) / HS)
    angles = jnp.arange(group_len, dtype=f32)[:, None] * frequency[None, :]
    cosines, sines = jnp.cos(angles), jnp.sin(angles)
    cos = jnp.concatenate([cosines, cosines], axis=1)
    sin = jnp.concatenate([-sines, sines], axis=1)

    trees = total // group_len
    block = lambda width: pl.BlockSpec((group_len, width), lambda i: (i, 0))
    part_att, x1, kept, gate1 = pl.pallas_call(
        att_fwd_kernel,
        grid=(trees,),
        in_specs=[
            block(wide_cols), whole(w_att), whole(parts1), whole(gain1), whole(cos), whole(sin)
        ],
        out_specs=[block(dim), block(dim), block(6 * HS), block(SIDE)],
        out_shape=[
            shape((total, dim), bf16), shape((total, dim), bf16), shape((total, 6 * HS), bf16),
            shape((total, SIDE), f32),
        ],
        compiler_params=params(),
        cost_estimate=cost(2 * total * dim * 11 * HS, 6 * total * dim),
        name="att_fwd",
    )(group_tokens, w_att, parts1, gain1, cos, sin)
    sum_att = lax.psum_scatter(part_att, GROUP, scatter_dimension=0, tiled=True)

    packed2, middle, gate2 = pl.pallas_call(
        mid_kernel,
        out_shape=[shape((rows, wide_cols), bf16), shape((rows, dim), f32), shape((rows, SIDE), f32)],
        compiler_params=params(),
        name="mid",
    )(sum_att, packed, gain2, parts2)
    x2 = lax.all_gather(packed2, GROUP, axis=0, tiled=True)

    width = w_gate.shape[1]
    step = 256
    rows_of = lambda w: pl.BlockSpec((step, w), lambda i, s: (i, 0))
    fixed = lambda: pl.BlockSpec(
        (dim, width), lambda i, s: (0, 0), pipeline_mode=pl.Buffered(buffer_count=1)
    )
    back2, act, gate_grad, up_grad = pl.pallas_call(
        ffn_kernel,
        grid_spec=pltpu.PrefetchScalarGridSpec(
            num_scalar_prefetch=1,
            grid=(total // step,),
            in_specs=[rows_of(wide_cols), rows_of(dim), fixed(), fixed(), fixed()],
            out_specs=[rows_of(wide_cols), rows_of(width), rows_of(width), rows_of(width)],
        ),
        out_shape=[shape((total, wide_cols), bf16)] + [shape((total, width), bf16)] * 3,
        compiler_params=params(),
        cost_estimate=cost(2 * total * dim * 5 * width, 6 * dim * width + 12 * total * dim),
        name="ffn",
    )(jnp.stack([zz]).astype(jnp.int32), x2, group_cot, w_gate, w_up, w_down)
    sum_back2 = lax.psum_scatter(back2, GROUP, scatter_dimension=0, tiled=True)

    part_ffn = dot_nt(act, w_down).astype(bf16)
    mixed = (
        middle + lax.psum_scatter(part_ffn, GROUP, scatter_dimension=0, tiled=True).astype(f32)
    ).astype(bf16)

    def norm_back(route_at, rsb, wide_rows, base, gain, router, gate, gate_at, outs, name):
        def pick(a):
            return pl.BlockSpec(a.shape, lambda i, w: (0,) * a.ndim)

        return pl.pallas_call(
            functools.partial(norm_back_kernel, route_at),
            grid_spec=pltpu.PrefetchScalarGridSpec(
                num_scalar_prefetch=1,
                grid=(1,),
                in_specs=[
                    pick(rsb), pl.BlockSpec((rows, dim), lambda i, w: (0, 0)), pick(base), pick(gain), pick(router),
                    pl.BlockSpec((rows, SIDE), lambda i, w: (w[0], 0)),
                    pl.BlockSpec((rows, SIDE), lambda i, w: (0, dim // SIDE)),
                ],
                out_specs=[pl.BlockSpec((8, dim), lambda i, w: (0, 0))]
                + [pl.BlockSpec((rows, dim), lambda i, w: (0, 0)) for _ in outs],
            ),
            out_shape=[shape((8, dim), f32)] + [shape((rows, dim), d) for d in outs],
            compiler_params=params(),
            name=name,
        )(gate_at, rsb, wide_rows, base, gain, router, gate, packed)

    zero = jnp.zeros((1,), jnp.int32)
    parts_ffn, middle_grad, att_cot = norm_back(
        7, sum_back2, middle, cotangent, gain2, router2, gate2, zero, [f32, bf16], "mid_back"
    )
    group_att_cot = lax.all_gather(att_cot, GROUP, axis=0, tiled=True)

    x2_low = x2[:, :dim]
    ffn_out = jnp.zeros(ffn_maps.shape, f32)
    for kind, grad in (
        (2, dot_tn(group_cot, act)), (0, dot_tn(x2_low, gate_grad)), (1, dot_tn(x2_low, up_grad))
    ):
        for k, piece in enumerate(return_rows(grad.astype(bf16))):
            index = kind * EXPERTS + (zz - k) % zs
            ffn_out = lax.dynamic_update_slice(ffn_out, piece.astype(f32)[None], (index, 0, 0))

    back1, grad_qkv, z = pl.pallas_call(
        att_bwd_kernel,
        grid=(trees,),
        in_specs=[
            block(dim), whole(w_att), block(6 * HS), block(SIDE),
            pl.BlockSpec((group_len, SIDE), lambda i: (i, dim // SIDE)), whole(cos), whole(sin),
        ],
        out_specs=[block(wide_cols), block(6 * HS), block(EXPERTS * HS)],
        out_shape=[
            shape((total, wide_cols), bf16), shape((total, 6 * HS), bf16),
            shape((total, EXPERTS * HS), bf16),
        ],
        compiler_params=params(),
        cost_estimate=cost(2 * total * dim * 11 * HS, 6 * total * dim),
        name="att_bwd",
    )(group_att_cot, w_att, kept, gate1, group_tokens, cos, sin)
    sum_back1 = lax.psum_scatter(back1, GROUP, scatter_dimension=0, tiled=True)

    grad_att = jnp.concatenate(
        [dot_tn(x1, grad_qkv).astype(bf16), dot_tn(group_att_cot, z).astype(bf16)], axis=1
    )
    gathered = jnp.zeros((zs, part, count * HS), bf16)
    for k, piece in enumerate(return_rows(grad_att)):
        gathered = lax.dynamic_update_slice(gathered, piece[None], ((zz - k) % zs, 0, 0))
    maps_grad = (
        gathered.reshape(zs, part, count, HS).transpose(2, 1, 0, 3).reshape(maps.shape).astype(f32)
    )

    parts_att, input_grad = norm_back(
        0, sum_back1, tokens, middle_grad, gain1, router1, gate1,
        (zz * ts + tt)[None].astype(jnp.int32), [bf16], "input_back",
    )

    def small_sum(parts):
        parts = parts.reshape(8, zs * xs * ts, -1).transpose(1, 0, 2)
        devices = parts.shape[0]
        summed = lax.psum_scatter(
            parts.reshape(devices, -1), ALL, scatter_dimension=0, tiled=True
        ).reshape(8, -1)
        return summed[EXPERTS], summed[:EXPERTS].T

    gain2_grad, ffn_router_grad = small_sum(parts_ffn)
    gain1_grad, att_router_grad = small_sum(parts_att)
    queries = query_maps.shape[0]
    keys = kv_maps.shape[0]
    return (
        mixed,
        input_grad,
        gain1_grad,
        gain2_grad,
        att_router_grad,
        maps_grad[:queries],
        maps_grad[queries : queries + keys],
        maps_grad[queries + keys :],
        ffn_router_grad,
        ffn_out,
    )


def solution(mesh):
    dp, tensor = mesh.shape["dp"], mesh.shape["tensor"]
    fine = Mesh(mesh.devices.reshape(EXPERTS, dp // EXPERTS, tensor), ALL)
    dps = ("zz", "xx")
    rows, flat, maps = P(ALL, None), P(ALL), P(None, dps, "tensor")
    placed = (
        rows, flat, flat, rows, maps, maps, maps, rows, maps, P(dps, None), P(dps, None), P(dps), rows
    )
    return jax.shard_map(
        local,
        mesh=fine,
        in_specs=placed,
        out_specs=(rows, rows, flat, flat, rows, maps, maps, maps, rows, maps),
        check_vma=False,
    )
```

```python
import functools

import jax
import jax.numpy as jnp
from jax import lax
from jax.experimental import pallas as pl
from jax.experimental.pallas import tpu as pltpu
from jax.sharding import Mesh, PartitionSpec as P

EXPERTS = 4
HS = 128
SEG = 128
SIDE = 128
epsilon = 1e-05
rope_base = 10000.0
f32 = jnp.float32
bf16 = jnp.bfloat16
ALL = ("zz", "xx", "tensor")
GROUP = ("zz", "tensor")
VMEM = 60 * 1024 * 1024


def dot(a, b):
    return lax.dot_general(a, b, (((1,), (0,)), ((), ())), preferred_element_type=f32)


def dot_nt(a, b):
    return lax.dot_general(a, b, (((1,), (1,)), ((), ())), preferred_element_type=f32)


def dot_tn(a, b):
    return lax.dot_general(a, b, (((0,), (0,)), ((), ())), preferred_element_type=f32)


def lanes(rows):
    return lax.broadcasted_iota(jnp.int32, (rows, SIDE), 1).astype(f32)


def put(columns, rows):
    lane = lanes(rows)
    out = jnp.zeros((rows, SIDE), f32)
    for place, column in columns.items():
        out = jnp.where(lane == place, column, out)
    return out


def norm_scale(rows):
    return lax.rsqrt(jnp.mean(rows * rows, axis=-1, keepdims=True) + epsilon)


def gate_probs(low, router_parts, route0, route1):
    rows = low.shape[0]
    parts = dot(low, router_parts)
    lane = lanes(rows)
    logits = (
        parts
        + pltpu.roll(parts, SIDE - EXPERTS, 1)
        + pltpu.roll(parts, SIDE - 2 * EXPERTS, 1)
    )
    c0 = jnp.sum(jnp.where(lane == route0, logits, 0.0), axis=1, keepdims=True)
    c1 = jnp.sum(jnp.where(lane == route1, logits, 0.0), axis=1, keepdims=True)
    top = jnp.maximum(c0, c1)
    e0 = jnp.exp(c0 - top)
    e1 = jnp.exp(c1 - top)
    total = e0 + e1
    return put({0: e0 / total, 1: e1 / total}, rows)


def choose(wide, route):
    out = wide[:, :HS]
    for e in range(1, EXPERTS):
        out = jnp.where(route == e, wide[:, e * HS : (e + 1) * HS], out)
    return out


def spread(slots, routes):
    blocks = []
    for e in range(EXPERTS):
        block = jnp.where(routes[0] == e, slots[0], 0.0)
        blocks.append(block + jnp.where(routes[1] == e, slots[1], 0.0))
    return blocks


def rope_rows(depth, table_ref):
    segments = table_ref.shape[0] // SEG
    out = table_ref[0:SEG, :]
    for d in range(1, segments):
        out = jnp.where(depth == d, table_ref[d * SEG : (d + 1) * SEG, :], out)
    return out


def allow_mask(side, seg):
    rows = side[seg * SEG : (seg + 1) * SEG]
    blocks = [jnp.broadcast_to(rows[:, 2 + b : 3 + b], (SEG, SEG)) for b in range(seg)]
    later = lax.broadcasted_iota(jnp.int32, (SEG, SEG), 1)
    here = lax.broadcasted_iota(jnp.int32, (SEG, SEG), 0)
    blocks.append((later <= here).astype(f32))
    mask = jnp.concatenate(blocks, axis=1) if seg else blocks[0]
    return jnp.concatenate([mask, mask], axis=0)


def weights_of(queries, keys, mask):
    scores = dot_nt(queries, keys) * (HS**-0.5)
    scores = jnp.where(mask > 0.5, scores, -1e30)
    top = jnp.max(scores, axis=-1, keepdims=True)
    exponent = jnp.exp(scores - top)
    return exponent / jnp.sum(exponent, axis=-1, keepdims=True)


def pack_kernel(where_ref, parents_ref, tok_ref, att_ref, ffn_ref, out_ref):
    rows = tok_ref.shape[0]
    dim = tok_ref.shape[1]
    out_ref[:, :dim] = tok_ref[...]
    segments = parents_ref.shape[0]
    current = where_ref[0]
    reached = [current == b for b in range(segments)]
    for step in range(segments - 1):
        parent = parents_ref[jnp.maximum(current, 0)]
        current = jnp.where(current > 0, parent, 0)
        reached = [r | (current == b) for b, r in enumerate(reached)]
    flags = [jnp.where(r, 1.0, 0.0) for r in reached]
    depth = functools.reduce(lambda a, b: a + b, flags) - 1.0
    att = att_ref[...].astype(f32)
    ffn = ffn_ref[...].astype(f32)
    columns = {0: att[:, 0:1], 1: att[:, 1:2], 6: depth, 7: ffn[:, 0:1], 8: ffn[:, 1:2]}
    for b in range(segments):
        columns[2 + b] = flags[b]
    out_ref[:, dim:] = put(columns, rows).astype(bf16)


def att_fwd_kernel(
    tok_ref, w_ref, router_ref, gain_ref, cos_ref, sin_ref, part_ref, x_ref, keep_ref, gate_ref
):
    dim = x_ref.shape[1]
    rows = x_ref.shape[0]
    side = tok_ref[:, dim:].astype(f32)
    wide = tok_ref[:, :dim].astype(f32)
    x = (wide * norm_scale(wide) * gain_ref[...]).astype(bf16)
    x_ref[...] = x
    qkv_width = (EXPERTS + 2) * HS
    qkv = dot(x, w_ref[:, :qkv_width])
    routes = (side[:, 0:1], side[:, 1:2])
    probs = gate_probs(x, router_ref[...], routes[0], routes[1])
    gate_ref[...] = probs
    gates = probs.astype(bf16).astype(f32)
    segments = rows // SEG
    cos, sin = [], []
    for a in range(segments):
        depth = side[a * SEG : (a + 1) * SEG, 6:7]
        cos.append(rope_rows(depth, cos_ref))
        sin.append(rope_rows(depth, sin_ref))
    cos = jnp.concatenate(cos, axis=0)
    sin = jnp.concatenate(sin, axis=0)

    def turn(v):
        return (v * cos + pltpu.roll(v, HS // 2, 1) * sin).astype(bf16)

    q = [turn(choose(qkv, r)) for r in routes]
    k = turn(qkv[:, EXPERTS * HS : (EXPERTS + 1) * HS])
    v = qkv[:, (EXPERTS + 1) * HS :].astype(bf16)
    heads = [[], []]
    for a in range(segments):
        here = slice(a * SEG, (a + 1) * SEG)
        upto = (a + 1) * SEG
        qa = jnp.concatenate([q[0][here], q[1][here]], axis=0)
        p = weights_of(qa, k[:upto], allow_mask(side, a))
        o = dot(p.astype(bf16), v[:upto]).astype(bf16)
        heads[0].append(o[:SEG])
        heads[1].append(o[SEG:])
    heads = [jnp.concatenate(h, axis=0) for h in heads]
    for i, piece in enumerate([q[0], q[1], k, v, heads[0], heads[1]]):
        keep_ref[:, i * HS : (i + 1) * HS] = piece
    gated = [gates[:, s : s + 1] * heads[s].astype(f32) for s in range(2)]
    z = jnp.concatenate([b.astype(bf16) for b in spread(gated, routes)], axis=1)
    part_ref[...] = dot_nt(z, w_ref[:, qkv_width:]).astype(bf16)


def att_bwd_kernel(
    c_ref, w_ref, keep_ref, gate_ref, side_ref, cos_ref, sin_ref, back_ref, grad_ref, z_ref
):
    dim = c_ref.shape[1]
    rows = c_ref.shape[0]
    qkv_width = (EXPERTS + 2) * HS
    side = side_ref[...].astype(f32)
    routes = (side[:, 0:1], side[:, 1:2])
    gates = gate_ref[...].astype(bf16).astype(f32)
    g = dot(c_ref[...], w_ref[:, qkv_width:])
    q = [keep_ref[:, :HS], keep_ref[:, HS : 2 * HS]]
    k = keep_ref[:, 2 * HS : 3 * HS]
    v = keep_ref[:, 3 * HS : 4 * HS]
    heads = [keep_ref[:, 4 * HS : 5 * HS].astype(f32), keep_ref[:, 5 * HS :].astype(f32)]
    chosen = [choose(g, r) for r in routes]
    parts = [jnp.sum(heads[s] * chosen[s], axis=1, keepdims=True) for s in range(2)]
    hg = [(gates[:, s : s + 1] * chosen[s]).astype(bf16) for s in range(2)]
    gated = [gates[:, s : s + 1] * heads[s] for s in range(2)]
    for e, block in enumerate(spread(gated, routes)):
        z_ref[:, e * HS : (e + 1) * HS] = block.astype(bf16)
    segments = rows // SEG
    dk = [jnp.zeros((SEG, HS), f32) for _ in range(segments)]
    dv = [jnp.zeros((SEG, HS), f32) for _ in range(segments)]
    dq = [[], []]
    for a in range(segments):
        here = slice(a * SEG, (a + 1) * SEG)
        upto = (a + 1) * SEG
        qa = jnp.concatenate([q[0][here], q[1][here]], axis=0)
        ha = jnp.concatenate([hg[0][here], hg[1][here]], axis=0)
        p = weights_of(qa, k[:upto], allow_mask(side, a))
        pg = dot_nt(ha, v[:upto])
        sg = (p * (pg - jnp.sum(p * pg, axis=-1, keepdims=True))).astype(bf16)
        dqa = dot(sg, k[:upto]) * (HS**-0.5)
        dq[0].append(dqa[:SEG])
        dq[1].append(dqa[SEG:])
        dka = dot_tn(sg, qa) * (HS**-0.5)
        dva = dot_tn(p.astype(bf16), ha)
        for b in range(a + 1):
            dk[b] = dk[b] + dka[b * SEG : (b + 1) * SEG]
            dv[b] = dv[b] + dva[b * SEG : (b + 1) * SEG]
    cos, sin = [], []
    for a in range(segments):
        depth = side[a * SEG : (a + 1) * SEG, 6:7]
        cos.append(rope_rows(depth, cos_ref))
        sin.append(rope_rows(depth, sin_ref))
    cos = jnp.concatenate(cos, axis=0)
    sin = jnp.concatenate(sin, axis=0)

    def unturn(v):
        return v * cos - pltpu.roll(v, HS // 2, 1) * sin

    dq = [unturn(jnp.concatenate(d, axis=0)) for d in dq]
    blocks = spread(dq, routes) + [unturn(jnp.concatenate(dk, axis=0)), jnp.concatenate(dv, axis=0)]
    grad = jnp.concatenate([b.astype(bf16) for b in blocks], axis=1)
    grad_ref[...] = grad
    back_ref[:, :dim] = dot_nt(grad, w_ref[:, :qkv_width]).astype(bf16)
    back_ref[:, dim:] = put({0: parts[0], 1: parts[1]}, rows).astype(bf16)


def mid_kernel(rs_ref, packed_ref, gain_ref, router_ref, *refs):
    out_ref, middle_ref, gate_ref = refs[-3:]
    rows, dim = rs_ref.shape
    side = packed_ref[:, dim:].astype(f32)
    middle = packed_ref[:, :dim].astype(f32) + rs_ref[...].astype(f32)
    middle_ref[...] = middle
    low = (middle * norm_scale(middle) * gain_ref[...]).astype(bf16)
    out_ref[:, :dim] = low
    probs = gate_probs(low, router_ref[...], side[:, 7:8], side[:, 8:9])
    gate_ref[...] = probs
    out_ref[:, dim:] = put(
        {0: probs[:, 0:1], 1: probs[:, 1:2], 2: side[:, 7:8], 3: side[:, 8:9]}, rows
    ).astype(bf16)


def norm_back_kernel(
    route_at, outs, where_ref, rsb_ref, rows_ref, base_ref, gain_ref, router_ref, gate_ref, side_ref,
    *refs
):
    out_refs = refs[-outs:]
    count, dim = rows_ref.shape
    grad = rsb_ref[:, :dim].astype(f32)
    gp = rsb_ref[:, dim:].astype(f32)
    side = side_ref[...].astype(f32)
    p0, p1 = gate_ref[:, 0:1], gate_ref[:, 1:2]
    q0, q1 = gp[:, 0:1], gp[:, 1:2]
    inner = p0 * q0 + p1 * q1
    i0, i1 = p0 * (q0 - inner), p1 * (q1 - inner)
    rows = rows_ref[...].astype(f32)
    scale = norm_scale(rows)
    normal = rows * scale
    gain = gain_ref[...]
    low = (normal * gain).astype(bf16).astype(f32)
    route0, route1 = side[:, route_at : route_at + 1], side[:, route_at + 1 : route_at + 2]
    parts = []
    for e in range(EXPERTS):
        logit_grad = jnp.where(route0 == e, i0, 0.0) + jnp.where(route1 == e, i1, 0.0)
        grad = grad + logit_grad * router_ref[e : e + 1, :]
        parts.append(jnp.sum(logit_grad * low, axis=0, keepdims=True))
    parts.append(jnp.sum(grad * normal, axis=0, keepdims=True))
    parts.append(jnp.zeros((8 - len(parts), dim), f32))
    out_refs[0][...] = jnp.concatenate(parts, axis=0)
    weighted = grad * gain
    total = base_ref[...].astype(f32) + scale * (
        weighted - normal * jnp.mean(weighted * normal, axis=-1, keepdims=True)
    )
    for ref in out_refs[1:]:
        ref[...] = total.astype(ref.dtype)


def ffn_coef(side, mine):
    in0, in1 = side[:, 2:3] == mine, side[:, 3:4] == mine
    return in0, in1, jnp.where(in0, side[:, 0:1], 0.0) + jnp.where(in1, side[:, 1:2], 0.0)


def ffn_fwd_kernel(where_ref, x_ref, wg_ref, wu_ref, gate_ref, up_ref, a_ref):
    dim = wg_ref.shape[0]
    side = x_ref[:, dim:].astype(f32)
    coef = ffn_coef(side, where_ref[0].astype(f32))[2]
    x = x_ref[:, :dim]
    gate = dot(x, wg_ref[...])
    up = dot(x, wu_ref[...])
    gate_ref[...] = gate.astype(bf16)
    up_ref[...] = up.astype(bf16)
    a_ref[...] = (gate * jax.nn.sigmoid(gate) * up * coef).astype(bf16)


def ffn_act_kernel(
    where_ref, side_ref, gate_ref, up_ref, c_ref, wd_ref, wait_ref, gg_ref, ug_ref, part_ref
):
    rows = c_ref.shape[0]
    in0, in1, coef = ffn_coef(side_ref[...].astype(f32), where_ref[0].astype(f32))
    gate = gate_ref[...].astype(f32)
    up = up_ref[...].astype(f32)
    act_grad = dot(c_ref[...], wd_ref[...])
    sig = jax.nn.sigmoid(gate)
    silu = gate * sig
    part = jnp.sum(silu * up * act_grad, axis=-1, keepdims=True)
    act_grad = act_grad * coef
    gg_ref[...] = (act_grad * up * sig * (1.0 + gate * (1.0 - sig))).astype(bf16)
    ug_ref[...] = (act_grad * silu).astype(bf16)
    part_ref[...] = put(
        {0: jnp.where(in0, part, 0.0), 1: jnp.where(in1, part, 0.0)}, rows
    ).astype(bf16)


def ffn_back_kernel(gg_ref, ug_ref, part_ref, wg_ref, wu_ref, wait_ref, back_ref):
    dim = wg_ref.shape[0]
    back_ref[:, :dim] = (
        dot_nt(gg_ref[...], wg_ref[...]) + dot_nt(ug_ref[...], wu_ref[...])
    ).astype(bf16)
    back_ref[:, dim:] = part_ref[...]


def split_kernel(query_ref, kv_ref, out_ref, wait_ref, piece_ref):
    for head in range(piece_ref.shape[0]):
        place = 0
        for ref in (query_ref, kv_ref, out_ref):
            for m in range(ref.shape[0]):
                rows = ref[m, :, head * HS : (head + 1) * HS]
                piece_ref[head, :, place : place + HS] = rows.astype(bf16)
                place += HS


def cast_kernel(*refs):
    kinds = (len(refs) - 1) // 3
    for kind in range(kinds):
        first, second = refs[kinds + 1 + 2 * kind : kinds + 3 + 2 * kind]
        cut = first.shape[1]
        first[...] = refs[kind][:, :cut].astype(bf16)
        second[...] = refs[kind][:, cut:].astype(bf16)


def join_kernel(piece_ref, *outs):
    for head in range(piece_ref.shape[0]):
        place = 0
        for ref in outs:
            for m in range(ref.shape[0]):
                rows = piece_ref[head, :, place : place + HS]
                ref[m, :, head * HS : (head + 1) * HS] = rows.astype(f32)
                place += HS


def after(value, *waited):
    def body(*refs):
        pass

    anywhere = pl.BlockSpec(memory_space=pl.ANY)
    return pl.pallas_call(
        body,
        in_specs=[anywhere] * (1 + len(waited)),
        out_specs=anywhere,
        out_shape=shape(value.shape, value.dtype),
        input_output_aliases={0: 0},
        cost_estimate=cost(1e6, 1e3),
        name="after",
    )(value, *waited)


def params():
    return pltpu.CompilerParams(vmem_limit_bytes=VMEM)


def cost(flops, nbytes):
    return pl.CostEstimate(flops=int(flops), bytes_accessed=int(nbytes), transcendentals=0)


def wall():
    return cost(2e11, 1e6)


def shape(dims, dtype):
    return jax.ShapeDtypeStruct(dims, dtype)


def whole(array):
    zeros = (0,) * array.ndim
    return pl.BlockSpec(array.shape, lambda *unused: zeros)


def router_parts(router):
    high = lax.reduce_precision(router, 8, 7)
    rest = router - high
    middle = lax.reduce_precision(rest, 8, 7)
    low = rest - middle
    parts = jnp.concatenate([high, middle, low], axis=1)
    return jnp.pad(parts, ((0, 0), (0, SIDE - parts.shape[1]))).astype(bf16)


def shift(value, axis, step, size):
    return lax.ppermute(value, axis, [(i, (i + step) % size) for i in range(size)])


def local(
    tokens, norm_gain1, norm_gain2, att_router, query_maps, kv_maps, out_maps, ffn_router,
    ffn_maps, att_route, ffn_route, parents, cotangent,
):
    rows, dim = tokens.shape
    group_len = att_route.shape[0]
    zz, xx, tt = lax.axis_index("zz"), lax.axis_index("xx"), lax.axis_index("tensor")
    zs, xs, ts = lax.axis_size("zz"), lax.axis_size("xx"), lax.axis_size("tensor")
    here = jnp.stack([tt]).astype(jnp.int32)
    total = rows * zs * ts
    wide_cols = dim + SIDE

    def exchange(value):
        return lax.all_to_all(value, "zz", 0, 0, tiled=True)

    def swap(half):
        return shift(half, "xx", 1, 2) if xs == 2 else half

    def assemble(halves, others, *ready):
        chunks = len(halves)
        part, width = halves[0].shape[1:]
        if xs == 2:
            full = jnp.zeros((zs, xs, chunks, part, width), bf16)
            full = after(full, *ready) if ready else full
            for n in range(chunks):
                for piece, column in ((halves[n], xx), (others[n], 1 - xx)):
                    full = lax.dynamic_update_slice(
                        full, piece[:, None, None], (0, column, n, 0, 0)
                    )
        else:
            full = jnp.stack([lax.all_gather(h, "xx", axis=1) for h in halves], axis=2)
        return full.reshape(zs * xs * chunks * part, width)

    core, line = tt % 2, tt // 2
    across_core = [(i, i ^ 1) for i in range(ts)]
    across_line = [(i, i ^ 2) for i in range(ts)]

    def gather_line(mine):
        spread_rows = jnp.broadcast_to(mine[None], (zs,) + mine.shape)
        by_zz = exchange(spread_rows)
        return by_zz, lax.ppermute(by_zz, "tensor", across_line)

    def gather_core(by_zz, other_line):
        pair = jnp.zeros((zs, 2) + by_zz.shape[1:], by_zz.dtype)
        for piece, place in ((by_zz, line), (other_line, 1 - line)):
            pair = lax.dynamic_update_slice(pair, piece[:, None], (0, place, 0, 0))
        other_core = lax.ppermute(pair, "tensor", across_core)
        full = jnp.zeros((zs, 2, 2) + by_zz.shape[1:], by_zz.dtype)
        for piece, place in ((pair, core), (other_core, 1 - core)):
            full = lax.dynamic_update_slice(full, piece[:, :, None], (0, 0, place, 0, 0))
        return full.reshape(-1, by_zz.shape[-1])

    def fold(value, axis, place, pairs):
        sent = lax.dynamic_index_in_dim(value, 1 - place, axis, keepdims=False)
        kept = lax.dynamic_index_in_dim(value, place, axis, keepdims=False)
        came = lax.ppermute(sent, "tensor", pairs)
        return (kept.astype(f32) + came.astype(f32)).astype(bf16)

    def return_x(grad, parts=1):
        grad = grad.reshape(zs, xs, -1, grad.shape[1])
        halves = [grad[i * zs // parts : (i + 1) * zs // parts] for i in range(parts)]
        if xs != 2:
            came = [
                lax.psum_scatter(h.transpose(1, 0, 2, 3), "xx", scatter_dimension=0, tiled=False)
                for h in halves
            ]
            return came, jnp.concatenate(came, axis=0)
        came = [
            shift(lax.dynamic_index_in_dim(h, 1 - xx, 1, keepdims=False), "xx", 1, 2)
            for h in halves
        ]
        kept = lax.dynamic_index_in_dim(grad, xx, 1, keepdims=False)
        return came, (kept.astype(f32) + jnp.concatenate(came, 0).astype(f32)).astype(bf16)

    packed = pl.pallas_call(
        pack_kernel,
        grid_spec=pltpu.PrefetchScalarGridSpec(
            num_scalar_prefetch=2,
            grid=(1,),
            in_specs=[
                pl.BlockSpec((rows, dim), lambda i, w, p: (0, 0)),
                pl.BlockSpec((rows, 2), lambda i, w, p: (w[0], 0)),
                pl.BlockSpec((rows, 2), lambda i, w, p: (w[0], 0)),
            ],
            out_specs=pl.BlockSpec((rows, wide_cols), lambda i, w, p: (0, 0)),
        ),
        out_shape=shape((rows, wide_cols), bf16),
        compiler_params=params(),
        name="pack",
    )(here, parents, tokens, att_route, ffn_route)

    group_tokens = lax.all_gather(packed, GROUP, axis=0, tiled=True)
    small = jnp.concatenate(
        [norm_gain1[None], norm_gain2[None], att_router.T, ffn_router.T], axis=0
    )
    devices = zs * xs * ts
    small = jnp.broadcast_to(small.reshape(1, -1), (devices, small.size))
    small = after(small, packed)
    small = lax.all_to_all(small, ALL, 0, 0, tiled=True)
    small = small.reshape(devices, 2 + 2 * EXPERTS, norm_gain1.shape[0])
    small = small.transpose(1, 0, 2).reshape(2 + 2 * EXPERTS, dim)
    gain1, gain2 = small[0:1], small[1:2]
    router1 = jnp.pad(small[2 : 2 + EXPERTS], ((0, 8 - EXPERTS), (0, 0)))
    router2 = jnp.pad(small[2 + EXPERTS :], ((0, 8 - EXPERTS), (0, 0)))
    parts1 = router_parts(small[2 : 2 + EXPERTS].T)
    parts2 = router_parts(small[2 + EXPERTS :].T)

    count = query_maps.shape[0] + kv_maps.shape[0] + out_maps.shape[0]
    part = query_maps.shape[1]
    zz_one = jnp.stack([zz]).astype(jnp.int32)
    vmem = pl.BlockSpec(memory_space=pltpu.VMEM)
    anywhere = pl.BlockSpec(memory_space=pl.ANY)
    by_head = pl.pallas_call(
        split_kernel,
        in_specs=[vmem, vmem, vmem, anywhere],
        out_specs=vmem,
        out_shape=shape((zs, part, count * HS), bf16),
        compiler_params=params(),
        name="split",
    )(query_maps, kv_maps, out_maps, small)
    att_half = exchange(by_head)
    att_other = swap(att_half)
    w_att = assemble([att_half], [att_other])

    cut, width = part // 2, ffn_maps.shape[2]
    cast = pl.pallas_call(
        cast_kernel,
        grid=(EXPERTS,),
        in_specs=[
            pl.BlockSpec((1, part, width), lambda i, kind=kind: (kind * EXPERTS + i, 0, 0))
            for kind in range(3)
        ]
        + [anywhere],
        out_specs=[pl.BlockSpec((1, cut, width), lambda i: (i, 0, 0))] * 6,
        out_shape=[shape((EXPERTS, cut, width), bf16)] * 6,
        compiler_params=params(),
        cost_estimate=wall(),
        name="cast",
    )(ffn_maps, ffn_maps, ffn_maps, by_head)
    chunks = []

    def chunk(n, *ready):
        value = exchange(after(cast[n], *ready))
        chunks.append(value)
        others.append(swap(value))

    others = []
    chunk(0, att_half)
    chunk(1, chunks[0])
    chunk(2, chunks[1], others[0])
    cot_zz, cot_line = gather_line(after(cotangent, chunks[2]))
    chunk(3, cot_zz, others[1])
    chunk(4, chunks[3], others[2])
    chunk(5, chunks[4], others[3])
    w_gate, w_up = [assemble(chunks[n : n + 2], others[n : n + 2]) for n in (0, 2)]

    half = HS // 2
    frequency = rope_base ** (-2.0 * jnp.arange(half, dtype=f32) / HS)
    angles = jnp.arange(group_len, dtype=f32)[:, None] * frequency[None, :]
    cosines, sines = jnp.cos(angles), jnp.sin(angles)
    cos = jnp.concatenate([cosines, cosines], axis=1)
    sin = jnp.concatenate([-sines, sines], axis=1)

    trees = total // group_len
    block = lambda width: pl.BlockSpec((group_len, width), lambda i: (i, 0))
    part_att, x1, kept, gate1 = pl.pallas_call(
        att_fwd_kernel,
        grid=(trees,),
        in_specs=[
            block(wide_cols), whole(w_att), whole(parts1), whole(gain1), whole(cos), whole(sin)
        ],
        out_specs=[block(dim), block(dim), block(6 * HS), block(SIDE)],
        out_shape=[
            shape((total, dim), bf16), shape((total, dim), bf16), shape((total, 6 * HS), bf16),
            shape((total, SIDE), f32),
        ],
        compiler_params=params(),
        cost_estimate=wall(),
        name="att_fwd",
    )(group_tokens, w_att, parts1, gain1, cos, sin)
    part_att = after(part_att, others[0], chunks[1])
    sum_att = lax.psum_scatter(part_att, GROUP, scatter_dimension=0, tiled=True)

    waited = [cot_zz, others[1]]
    packed2, middle, gate2 = pl.pallas_call(
        mid_kernel,
        in_specs=[vmem] * 4 + [pl.BlockSpec(memory_space=pl.ANY)] * len(waited),
        out_shape=[shape((rows, wide_cols), bf16), shape((rows, dim), f32), shape((rows, SIDE), f32)],
        compiler_params=params(),
        cost_estimate=wall(),
        name="mid",
    )(sum_att, packed, gain2, parts2, *waited)
    x2 = lax.all_gather(packed2, GROUP, axis=0, tiled=True)

    step = 512
    steps = (total // step,)
    rows_of = lambda w: pl.BlockSpec((step, w), lambda i, *s: (i, 0))
    side_of = pl.BlockSpec((step, SIDE), lambda i, *s: (i, dim // SIDE))
    fixed = pl.BlockSpec(
        (dim, width), lambda i, *s: (0, 0), pipeline_mode=pl.Buffered(buffer_count=1)
    )
    gate_h, up_h, act = pl.pallas_call(
        ffn_fwd_kernel,
        grid_spec=pltpu.PrefetchScalarGridSpec(
            num_scalar_prefetch=1,
            grid=steps,
            in_specs=[rows_of(wide_cols), fixed, fixed],
            out_specs=[rows_of(width)] * 3,
        ),
        out_shape=[shape((total, width), bf16)] * 3,
        compiler_params=params(),
        cost_estimate=wall(),
        name="ffn_fwd",
    )(zz_one, x2, w_gate, w_up)
    group_cot = gather_core(cot_zz, cot_line)
    down_grad = dot_tn(group_cot, act).astype(bf16)
    down_came, down_sum = return_x(down_grad, 2)
    w_down = assemble(chunks[4:], others[4:], act)
    gate_grad, up_grad, part2 = pl.pallas_call(
        ffn_act_kernel,
        grid_spec=pltpu.PrefetchScalarGridSpec(
            num_scalar_prefetch=1,
            grid=steps,
            in_specs=[
                side_of, rows_of(width), rows_of(width), rows_of(dim), fixed, anywhere
            ],
            out_specs=[rows_of(width)] * 2 + [rows_of(SIDE)],
        ),
        out_shape=[shape((total, width), bf16)] * 2 + [shape((total, SIDE), bf16)],
        compiler_params=params(),
        cost_estimate=wall(),
        name="ffn_act",
    )(zz_one, x2, gate_h, up_h, group_cot, w_down, down_grad)
    back2 = pl.pallas_call(
        ffn_back_kernel,
        grid=steps,
        in_specs=[rows_of(width), rows_of(width), rows_of(SIDE), fixed, fixed, anywhere],
        out_specs=rows_of(wide_cols),
        out_shape=shape((total, wide_cols), bf16),
        compiler_params=params(),
        cost_estimate=wall(),
        name="ffn_back",
    )(gate_grad, up_grad, part2, w_gate, w_up, down_came[0])
    sum_back2 = lax.psum_scatter(back2, GROUP, scatter_dimension=0, tiled=True)

    x2_low = x2[:, :dim]
    gate_dw = dot_tn(x2_low, after(gate_grad, down_sum, back2)).astype(bf16)
    up_dw = dot_tn(x2_low, after(up_grad, gate_dw)).astype(bf16)
    gate_came, gate_sum = return_x(gate_dw)
    up_came, up_sum = return_x(up_dw)
    down_back = exchange(down_sum)
    gate_back = exchange(after(gate_sum, down_back))
    up_back = exchange(after(up_sum, gate_back))
    part_ffn = dot_nt(after(act, up_dw), w_down).astype(bf16)
    by_core = fold(part_ffn.reshape(zs, 2, 2, rows, dim), 2, core, across_core)

    def norm_back(route_at, rsb, wide_rows, base, gain, router, gate, gate_at, outs, name, *waited):
        def pick(a):
            return pl.BlockSpec(a.shape, lambda i, w: (0,) * a.ndim)

        return pl.pallas_call(
            functools.partial(norm_back_kernel, route_at, 1 + len(outs)),
            grid_spec=pltpu.PrefetchScalarGridSpec(
                num_scalar_prefetch=1,
                grid=(1,),
                in_specs=[
                    pick(rsb), pl.BlockSpec((rows, dim), lambda i, w: (0, 0)), pick(base), pick(gain), pick(router),
                    pl.BlockSpec((rows, SIDE), lambda i, w: (w[0], 0)),
                    pl.BlockSpec((rows, SIDE), lambda i, w: (0, dim // SIDE)),
                ]
                + [anywhere] * len(waited),
                out_specs=[pl.BlockSpec((8, dim), lambda i, w: (0, 0))]
                + [pl.BlockSpec((rows, dim), lambda i, w: (0, 0)) for _ in outs],
            ),
            out_shape=[shape((8, dim), f32)] + [shape((rows, dim), d) for d in outs],
            compiler_params=params(),
            cost_estimate=wall(),
            name=name,
        )(gate_at, rsb, wide_rows, base, gain, router, gate, packed, *waited)

    zero = jnp.zeros((1,), jnp.int32)
    parts_ffn, middle_grad, att_cot = norm_back(
        7, sum_back2, middle, cotangent, gain2, router2, gate2, zero, [f32, bf16], "mid_back",
        down_back, gate_sum, part_ffn,
    )
    group_att_cot = lax.all_gather(att_cot, GROUP, axis=0, tiled=True)

    group_att_cot = after(group_att_cot, gate_back, up_sum, by_core)
    back1, grad_qkv, z = pl.pallas_call(
        att_bwd_kernel,
        grid=(trees,),
        in_specs=[
            block(dim), whole(w_att), block(6 * HS), block(SIDE),
            pl.BlockSpec((group_len, SIDE), lambda i: (i, dim // SIDE)), whole(cos), whole(sin),
        ],
        out_specs=[block(wide_cols), block(6 * HS), block(EXPERTS * HS)],
        out_shape=[
            shape((total, wide_cols), bf16), shape((total, 6 * HS), bf16),
            shape((total, EXPERTS * HS), bf16),
        ],
        compiler_params=params(),
        cost_estimate=wall(),
        name="att_bwd",
    )(group_att_cot, w_att, kept, gate1, group_tokens, cos, sin)
    sum_back1 = lax.psum_scatter(back1, GROUP, scatter_dimension=0, tiled=True)

    grad_att = jnp.concatenate(
        [dot_tn(x1, grad_qkv).astype(bf16), dot_tn(group_att_cot, z).astype(bf16)], axis=1
    )
    by_line = fold(after(by_core, grad_att), 1, line, across_line)
    att_sum = return_x(grad_att)[1]
    att_back = exchange(after(att_sum, up_back))
    mixed_zz = exchange(after(by_line, up_back, att_sum))
    query_grad, kv_grad, out_grad = pl.pallas_call(
        join_kernel,
        in_specs=[vmem],
        out_specs=[vmem] * 3,
        out_shape=[shape(a.shape, f32) for a in (query_maps, kv_maps, out_maps)],
        compiler_params=params(),
        name="join",
    )(att_back)
    ffn_out = jnp.concatenate([v.astype(f32) for v in (gate_back, up_back, down_back)], axis=0)

    mixed = (middle + jnp.sum(mixed_zz.astype(f32), axis=0)).astype(bf16)

    parts_att, input_grad = norm_back(
        0, sum_back1, tokens, middle_grad, gain1, router1, gate1,
        (zz * ts + tt)[None].astype(jnp.int32), [bf16], "input_back",
    )

    used = EXPERTS + 1
    parts = jnp.concatenate([parts_ffn[:used], parts_att[:used]], axis=0)
    parts = parts.reshape(2 * used, devices, -1).transpose(1, 0, 2).reshape(devices, -1)
    parts = jnp.sum(lax.all_to_all(parts, ALL, 0, 0, tiled=True), axis=0).reshape(2, used, -1)
    ffn_router_grad, gain2_grad = parts[0, :EXPERTS].T, parts[0, EXPERTS]
    att_router_grad, gain1_grad = parts[1, :EXPERTS].T, parts[1, EXPERTS]
    return (
        mixed,
        input_grad,
        gain1_grad,
        gain2_grad,
        att_router_grad,
        query_grad,
        kv_grad,
        out_grad,
        ffn_router_grad,
        ffn_out,
    )


def solution(mesh):
    dp, tensor = mesh.shape["dp"], mesh.shape["tensor"]
    fine = Mesh(mesh.devices.reshape(EXPERTS, dp // EXPERTS, tensor), ALL)
    dps = ("zz", "xx")
    rows, flat, maps = P(ALL, None), P(ALL), P(None, dps, "tensor")
    placed = (
        rows, flat, flat, rows, maps, maps, maps, rows, maps, P(dps, None), P(dps, None), P(dps), rows
    )
    return jax.shard_map(
        local,
        mesh=fine,
        in_specs=placed,
        out_specs=(rows, rows, flat, flat, rows, maps, maps, maps, rows, maps),
        check_vma=False,
    )
```

```python
import functools

import jax
import jax.numpy as jnp
from jax import lax
from jax.experimental import pallas as pl
from jax.experimental.pallas import tpu as pltpu
from jax.sharding import Mesh, PartitionSpec as P

EXPERTS = 4
HS = 128
SEG = 128
SIDE = 128
epsilon = 1e-05
rope_base = 10000.0
f32 = jnp.float32
bf16 = jnp.bfloat16
ALL = ("zz", "xx", "tensor")
GROUP = ("zz", "tensor")
VMEM = 60 * 1024 * 1024


def dot(a, b):
    return lax.dot_general(a, b, (((1,), (0,)), ((), ())), preferred_element_type=f32)


def dot_nt(a, b):
    return lax.dot_general(a, b, (((1,), (1,)), ((), ())), preferred_element_type=f32)


def dot_tn(a, b):
    return lax.dot_general(a, b, (((0,), (0,)), ((), ())), preferred_element_type=f32)


def lanes(rows):
    return lax.broadcasted_iota(jnp.int32, (rows, SIDE), 1).astype(f32)


def put(columns, rows):
    lane = lanes(rows)
    out = jnp.zeros((rows, SIDE), f32)
    for place, column in columns.items():
        out = jnp.where(lane == place, column, out)
    return out


def norm_scale(rows):
    return lax.rsqrt(jnp.mean(rows * rows, axis=-1, keepdims=True) + epsilon)


def gate_probs(low, router_parts, route0, route1):
    rows = low.shape[0]
    parts = dot(low, router_parts)
    lane = lanes(rows)
    logits = (
        parts
        + pltpu.roll(parts, SIDE - EXPERTS, 1)
        + pltpu.roll(parts, SIDE - 2 * EXPERTS, 1)
    )
    c0 = jnp.sum(jnp.where(lane == route0, logits, 0.0), axis=1, keepdims=True)
    c1 = jnp.sum(jnp.where(lane == route1, logits, 0.0), axis=1, keepdims=True)
    top = jnp.maximum(c0, c1)
    e0 = jnp.exp(c0 - top)
    e1 = jnp.exp(c1 - top)
    total = e0 + e1
    return put({0: e0 / total, 1: e1 / total}, rows)


def choose(wide, route):
    out = wide[:, :HS]
    for e in range(1, EXPERTS):
        out = jnp.where(route == e, wide[:, e * HS : (e + 1) * HS], out)
    return out


def spread(slots, routes):
    blocks = []
    for e in range(EXPERTS):
        block = jnp.where(routes[0] == e, slots[0], 0.0)
        blocks.append(block + jnp.where(routes[1] == e, slots[1], 0.0))
    return blocks


def rope_rows(depth, table_ref):
    segments = table_ref.shape[0] // SEG
    out = table_ref[0:SEG, :]
    for d in range(1, segments):
        out = jnp.where(depth == d, table_ref[d * SEG : (d + 1) * SEG, :], out)
    return out


def allow_mask(side, seg):
    rows = side[seg * SEG : (seg + 1) * SEG]
    blocks = [jnp.broadcast_to(rows[:, 2 + b : 3 + b], (SEG, SEG)) for b in range(seg)]
    later = lax.broadcasted_iota(jnp.int32, (SEG, SEG), 1)
    here = lax.broadcasted_iota(jnp.int32, (SEG, SEG), 0)
    blocks.append((later <= here).astype(f32))
    mask = jnp.concatenate(blocks, axis=1) if seg else blocks[0]
    return jnp.concatenate([mask, mask], axis=0)


def weights_of(queries, keys, mask):
    scores = dot_nt(queries, keys) * (HS**-0.5)
    scores = jnp.where(mask > 0.5, scores, -1e30)
    top = jnp.max(scores, axis=-1, keepdims=True)
    exponent = jnp.exp(scores - top)
    return exponent / jnp.sum(exponent, axis=-1, keepdims=True)


def by_core(ref, core):
    half = ref.shape[0] // 4
    parts = []
    for other in range(2):
        for line in range(2):
            first = (2 * line + lax.rem(core + other, 2)) * half
            parts.append(ref[pl.ds(pl.multiple_of(first, half), half), :])
    return jnp.concatenate(parts, axis=0)


def split_rows(value, kept_ref, sent_ref, columns):
    half = value.shape[0] // 4
    for i, ref in enumerate((kept_ref, kept_ref, sent_ref, sent_ref)):
        ref[i % 2, 0, :, columns] = value[i * half : (i + 1) * half]


def pack_kernel(where_ref, parents_ref, tok_ref, att_ref, ffn_ref, out_ref):
    rows = tok_ref.shape[0]
    dim = tok_ref.shape[1]
    out_ref[:, :dim] = tok_ref[...]
    segments = parents_ref.shape[0]
    current = where_ref[0]
    reached = [current == b for b in range(segments)]
    for step in range(segments - 1):
        parent = parents_ref[jnp.maximum(current, 0)]
        current = jnp.where(current > 0, parent, 0)
        reached = [r | (current == b) for b, r in enumerate(reached)]
    flags = [jnp.where(r, 1.0, 0.0) for r in reached]
    depth = functools.reduce(lambda a, b: a + b, flags) - 1.0
    att = att_ref[...].astype(f32)
    ffn = ffn_ref[...].astype(f32)
    columns = {0: att[:, 0:1], 1: att[:, 1:2], 6: depth, 7: ffn[:, 0:1], 8: ffn[:, 1:2]}
    for b in range(segments):
        columns[2 + b] = flags[b]
    out_ref[:, dim:] = put(columns, rows).astype(bf16)


def att_fwd_kernel(
    core_ref, tok_ref, w_ref, router_ref, gain_ref, cos_ref, sin_ref, kept_ref, sent_ref, x_ref,
    keep_ref, gate_ref, z_ref
):
    dim = x_ref.shape[1]
    rows = x_ref.shape[0]
    side = tok_ref[:, dim:].astype(f32)
    wide = tok_ref[:, :dim].astype(f32)
    x = (wide * norm_scale(wide) * gain_ref[...]).astype(bf16)
    x_ref[...] = x
    qkv_width = (EXPERTS + 2) * HS
    qkv = dot(x, w_ref[:, :qkv_width])
    routes = (side[:, 0:1], side[:, 1:2])
    probs = gate_probs(x, router_ref[...], routes[0], routes[1])
    gate_ref[...] = probs
    gates = probs.astype(bf16).astype(f32)
    segments = rows // SEG
    cos, sin = [], []
    for a in range(segments):
        depth = side[a * SEG : (a + 1) * SEG, 6:7]
        cos.append(rope_rows(depth, cos_ref))
        sin.append(rope_rows(depth, sin_ref))
    cos = jnp.concatenate(cos, axis=0)
    sin = jnp.concatenate(sin, axis=0)

    def turn(v):
        return (v * cos + pltpu.roll(v, HS // 2, 1) * sin).astype(bf16)

    q = [turn(choose(qkv, r)) for r in routes]
    k = turn(qkv[:, EXPERTS * HS : (EXPERTS + 1) * HS])
    v = qkv[:, (EXPERTS + 1) * HS :].astype(bf16)
    heads = [[], []]
    for a in range(segments):
        here = slice(a * SEG, (a + 1) * SEG)
        upto = (a + 1) * SEG
        qa = jnp.concatenate([q[0][here], q[1][here]], axis=0)
        p = weights_of(qa, k[:upto], allow_mask(side, a))
        o = dot(p.astype(bf16), v[:upto]).astype(bf16)
        heads[0].append(o[:SEG])
        heads[1].append(o[SEG:])
    heads = [jnp.concatenate(h, axis=0) for h in heads]
    for i, piece in enumerate([q[0], q[1], k, v, heads[0], heads[1]]):
        keep_ref[:, i * HS : (i + 1) * HS] = piece
    gated = [gates[:, s : s + 1] * heads[s].astype(f32) for s in range(2)]
    z_ref[...] = jnp.concatenate([b.astype(bf16) for b in spread(gated, routes)], axis=1)
    part = dot_nt(by_core(z_ref, core_ref[0]), w_ref[:, qkv_width:]).astype(bf16)
    split_rows(part, kept_ref, sent_ref, slice(None))


def att_bwd_kernel(
    core_ref, c_ref, w_ref, keep_ref, gate_ref, side_ref, cos_ref, sin_ref, kept_ref, sent_ref,
    grad_ref, z_ref, part_ref
):
    dim = c_ref.shape[1]
    rows = c_ref.shape[0]
    qkv_width = (EXPERTS + 2) * HS
    side = side_ref[...].astype(f32)
    routes = (side[:, 0:1], side[:, 1:2])
    gates = gate_ref[...].astype(bf16).astype(f32)
    g = dot(c_ref[...], w_ref[:, qkv_width:])
    q = [keep_ref[:, :HS], keep_ref[:, HS : 2 * HS]]
    k = keep_ref[:, 2 * HS : 3 * HS]
    v = keep_ref[:, 3 * HS : 4 * HS]
    heads = [keep_ref[:, 4 * HS : 5 * HS].astype(f32), keep_ref[:, 5 * HS :].astype(f32)]
    chosen = [choose(g, r) for r in routes]
    parts = [jnp.sum(heads[s] * chosen[s], axis=1, keepdims=True) for s in range(2)]
    hg = [(gates[:, s : s + 1] * chosen[s]).astype(bf16) for s in range(2)]
    gated = [gates[:, s : s + 1] * heads[s] for s in range(2)]
    for e, block in enumerate(spread(gated, routes)):
        z_ref[:, e * HS : (e + 1) * HS] = block.astype(bf16)
    segments = rows // SEG
    dk = [jnp.zeros((SEG, HS), f32) for _ in range(segments)]
    dv = [jnp.zeros((SEG, HS), f32) for _ in range(segments)]
    dq = [[], []]
    for a in range(segments):
        here = slice(a * SEG, (a + 1) * SEG)
        upto = (a + 1) * SEG
        qa = jnp.concatenate([q[0][here], q[1][here]], axis=0)
        ha = jnp.concatenate([hg[0][here], hg[1][here]], axis=0)
        p = weights_of(qa, k[:upto], allow_mask(side, a))
        pg = dot_nt(ha, v[:upto])
        sg = (p * (pg - jnp.sum(p * pg, axis=-1, keepdims=True))).astype(bf16)
        dqa = dot(sg, k[:upto]) * (HS**-0.5)
        dq[0].append(dqa[:SEG])
        dq[1].append(dqa[SEG:])
        dka = dot_tn(sg, qa) * (HS**-0.5)
        dva = dot_tn(p.astype(bf16), ha)
        for b in range(a + 1):
            dk[b] = dk[b] + dka[b * SEG : (b + 1) * SEG]
            dv[b] = dv[b] + dva[b * SEG : (b + 1) * SEG]
    cos, sin = [], []
    for a in range(segments):
        depth = side[a * SEG : (a + 1) * SEG, 6:7]
        cos.append(rope_rows(depth, cos_ref))
        sin.append(rope_rows(depth, sin_ref))
    cos = jnp.concatenate(cos, axis=0)
    sin = jnp.concatenate(sin, axis=0)

    def unturn(v):
        return v * cos - pltpu.roll(v, HS // 2, 1) * sin

    dq = [unturn(jnp.concatenate(d, axis=0)) for d in dq]
    blocks = spread(dq, routes) + [unturn(jnp.concatenate(dk, axis=0)), jnp.concatenate(dv, axis=0)]
    grad = jnp.concatenate([b.astype(bf16) for b in blocks], axis=1)
    grad_ref[...] = grad
    part_ref[...] = put({0: parts[0], 1: parts[1]}, rows).astype(bf16)
    core = core_ref[0]
    back = dot_nt(by_core(grad_ref, core), w_ref[:, :qkv_width]).astype(bf16)
    split_rows(back, kept_ref, sent_ref, slice(0, dim))
    split_rows(by_core(part_ref, core), kept_ref, sent_ref, slice(dim, dim + SIDE))


def att_grad_kernel(x_ref, c_ref, grad_ref, z_ref, wait_ref, out_ref):
    width = grad_ref.shape[1]
    out_ref[:, :width] = dot_tn(x_ref[...], grad_ref[...]).astype(bf16)
    out_ref[:, width:] = dot_tn(c_ref[...], z_ref[...]).astype(bf16)


def mid_kernel(rs_ref, packed_ref, gain_ref, router_ref, *refs):
    out_ref, middle_ref, gate_ref = refs[-3:]
    rows, dim = rs_ref.shape
    side = packed_ref[:, dim:].astype(f32)
    middle = packed_ref[:, :dim].astype(f32) + rs_ref[...].astype(f32)
    middle_ref[...] = middle
    low = (middle * norm_scale(middle) * gain_ref[...]).astype(bf16)
    out_ref[:, :dim] = low
    probs = gate_probs(low, router_ref[...], side[:, 7:8], side[:, 8:9])
    gate_ref[...] = probs
    out_ref[:, dim:] = put(
        {0: probs[:, 0:1], 1: probs[:, 1:2], 2: side[:, 7:8], 3: side[:, 8:9]}, rows
    ).astype(bf16)


def norm_back_kernel(
    route_at, outs, where_ref, rsb_ref, rows_ref, base_ref, gain_ref, router_ref, gate_ref, side_ref,
    *refs
):
    out_refs = refs[-outs:]
    count, dim = rows_ref.shape
    grad = rsb_ref[:, :dim].astype(f32)
    gp = rsb_ref[:, dim:].astype(f32)
    side = side_ref[...].astype(f32)
    p0, p1 = gate_ref[:, 0:1], gate_ref[:, 1:2]
    q0, q1 = gp[:, 0:1], gp[:, 1:2]
    inner = p0 * q0 + p1 * q1
    i0, i1 = p0 * (q0 - inner), p1 * (q1 - inner)
    rows = rows_ref[...].astype(f32)
    scale = norm_scale(rows)
    normal = rows * scale
    gain = gain_ref[...]
    low = (normal * gain).astype(bf16).astype(f32)
    route0, route1 = side[:, route_at : route_at + 1], side[:, route_at + 1 : route_at + 2]
    parts = []
    for e in range(EXPERTS):
        logit_grad = jnp.where(route0 == e, i0, 0.0) + jnp.where(route1 == e, i1, 0.0)
        grad = grad + logit_grad * router_ref[e : e + 1, :]
        parts.append(jnp.sum(logit_grad * low, axis=0, keepdims=True))
    parts.append(jnp.sum(grad * normal, axis=0, keepdims=True))
    parts.append(jnp.zeros((8 - len(parts), dim), f32))
    out_refs[0][...] = jnp.concatenate(parts, axis=0)
    weighted = grad * gain
    total = base_ref[...].astype(f32) + scale * (
        weighted - normal * jnp.mean(weighted * normal, axis=-1, keepdims=True)
    )
    for ref in out_refs[1:]:
        ref[...] = total.astype(ref.dtype)


def ffn_coef(side, mine):
    in0, in1 = side[:, 2:3] == mine, side[:, 3:4] == mine
    return in0, in1, jnp.where(in0, side[:, 0:1], 0.0) + jnp.where(in1, side[:, 1:2], 0.0)


def ffn_fwd_kernel(where_ref, x_ref, wg_ref, wu_ref, gate_ref, up_ref, a_ref):
    dim = wg_ref.shape[0]
    side = x_ref[:, dim:].astype(f32)
    coef = ffn_coef(side, where_ref[0].astype(f32))[2]
    x = x_ref[:, :dim]
    gate = dot(x, wg_ref[...])
    up = dot(x, wu_ref[...])
    gate_ref[...] = gate.astype(bf16)
    up_ref[...] = up.astype(bf16)
    a_ref[...] = (gate * jax.nn.sigmoid(gate) * up * coef).astype(bf16)


def ffn_act_kernel(
    where_ref, side_ref, gate_ref, up_ref, c_ref, wd_ref, wait_ref, gg_ref, ug_ref, part_ref
):
    rows = c_ref.shape[0]
    in0, in1, coef = ffn_coef(side_ref[...].astype(f32), where_ref[0].astype(f32))
    gate = gate_ref[...].astype(f32)
    up = up_ref[...].astype(f32)
    act_grad = dot(c_ref[...], wd_ref[...])
    sig = jax.nn.sigmoid(gate)
    silu = gate * sig
    part = jnp.sum(silu * up * act_grad, axis=-1, keepdims=True)
    act_grad = act_grad * coef
    gg_ref[...] = (act_grad * up * sig * (1.0 + gate * (1.0 - sig))).astype(bf16)
    ug_ref[...] = (act_grad * silu).astype(bf16)
    part_ref[...] = put(
        {0: jnp.where(in0, part, 0.0), 1: jnp.where(in1, part, 0.0)}, rows
    ).astype(bf16)


def ffn_back_kernel(
    core_ref, gg_ref, ug_ref, part_ref, wg_ref, wu_ref, wait_ref, kept_ref, sent_ref
):
    dim = wg_ref.shape[0]
    core = core_ref[0]
    back = dot_nt(by_core(gg_ref, core), wg_ref[...]) + dot_nt(by_core(ug_ref, core), wu_ref[...])
    split_rows(back.astype(bf16), kept_ref, sent_ref, slice(0, dim))
    split_rows(by_core(part_ref, core), kept_ref, sent_ref, slice(dim, dim + SIDE))


def split_kernel(query_ref, kv_ref, out_ref, wait_ref, *piece_refs):
    cut = piece_refs[0].shape[1]
    for n, piece_ref in enumerate(piece_refs):
        for head in range(piece_ref.shape[0]):
            place = 0
            for ref in (query_ref, kv_ref, out_ref):
                for m in range(ref.shape[0]):
                    rows = ref[m, n * cut : (n + 1) * cut, head * HS : (head + 1) * HS]
                    piece_ref[head, :, place : place + HS] = rows.astype(bf16)
                    place += HS


def cast_kernel(*refs):
    kinds = (len(refs) - 1) // 3
    for kind in range(kinds):
        first, second = refs[kinds + 1 + 2 * kind : kinds + 3 + 2 * kind]
        cut = first.shape[1]
        first[...] = refs[kind][:, :cut].astype(bf16)
        second[...] = refs[kind][:, cut:].astype(bf16)


def join_kernel(piece_ref, *outs):
    for head in range(piece_ref.shape[0]):
        place = 0
        for ref in outs:
            for m in range(ref.shape[0]):
                rows = piece_ref[head, :, place : place + HS]
                ref[m, :, head * HS : (head + 1) * HS] = rows.astype(f32)
                place += HS


def after(value, *waited):
    def body(*refs):
        pass

    anywhere = pl.BlockSpec(memory_space=pl.ANY)
    return pl.pallas_call(
        body,
        in_specs=[anywhere] * (1 + len(waited)),
        out_specs=anywhere,
        out_shape=shape(value.shape, value.dtype),
        input_output_aliases={0: 0},
        cost_estimate=cost(1e6, 1e3),
        name="after",
    )(value, *waited)


def params():
    return pltpu.CompilerParams(vmem_limit_bytes=VMEM)


def cost(flops, nbytes):
    return pl.CostEstimate(flops=int(flops), bytes_accessed=int(nbytes), transcendentals=0)


def wall():
    return cost(2e11, 1e6)


def shape(dims, dtype):
    return jax.ShapeDtypeStruct(dims, dtype)


def whole(array):
    zeros = (0,) * array.ndim
    return pl.BlockSpec(array.shape, lambda *unused: zeros)


def router_parts(router):
    high = lax.reduce_precision(router, 8, 7)
    rest = router - high
    middle = lax.reduce_precision(rest, 8, 7)
    low = rest - middle
    parts = jnp.concatenate([high, middle, low], axis=1)
    return jnp.pad(parts, ((0, 0), (0, SIDE - parts.shape[1]))).astype(bf16)


def shift(value, axis, step, size):
    return lax.ppermute(value, axis, [(i, (i + step) % size) for i in range(size)])


def local(
    tokens, norm_gain1, norm_gain2, att_router, query_maps, kv_maps, out_maps, ffn_router,
    ffn_maps, att_route, ffn_route, parents, cotangent,
):
    rows, dim = tokens.shape
    group_len = att_route.shape[0]
    zz, xx, tt = lax.axis_index("zz"), lax.axis_index("xx"), lax.axis_index("tensor")
    zs, xs, ts = lax.axis_size("zz"), lax.axis_size("xx"), lax.axis_size("tensor")
    here = jnp.stack([tt]).astype(jnp.int32)
    total = rows * zs * ts
    wide_cols = dim + SIDE

    def exchange(value):
        return lax.all_to_all(value, "zz", 0, 0, tiled=True)

    def swap(half):
        return shift(half, "xx", 1, 2) if xs == 2 else half

    def assemble(halves, others, *ready):
        chunks = len(halves)
        part, width = halves[0].shape[1:]
        if xs == 2:
            full = jnp.zeros((zs, xs, chunks, part, width), bf16)
            for n in range(chunks):
                if ready and n == chunks - 1:
                    full = after(full, *ready)
                for piece, column in ((halves[n], xx), (others[n], 1 - xx)):
                    full = lax.dynamic_update_slice(
                        full, piece[:, None, None], (0, column, n, 0, 0)
                    )
        else:
            full = jnp.stack([lax.all_gather(h, "xx", axis=1) for h in halves], axis=2)
        return full.reshape(zs * xs * chunks * part, width)

    core, line = tt % 2, tt // 2
    across_core = [(i, i ^ 1) for i in range(ts)]
    across_line = [(i, i ^ 2) for i in range(ts)]

    def gather_line(mine):
        by_zz = lax.all_gather(mine, "zz", axis=0)
        return by_zz, lax.ppermute(by_zz, "tensor", across_line)

    def gather_core(by_zz, other_line):
        pair = jnp.zeros((zs, 2) + by_zz.shape[1:], by_zz.dtype)
        for piece, place in ((by_zz, line), (other_line, 1 - line)):
            pair = lax.dynamic_update_slice(pair, piece[:, None], (0, place, 0, 0))
        other_core = lax.ppermute(pair, "tensor", across_core)
        full = jnp.zeros((zs, 2, 2) + by_zz.shape[1:], by_zz.dtype)
        for piece, place in ((pair, core), (other_core, 1 - core)):
            full = lax.dynamic_update_slice(full, piece[:, :, None], (0, 0, place, 0, 0))
        return full.reshape(-1, by_zz.shape[-1])

    def fold(value, axis, place, pairs):
        sent = lax.dynamic_index_in_dim(value, 1 - place, axis, keepdims=False)
        kept = lax.dynamic_index_in_dim(value, place, axis, keepdims=False)
        came = lax.ppermute(sent, "tensor", pairs)
        return (kept.astype(f32) + came.astype(f32)).astype(bf16)

    core_one = jnp.stack([core]).astype(jnp.int32)
    smem = pl.BlockSpec(memory_space=pltpu.SMEM)
    segment = group_len // 4

    def halves_of(w):
        return [pl.BlockSpec((2, 1, segment, w), lambda i, *s: (0, i, 0, 0))] * 2

    def halves_shape(w):
        return [shape((2, zs, segment, w), bf16)] * 2

    def add(one, two):
        return (one.astype(f32) + two.astype(f32)).astype(bf16)

    def sum_core(kept, sent):
        came = lax.ppermute(sent, "tensor", across_core)
        pick = lambda v, place: lax.dynamic_index_in_dim(v, place, 0, keepdims=False)
        return [add(pick(kept, place), pick(came, place)) for place in (1 - line, line)]

    def sum_line(sent, kept):
        return add(kept, lax.ppermute(sent, "tensor", across_line))

    def return_x(grad, parts=1):
        grad = grad.reshape(zs, xs, -1, grad.shape[1])
        halves = [grad[i * zs // parts : (i + 1) * zs // parts] for i in range(parts)]
        if xs != 2:
            came = [
                lax.psum_scatter(h.transpose(1, 0, 2, 3), "xx", scatter_dimension=0, tiled=False)
                for h in halves
            ]
            return halves, came, jnp.concatenate(came, axis=0)
        sent = [lax.dynamic_index_in_dim(h, 1 - xx, 1, keepdims=False) for h in halves]
        came = [shift(h, "xx", 1, 2) for h in sent]
        kept = lax.dynamic_index_in_dim(grad, xx, 1, keepdims=False)
        return sent, came, (kept.astype(f32) + jnp.concatenate(came, 0).astype(f32)).astype(bf16)

    packed = pl.pallas_call(
        pack_kernel,
        grid_spec=pltpu.PrefetchScalarGridSpec(
            num_scalar_prefetch=2,
            grid=(1,),
            in_specs=[
                pl.BlockSpec((rows, dim), lambda i, w, p: (0, 0)),
                pl.BlockSpec((rows, 2), lambda i, w, p: (w[0], 0)),
                pl.BlockSpec((rows, 2), lambda i, w, p: (w[0], 0)),
            ],
            out_specs=pl.BlockSpec((rows, wide_cols), lambda i, w, p: (0, 0)),
        ),
        out_shape=shape((rows, wide_cols), bf16),
        compiler_params=params(),
        name="pack",
    )(here, parents, tokens, att_route, ffn_route)

    group_tokens = lax.all_gather(packed, GROUP, axis=0, tiled=True)
    small = jnp.concatenate(
        [norm_gain1[None], norm_gain2[None], att_router.T, ffn_router.T], axis=0
    )
    devices = zs * xs * ts
    small = jnp.broadcast_to(small.reshape(1, -1), (devices, small.size))
    small = after(small, packed)
    small = lax.all_to_all(small, ALL, 0, 0, tiled=True)
    small = small.reshape(devices, 2 + 2 * EXPERTS, norm_gain1.shape[0])
    small = small.transpose(1, 0, 2).reshape(2 + 2 * EXPERTS, dim)
    gain1, gain2 = small[0:1], small[1:2]
    router1 = jnp.pad(small[2 : 2 + EXPERTS], ((0, 8 - EXPERTS), (0, 0)))
    router2 = jnp.pad(small[2 + EXPERTS :], ((0, 8 - EXPERTS), (0, 0)))
    parts1 = router_parts(small[2 : 2 + EXPERTS].T)
    parts2 = router_parts(small[2 + EXPERTS :].T)

    count = query_maps.shape[0] + kv_maps.shape[0] + out_maps.shape[0]
    part = query_maps.shape[1]
    zz_one = jnp.stack([zz]).astype(jnp.int32)
    vmem = pl.BlockSpec(memory_space=pltpu.VMEM)
    anywhere = pl.BlockSpec(memory_space=pl.ANY)
    cut, width = part // 2, ffn_maps.shape[2]
    by_head = pl.pallas_call(
        split_kernel,
        in_specs=[vmem, vmem, vmem, anywhere],
        out_specs=[vmem] * 2,
        out_shape=[shape((zs, cut, count * HS), bf16)] * 2,
        compiler_params=params(),
        name="split",
    )(query_maps, kv_maps, out_maps, small)
    att_first = exchange(by_head[0])
    att_half = exchange(after(by_head[1], att_first))
    w_att = assemble([att_first, att_half], [swap(att_first), swap(att_half)])

    cast = pl.pallas_call(
        cast_kernel,
        grid=(EXPERTS,),
        in_specs=[
            pl.BlockSpec((1, part, width), lambda i, kind=kind: (kind * EXPERTS + i, 0, 0))
            for kind in range(3)
        ]
        + [anywhere],
        out_specs=[pl.BlockSpec((1, cut, width), lambda i: (i, 0, 0))] * 6,
        out_shape=[shape((EXPERTS, cut, width), bf16)] * 6,
        compiler_params=params(),
        cost_estimate=cost(1e6, 6 * ffn_maps.size),
        name="cast",
    )(ffn_maps, ffn_maps, ffn_maps, by_head[0])
    chunks = []

    def chunk(n, *ready):
        value = exchange(after(cast[n], *ready))
        chunks.append(value)
        others.append(swap(value))

    others = []
    chunk(0, att_half)
    chunk(1, chunks[0])
    cot_zz, cot_line = gather_line(after(cotangent, chunks[0]))
    for n in range(2, 6):
        chunk(n, chunks[-1])
    w_gate, w_up = [assemble(chunks[n : n + 2], others[n : n + 2]) for n in (0, 2)]

    half = HS // 2
    frequency = rope_base ** (-2.0 * jnp.arange(half, dtype=f32) / HS)
    angles = jnp.arange(group_len, dtype=f32)[:, None] * frequency[None, :]
    cosines, sines = jnp.cos(angles), jnp.sin(angles)
    cos = jnp.concatenate([cosines, cosines], axis=1)
    sin = jnp.concatenate([-sines, sines], axis=1)

    trees = total // group_len
    block = lambda width: pl.BlockSpec((group_len, width), lambda i: (i, 0))
    kept_att, sent_att, x1, kept, gate1 = pl.pallas_call(
        att_fwd_kernel,
        grid=(trees,),
        in_specs=[
            smem, block(wide_cols), whole(w_att), whole(parts1), whole(gain1), whole(cos), whole(sin)
        ],
        out_specs=[*halves_of(dim), block(dim), block(6 * HS), block(SIDE)],
        out_shape=[
            *halves_shape(dim), shape((total, dim), bf16), shape((total, 6 * HS), bf16),
            shape((total, SIDE), f32),
        ],
        scratch_shapes=[pltpu.VMEM((group_len, EXPERTS * HS), bf16)],
        compiler_params=params(),
        cost_estimate=wall(),
        name="att_fwd",
    )(core_one, group_tokens, w_att, parts1, gain1, cos, sin)
    sent_att = after(sent_att, others[0], chunks[1])
    core_att = sum_core(kept_att, sent_att)
    line_att = after(sum_line(*core_att), cot_zz, others[1])
    sum_att = lax.psum_scatter(line_att, "zz", scatter_dimension=0, tiled=False)

    waited = [chunks[3], others[2], cot_line]
    packed2, middle, gate2 = pl.pallas_call(
        mid_kernel,
        in_specs=[vmem] * 4 + [pl.BlockSpec(memory_space=pl.ANY)] * len(waited),
        out_shape=[shape((rows, wide_cols), bf16), shape((rows, dim), f32), shape((rows, SIDE), f32)],
        compiler_params=params(),
        cost_estimate=wall(),
        name="mid",
    )(sum_att, packed, gain2, parts2, *waited)
    x2 = lax.all_gather(packed2, GROUP, axis=0, tiled=True)

    step = group_len
    steps = (total // step,)
    rows_of = lambda w: pl.BlockSpec((step, w), lambda i, *s: (i, 0))
    side_of = pl.BlockSpec((step, SIDE), lambda i, *s: (i, dim // SIDE))
    fixed = pl.BlockSpec(
        (dim, width), lambda i, *s: (0, 0), pipeline_mode=pl.Buffered(buffer_count=1)
    )
    gate_h, up_h, act = pl.pallas_call(
        ffn_fwd_kernel,
        grid_spec=pltpu.PrefetchScalarGridSpec(
            num_scalar_prefetch=1,
            grid=steps,
            in_specs=[rows_of(wide_cols), fixed, fixed],
            out_specs=[rows_of(width)] * 3,
        ),
        out_shape=[shape((total, width), bf16)] * 3,
        compiler_params=params(),
        cost_estimate=wall(),
        name="ffn_fwd",
    )(zz_one, x2, w_gate, w_up)
    group_cot = gather_core(cot_zz, cot_line)
    down_grad = dot_tn(group_cot, act).astype(bf16)
    down_sent, down_came, down_sum = return_x(down_grad, 2)
    w_down = assemble(chunks[4:], others[4:], act)
    gate_grad, up_grad, part2 = pl.pallas_call(
        ffn_act_kernel,
        grid_spec=pltpu.PrefetchScalarGridSpec(
            num_scalar_prefetch=1,
            grid=steps,
            in_specs=[
                side_of, rows_of(width), rows_of(width), rows_of(dim), fixed, anywhere
            ],
            out_specs=[rows_of(width)] * 2 + [rows_of(SIDE)],
        ),
        out_shape=[shape((total, width), bf16)] * 2 + [shape((total, SIDE), bf16)],
        compiler_params=params(),
        cost_estimate=wall(),
        name="ffn_act",
    )(zz_one, x2, gate_h, up_h, group_cot, w_down, down_grad)
    kept2, sent2 = pl.pallas_call(
        ffn_back_kernel,
        grid=steps,
        in_specs=[smem, rows_of(width), rows_of(width), rows_of(SIDE), fixed, fixed, anywhere],
        out_specs=halves_of(wide_cols),
        out_shape=halves_shape(wide_cols),
        compiler_params=params(),
        cost_estimate=wall(),
        name="ffn_back",
    )(core_one, gate_grad, up_grad, part2, w_gate, w_up, down_came[0])
    core2 = sum_core(kept2, after(sent2, down_came[1]))
    line2 = sum_line(*core2)
    sum_back2 = lax.psum_scatter(line2, "zz", scatter_dimension=0, tiled=False)

    x2_low = x2[:, :dim]
    gate_dw = dot_tn(x2_low, after(gate_grad, core2[0])).astype(bf16)
    up_dw = dot_tn(x2_low, after(up_grad, gate_dw)).astype(bf16)
    gate_sent, gate_came, gate_sum = return_x(gate_dw)
    up_sent, up_came, up_sum = return_x(up_dw)
    down_back = exchange(after(down_sum, core2[0]))
    gate_back = exchange(after(gate_sum, down_back))
    up_back = [exchange(after(up_sum[:, :cut], gate_back))]
    up_back.append(exchange(after(up_sum[:, cut:], up_back[0])))
    part_ffn = dot_nt(after(act, up_dw, line2), w_down).astype(bf16)
    core_ffn = fold(part_ffn.reshape(zs, 2, 2, rows, dim), 2, core, across_core)
    by_line = fold(after(core_ffn, gate_sum), 1, line, across_line)

    def norm_back(route_at, rsb, wide_rows, base, gain, router, gate, gate_at, outs, name, *waited):
        def pick(a):
            return pl.BlockSpec(a.shape, lambda i, w: (0,) * a.ndim)

        return pl.pallas_call(
            functools.partial(norm_back_kernel, route_at, 1 + len(outs)),
            grid_spec=pltpu.PrefetchScalarGridSpec(
                num_scalar_prefetch=1,
                grid=(1,),
                in_specs=[
                    pick(rsb), pl.BlockSpec((rows, dim), lambda i, w: (0, 0)), pick(base), pick(gain), pick(router),
                    pl.BlockSpec((rows, SIDE), lambda i, w: (w[0], 0)),
                    pl.BlockSpec((rows, SIDE), lambda i, w: (0, dim // SIDE)),
                ]
                + [anywhere] * len(waited),
                out_specs=[pl.BlockSpec((8, dim), lambda i, w: (0, 0))]
                + [pl.BlockSpec((rows, dim), lambda i, w: (0, 0)) for _ in outs],
            ),
            out_shape=[shape((8, dim), f32)] + [shape((rows, dim), d) for d in outs],
            compiler_params=params(),
            cost_estimate=wall(),
            name=name,
        )(gate_at, rsb, wide_rows, base, gain, router, gate, packed, *waited)

    zero = jnp.zeros((1,), jnp.int32)
    parts_ffn, middle_grad, att_cot = norm_back(
        7, sum_back2, middle, cotangent, gain2, router2, gate2, zero, [f32, bf16], "mid_back",
        down_back, gate_sum, part_ffn,
    )
    group_att_cot = lax.all_gather(att_cot, GROUP, axis=0, tiled=True)

    group_att_cot = after(group_att_cot, gate_back, up_sum, by_line)
    mixed_rows = lax.psum_scatter(
        after(by_line, group_att_cot), "zz", scatter_dimension=0, tiled=False
    )
    kept1, sent1, grad_qkv, z = pl.pallas_call(
        att_bwd_kernel,
        grid=(trees,),
        in_specs=[
            smem, block(dim), whole(w_att), block(6 * HS), block(SIDE),
            pl.BlockSpec((group_len, SIDE), lambda i: (i, dim // SIDE)), whole(cos), whole(sin),
        ],
        out_specs=[*halves_of(wide_cols), block(6 * HS), block(EXPERTS * HS)],
        out_shape=[
            *halves_shape(wide_cols), shape((total, 6 * HS), bf16),
            shape((total, EXPERTS * HS), bf16),
        ],
        scratch_shapes=[pltpu.VMEM((group_len, SIDE), bf16)],
        compiler_params=params(),
        cost_estimate=wall(),
        name="att_bwd",
    )(core_one, group_att_cot, w_att, kept, gate1, group_tokens, cos, sin)
    core1 = sum_core(kept1, after(sent1, up_back[0]))
    grad_att = pl.pallas_call(
        att_grad_kernel,
        grid=(zs,),
        in_specs=[
            pl.BlockSpec((total, dim // zs), lambda i: (0, i)),
            pl.BlockSpec((total, dim // zs), lambda i: (0, i)),
            whole(grad_qkv), whole(z), anywhere,
        ],
        out_specs=pl.BlockSpec((dim // zs, count * HS), lambda i: (i, 0)),
        out_shape=shape((dim, count * HS), bf16),
        compiler_params=params(),
        cost_estimate=cost(2 * total * dim * count * HS, 6 * total * dim),
        name="att_grad",
    )(x1, group_att_cot, grad_qkv, z, core1[0])
    att_sent, att_came, att_sum = return_x(grad_att)
    line1 = sum_line(core1[0], after(core1[1], *att_sent, mixed_rows, up_back[1]))
    sum_back1 = lax.psum_scatter(line1, "zz", scatter_dimension=0, tiled=False)
    att_back = exchange(after(att_sum, up_back[1]))
    query_grad, kv_grad, out_grad = pl.pallas_call(
        join_kernel,
        in_specs=[vmem],
        out_specs=[vmem] * 3,
        out_shape=[shape(a.shape, f32) for a in (query_maps, kv_maps, out_maps)],
        compiler_params=params(),
        name="join",
    )(att_back)
    ffn_out = jnp.concatenate([v.astype(f32) for v in (gate_back, jnp.concatenate(up_back, axis=1), down_back)], axis=0)

    mixed = (middle + mixed_rows.astype(f32)).astype(bf16)

    parts_att, input_grad = norm_back(
        0, sum_back1, tokens, middle_grad, gain1, router1, gate1,
        (zz * ts + tt)[None].astype(jnp.int32), [bf16], "input_back",
    )

    used = EXPERTS + 1
    parts = jnp.concatenate([parts_ffn[:used], parts_att[:used]], axis=0)
    parts = parts.reshape(2 * used, devices, -1).transpose(1, 0, 2).reshape(devices, -1)
    parts = jnp.sum(lax.all_to_all(parts, ALL, 0, 0, tiled=True), axis=0).reshape(2, used, -1)
    ffn_router_grad, gain2_grad = parts[0, :EXPERTS].T, parts[0, EXPERTS]
    att_router_grad, gain1_grad = parts[1, :EXPERTS].T, parts[1, EXPERTS]
    return (
        mixed,
        input_grad,
        gain1_grad,
        gain2_grad,
        att_router_grad,
        query_grad,
        kv_grad,
        out_grad,
        ffn_router_grad,
        ffn_out,
    )


def solution(mesh):
    dp, tensor = mesh.shape["dp"], mesh.shape["tensor"]
    fine = Mesh(mesh.devices.reshape(EXPERTS, dp // EXPERTS, tensor), ALL)
    dps = ("zz", "xx")
    rows, flat, maps = P(ALL, None), P(ALL), P(None, dps, "tensor")
    placed = (
        rows, flat, flat, rows, maps, maps, maps, rows, maps, P(dps, None), P(dps, None), P(dps), rows
    )
    return jax.shard_map(
        local,
        mesh=fine,
        in_specs=placed,
        out_specs=(rows, rows, flat, flat, rows, maps, maps, maps, rows, maps),
        check_vma=False,
    )
```

```python
import functools

import jax
import jax.numpy as jnp
from jax import lax
from jax.experimental import pallas as pl
from jax.experimental.pallas import tpu as pltpu
from jax.sharding import Mesh, PartitionSpec as P

EXPERTS = 4
HS = 128
SEG = 128
SIDE = 128
epsilon = 1e-05
rope_base = 10000.0
f32 = jnp.float32
bf16 = jnp.bfloat16
ALL = ("zz", "xx", "tensor")
GROUP = ("zz", "tensor")
VMEM = 60 * 1024 * 1024


def dot(a, b):
    return lax.dot_general(a, b, (((1,), (0,)), ((), ())), preferred_element_type=f32)


def dot_nt(a, b):
    return lax.dot_general(a, b, (((1,), (1,)), ((), ())), preferred_element_type=f32)


def dot_tn(a, b):
    return lax.dot_general(a, b, (((0,), (0,)), ((), ())), preferred_element_type=f32)


def lanes(rows):
    return lax.broadcasted_iota(jnp.int32, (rows, SIDE), 1).astype(f32)


def put(columns, rows):
    lane = lanes(rows)
    out = jnp.zeros((rows, SIDE), f32)
    for place, column in columns.items():
        out = jnp.where(lane == place, column, out)
    return out


def norm_scale(rows):
    return lax.rsqrt(jnp.mean(rows * rows, axis=-1, keepdims=True) + epsilon)


def gate_probs(low, router_parts, route0, route1):
    rows = low.shape[0]
    parts = dot(low, router_parts)
    lane = lanes(rows)
    logits = (
        parts
        + pltpu.roll(parts, SIDE - EXPERTS, 1)
        + pltpu.roll(parts, SIDE - 2 * EXPERTS, 1)
    )
    c0 = jnp.sum(jnp.where(lane == route0, logits, 0.0), axis=1, keepdims=True)
    c1 = jnp.sum(jnp.where(lane == route1, logits, 0.0), axis=1, keepdims=True)
    top = jnp.maximum(c0, c1)
    e0 = jnp.exp(c0 - top)
    e1 = jnp.exp(c1 - top)
    total = e0 + e1
    return put({0: e0 / total, 1: e1 / total}, rows)


def choose(wide, route):
    out = wide[:, :HS]
    for e in range(1, EXPERTS):
        out = jnp.where(route == e, wide[:, e * HS : (e + 1) * HS], out)
    return out


def spread(slots, routes):
    blocks = []
    for e in range(EXPERTS):
        block = jnp.where(routes[0] == e, slots[0], 0.0)
        blocks.append(block + jnp.where(routes[1] == e, slots[1], 0.0))
    return blocks


def rope_rows(depth, table_ref):
    segments = table_ref.shape[0] // SEG
    out = table_ref[0:SEG, :]
    for d in range(1, segments):
        out = jnp.where(depth == d, table_ref[d * SEG : (d + 1) * SEG, :], out)
    return out


def allow_mask(side, seg):
    rows = side[seg * SEG : (seg + 1) * SEG]
    blocks = [jnp.broadcast_to(rows[:, 2 + b : 3 + b], (SEG, SEG)) for b in range(seg)]
    later = lax.broadcasted_iota(jnp.int32, (SEG, SEG), 1)
    here = lax.broadcasted_iota(jnp.int32, (SEG, SEG), 0)
    blocks.append((later <= here).astype(f32))
    mask = jnp.concatenate(blocks, axis=1) if seg else blocks[0]
    return jnp.concatenate([mask, mask], axis=0)


def weights_of(queries, keys, mask):
    scores = dot_nt(queries, keys) * (HS**-0.5)
    scores = jnp.where(mask > 0.5, scores, -1e30)
    top = jnp.max(scores, axis=-1, keepdims=True)
    exponent = jnp.exp(scores - top)
    return exponent / jnp.sum(exponent, axis=-1, keepdims=True)


def by_core(ref, core):
    half = ref.shape[0] // 4
    parts = []
    for other in range(2):
        for line in range(2):
            first = (2 * line + lax.rem(core + other, 2)) * half
            parts.append(ref[pl.ds(pl.multiple_of(first, half), half), :])
    return jnp.concatenate(parts, axis=0)


def split_rows(value, kept_ref, sent_ref, columns):
    half = value.shape[0] // 4
    for i, ref in enumerate((kept_ref, kept_ref, sent_ref, sent_ref)):
        ref[i % 2, 0, :, columns] = value[i * half : (i + 1) * half]


def pack_kernel(where_ref, parents_ref, tok_ref, att_ref, ffn_ref, out_ref):
    rows = tok_ref.shape[0]
    dim = tok_ref.shape[1]
    out_ref[:, :dim] = tok_ref[...]
    segments = parents_ref.shape[0]
    current = where_ref[0]
    reached = [current == b for b in range(segments)]
    for step in range(segments - 1):
        parent = parents_ref[jnp.maximum(current, 0)]
        current = jnp.where(current > 0, parent, 0)
        reached = [r | (current == b) for b, r in enumerate(reached)]
    flags = [jnp.where(r, 1.0, 0.0) for r in reached]
    depth = functools.reduce(lambda a, b: a + b, flags) - 1.0
    att = att_ref[...].astype(f32)
    ffn = ffn_ref[...].astype(f32)
    columns = {0: att[:, 0:1], 1: att[:, 1:2], 6: depth, 7: ffn[:, 0:1], 8: ffn[:, 1:2]}
    for b in range(segments):
        columns[2 + b] = flags[b]
    out_ref[:, dim:] = put(columns, rows).astype(bf16)


def att_fwd_kernel(
    core_ref, tok_ref, w_ref, router_ref, gain_ref, cos_ref, sin_ref, kept_ref, sent_ref, x_ref,
    keep_ref, gate_ref, z_ref
):
    dim = x_ref.shape[1]
    rows = x_ref.shape[0]
    side = tok_ref[:, dim:].astype(f32)
    wide = tok_ref[:, :dim].astype(f32)
    x = (wide * norm_scale(wide) * gain_ref[...]).astype(bf16)
    x_ref[...] = x
    qkv_width = (EXPERTS + 2) * HS
    qkv = dot(x, w_ref[:, :qkv_width])
    routes = (side[:, 0:1], side[:, 1:2])
    probs = gate_probs(x, router_ref[...], routes[0], routes[1])
    gate_ref[...] = probs
    gates = probs.astype(bf16).astype(f32)
    segments = rows // SEG
    cos, sin = [], []
    for a in range(segments):
        depth = side[a * SEG : (a + 1) * SEG, 6:7]
        cos.append(rope_rows(depth, cos_ref))
        sin.append(rope_rows(depth, sin_ref))
    cos = jnp.concatenate(cos, axis=0)
    sin = jnp.concatenate(sin, axis=0)

    def turn(v):
        return (v * cos + pltpu.roll(v, HS // 2, 1) * sin).astype(bf16)

    q = [turn(choose(qkv, r)) for r in routes]
    k = turn(qkv[:, EXPERTS * HS : (EXPERTS + 1) * HS])
    v = qkv[:, (EXPERTS + 1) * HS :].astype(bf16)
    heads = [[], []]
    for a in range(segments):
        here = slice(a * SEG, (a + 1) * SEG)
        upto = (a + 1) * SEG
        qa = jnp.concatenate([q[0][here], q[1][here]], axis=0)
        p = weights_of(qa, k[:upto], allow_mask(side, a))
        o = dot(p.astype(bf16), v[:upto]).astype(bf16)
        heads[0].append(o[:SEG])
        heads[1].append(o[SEG:])
    heads = [jnp.concatenate(h, axis=0) for h in heads]
    for i, piece in enumerate([q[0], q[1], k, v, heads[0], heads[1]]):
        keep_ref[:, i * HS : (i + 1) * HS] = piece
    gated = [gates[:, s : s + 1] * heads[s].astype(f32) for s in range(2)]
    z_ref[...] = jnp.concatenate([b.astype(bf16) for b in spread(gated, routes)], axis=1)
    part = dot_nt(by_core(z_ref, core_ref[0]), w_ref[:, qkv_width:]).astype(bf16)
    split_rows(part, kept_ref, sent_ref, slice(None))


def att_bwd_kernel(
    core_ref, c_ref, w_ref, keep_ref, gate_ref, side_ref, cos_ref, sin_ref, kept_ref, sent_ref,
    grad_ref, z_ref, part_ref
):
    dim = c_ref.shape[1]
    rows = c_ref.shape[0]
    qkv_width = (EXPERTS + 2) * HS
    side = side_ref[...].astype(f32)
    routes = (side[:, 0:1], side[:, 1:2])
    gates = gate_ref[...].astype(bf16).astype(f32)
    g = dot(c_ref[...], w_ref[:, qkv_width:])
    q = [keep_ref[:, :HS], keep_ref[:, HS : 2 * HS]]
    k = keep_ref[:, 2 * HS : 3 * HS]
    v = keep_ref[:, 3 * HS : 4 * HS]
    heads = [keep_ref[:, 4 * HS : 5 * HS].astype(f32), keep_ref[:, 5 * HS :].astype(f32)]
    chosen = [choose(g, r) for r in routes]
    parts = [jnp.sum(heads[s] * chosen[s], axis=1, keepdims=True) for s in range(2)]
    hg = [(gates[:, s : s + 1] * chosen[s]).astype(bf16) for s in range(2)]
    gated = [gates[:, s : s + 1] * heads[s] for s in range(2)]
    for e, block in enumerate(spread(gated, routes)):
        z_ref[:, e * HS : (e + 1) * HS] = block.astype(bf16)
    segments = rows // SEG
    dk = [jnp.zeros((SEG, HS), f32) for _ in range(segments)]
    dv = [jnp.zeros((SEG, HS), f32) for _ in range(segments)]
    dq = [[], []]
    for a in range(segments):
        here = slice(a * SEG, (a + 1) * SEG)
        upto = (a + 1) * SEG
        qa = jnp.concatenate([q[0][here], q[1][here]], axis=0)
        ha = jnp.concatenate([hg[0][here], hg[1][here]], axis=0)
        p = weights_of(qa, k[:upto], allow_mask(side, a))
        pg = dot_nt(ha, v[:upto])
        sg = (p * (pg - jnp.sum(p * pg, axis=-1, keepdims=True))).astype(bf16)
        dqa = dot(sg, k[:upto]) * (HS**-0.5)
        dq[0].append(dqa[:SEG])
        dq[1].append(dqa[SEG:])
        dka = dot_tn(sg, qa) * (HS**-0.5)
        dva = dot_tn(p.astype(bf16), ha)
        for b in range(a + 1):
            dk[b] = dk[b] + dka[b * SEG : (b + 1) * SEG]
            dv[b] = dv[b] + dva[b * SEG : (b + 1) * SEG]
    cos, sin = [], []
    for a in range(segments):
        depth = side[a * SEG : (a + 1) * SEG, 6:7]
        cos.append(rope_rows(depth, cos_ref))
        sin.append(rope_rows(depth, sin_ref))
    cos = jnp.concatenate(cos, axis=0)
    sin = jnp.concatenate(sin, axis=0)

    def unturn(v):
        return v * cos - pltpu.roll(v, HS // 2, 1) * sin

    dq = [unturn(jnp.concatenate(d, axis=0)) for d in dq]
    blocks = spread(dq, routes) + [unturn(jnp.concatenate(dk, axis=0)), jnp.concatenate(dv, axis=0)]
    grad = jnp.concatenate([b.astype(bf16) for b in blocks], axis=1)
    grad_ref[...] = grad
    part_ref[...] = put({0: parts[0], 1: parts[1]}, rows).astype(bf16)
    core = core_ref[0]
    back = dot_nt(by_core(grad_ref, core), w_ref[:, :qkv_width]).astype(bf16)
    split_rows(back, kept_ref, sent_ref, slice(0, dim))
    split_rows(by_core(part_ref, core), kept_ref, sent_ref, slice(dim, dim + SIDE))


def att_grad_kernel(x_ref, c_ref, grad_ref, z_ref, wait_ref, out_ref):
    width = grad_ref.shape[1]
    out_ref[:, :width] = dot_tn(x_ref[...], grad_ref[...]).astype(bf16)
    out_ref[:, width:] = dot_tn(c_ref[...], z_ref[...]).astype(bf16)


def mid_kernel(rs_ref, packed_ref, gain_ref, router_ref, *refs):
    out_ref, middle_ref, gate_ref = refs[-3:]
    rows, dim = rs_ref.shape
    side = packed_ref[:, dim:].astype(f32)
    middle = packed_ref[:, :dim].astype(f32) + rs_ref[...].astype(f32)
    middle_ref[...] = middle
    low = (middle * norm_scale(middle) * gain_ref[...]).astype(bf16)
    out_ref[:, :dim] = low
    probs = gate_probs(low, router_ref[...], side[:, 7:8], side[:, 8:9])
    gate_ref[...] = probs
    out_ref[:, dim:] = put(
        {0: probs[:, 0:1], 1: probs[:, 1:2], 2: side[:, 7:8], 3: side[:, 8:9]}, rows
    ).astype(bf16)


def norm_back_kernel(
    route_at, outs, where_ref, rsb_ref, rows_ref, base_ref, gain_ref, router_ref, gate_ref, side_ref,
    *refs
):
    out_refs = refs[-outs:]
    count, dim = rows_ref.shape
    grad = rsb_ref[:, :dim].astype(f32)
    gp = rsb_ref[:, dim:].astype(f32)
    side = side_ref[...].astype(f32)
    p0, p1 = gate_ref[:, 0:1], gate_ref[:, 1:2]
    q0, q1 = gp[:, 0:1], gp[:, 1:2]
    inner = p0 * q0 + p1 * q1
    i0, i1 = p0 * (q0 - inner), p1 * (q1 - inner)
    rows = rows_ref[...].astype(f32)
    scale = norm_scale(rows)
    normal = rows * scale
    gain = gain_ref[...]
    low = (normal * gain).astype(bf16).astype(f32)
    route0, route1 = side[:, route_at : route_at + 1], side[:, route_at + 1 : route_at + 2]
    parts = []
    for e in range(EXPERTS):
        logit_grad = jnp.where(route0 == e, i0, 0.0) + jnp.where(route1 == e, i1, 0.0)
        grad = grad + logit_grad * router_ref[e : e + 1, :]
        parts.append(jnp.sum(logit_grad * low, axis=0, keepdims=True))
    parts.append(jnp.sum(grad * normal, axis=0, keepdims=True))
    parts.append(jnp.zeros((8 - len(parts), dim), f32))
    out_refs[0][...] = jnp.concatenate(parts, axis=0)
    weighted = grad * gain
    total = base_ref[...].astype(f32) + scale * (
        weighted - normal * jnp.mean(weighted * normal, axis=-1, keepdims=True)
    )
    for ref in out_refs[1:]:
        ref[...] = total.astype(ref.dtype)


def ffn_coef(side, mine):
    in0, in1 = side[:, 2:3] == mine, side[:, 3:4] == mine
    return in0, in1, jnp.where(in0, side[:, 0:1], 0.0) + jnp.where(in1, side[:, 1:2], 0.0)


def column_chunks(width):
    return [slice(n, min(n + 256, width)) for n in range(0, width, 256)]


def sigmoid(v):
    return 0.5 * jnp.tanh(0.5 * v) + 0.5


def ffn_fwd_kernel(where_ref, x_ref, wg_ref, wu_ref, gate_ref, up_ref, a_ref):
    dim, width = wg_ref.shape
    side = x_ref[:, dim:].astype(f32)
    coef = ffn_coef(side, where_ref[0].astype(f32))[2]
    x = x_ref[:, :dim]
    for at in column_chunks(width):
        gate = dot(x, wg_ref[:, at])
        up = dot(x, wu_ref[:, at])
        gate_ref[:, at] = gate.astype(bf16)
        up_ref[:, at] = up.astype(bf16)
        a_ref[:, at] = (gate * sigmoid(gate) * up * coef).astype(bf16)


def ffn_act_kernel(
    where_ref, side_ref, gate_ref, up_ref, c_ref, wd_ref, wait_ref, gg_ref, ug_ref, part_ref
):
    rows = c_ref.shape[0]
    in0, in1, coef = ffn_coef(side_ref[...].astype(f32), where_ref[0].astype(f32))
    c = c_ref[...]
    part = jnp.zeros((rows, 1), f32)
    for at in column_chunks(wd_ref.shape[1]):
        gate = gate_ref[:, at].astype(f32)
        up = up_ref[:, at].astype(f32)
        act_grad = dot(c, wd_ref[:, at])
        sig = sigmoid(gate)
        silu = gate * sig
        part = part + jnp.sum(silu * up * act_grad, axis=-1, keepdims=True)
        act_grad = act_grad * coef
        gg_ref[:, at] = (act_grad * up * (sig + silu * (1.0 - sig))).astype(bf16)
        ug_ref[:, at] = (act_grad * silu).astype(bf16)
    part_ref[...] = put(
        {0: jnp.where(in0, part, 0.0), 1: jnp.where(in1, part, 0.0)}, rows
    ).astype(bf16)


def ffn_back_kernel(
    core_ref, gg_ref, ug_ref, part_ref, wg_ref, wu_ref, wait_ref, kept_ref, sent_ref
):
    dim = wg_ref.shape[0]
    core = core_ref[0]
    back = dot_nt(by_core(gg_ref, core), wg_ref[...]) + dot_nt(by_core(ug_ref, core), wu_ref[...])
    split_rows(back.astype(bf16), kept_ref, sent_ref, slice(0, dim))
    split_rows(by_core(part_ref, core), kept_ref, sent_ref, slice(dim, dim + SIDE))


def split_kernel(query_ref, kv_ref, out_ref, wait_ref, *piece_refs):
    cut = piece_refs[0].shape[1]
    for n, piece_ref in enumerate(piece_refs):
        for head in range(piece_ref.shape[0]):
            place = 0
            for ref in (query_ref, kv_ref, out_ref):
                for m in range(ref.shape[0]):
                    rows = ref[m, n * cut : (n + 1) * cut, head * HS : (head + 1) * HS]
                    piece_ref[head, :, place : place + HS] = rows.astype(bf16)
                    place += HS


def cast_kernel(*refs):
    kinds = (len(refs) - 1) // 3
    for kind in range(kinds):
        first, second = refs[kinds + 1 + 2 * kind : kinds + 3 + 2 * kind]
        cut = first.shape[1]
        first[...] = refs[kind][:, :cut].astype(bf16)
        second[...] = refs[kind][:, cut:].astype(bf16)


def join_kernel(piece_ref, *outs):
    for head in range(piece_ref.shape[0]):
        place = 0
        for ref in outs:
            for m in range(ref.shape[0]):
                rows = piece_ref[head, :, place : place + HS]
                ref[m, :, head * HS : (head + 1) * HS] = rows.astype(f32)
                place += HS


def after(value, *waited):
    def body(*refs):
        pass

    anywhere = pl.BlockSpec(memory_space=pl.ANY)
    return pl.pallas_call(
        body,
        in_specs=[anywhere] * (1 + len(waited)),
        out_specs=anywhere,
        out_shape=shape(value.shape, value.dtype),
        input_output_aliases={0: 0},
        cost_estimate=cost(1e6, 1e3),
        name="after",
    )(value, *waited)


def params():
    return pltpu.CompilerParams(vmem_limit_bytes=VMEM)


def cost(flops, nbytes):
    return pl.CostEstimate(flops=int(flops), bytes_accessed=int(nbytes), transcendentals=0)


def wall():
    return cost(2e11, 1e6)


def shape(dims, dtype):
    return jax.ShapeDtypeStruct(dims, dtype)


def whole(array):
    zeros = (0,) * array.ndim
    return pl.BlockSpec(array.shape, lambda *unused: zeros)


def router_parts(router):
    high = lax.reduce_precision(router, 8, 7)
    rest = router - high
    middle = lax.reduce_precision(rest, 8, 7)
    low = rest - middle
    parts = jnp.concatenate([high, middle, low], axis=1)
    return jnp.pad(parts, ((0, 0), (0, SIDE - parts.shape[1]))).astype(bf16)


def shift(value, axis, step, size):
    return lax.ppermute(value, axis, [(i, (i + step) % size) for i in range(size)])


def local(
    tokens, norm_gain1, norm_gain2, att_router, query_maps, kv_maps, out_maps, ffn_router,
    ffn_maps, att_route, ffn_route, parents, cotangent,
):
    rows, dim = tokens.shape
    group_len = att_route.shape[0]
    zz, xx, tt = lax.axis_index("zz"), lax.axis_index("xx"), lax.axis_index("tensor")
    zs, xs, ts = lax.axis_size("zz"), lax.axis_size("xx"), lax.axis_size("tensor")
    here = jnp.stack([tt]).astype(jnp.int32)
    total = rows * zs * ts
    wide_cols = dim + SIDE

    def exchange(value):
        return lax.all_to_all(value, "zz", 0, 0, tiled=True)

    def swap(half):
        return shift(half, "xx", 1, 2) if xs == 2 else half

    def assemble(halves, others, *ready):
        chunks = len(halves)
        part, width = halves[0].shape[1:]
        if xs == 2:
            full = jnp.zeros((zs, xs, chunks, part, width), bf16)
            for n in range(chunks):
                if ready and n == chunks - 1:
                    full = after(full, *ready)
                for piece, column in ((halves[n], xx), (others[n], 1 - xx)):
                    full = lax.dynamic_update_slice(
                        full, piece[:, None, None], (0, column, n, 0, 0)
                    )
        else:
            full = jnp.stack([lax.all_gather(h, "xx", axis=1) for h in halves], axis=2)
        return full.reshape(zs * xs * chunks * part, width)

    core, line = tt % 2, tt // 2
    across_core = [(i, i ^ 1) for i in range(ts)]
    across_line = [(i, i ^ 2) for i in range(ts)]

    def gather_line(mine):
        by_zz = lax.all_gather(mine, "zz", axis=0)
        return by_zz, lax.ppermute(by_zz, "tensor", across_line)

    def gather_core(by_zz, other_line):
        pair = jnp.zeros((zs, 2) + by_zz.shape[1:], by_zz.dtype)
        for piece, place in ((by_zz, line), (other_line, 1 - line)):
            pair = lax.dynamic_update_slice(pair, piece[:, None], (0, place, 0, 0))
        other_core = lax.ppermute(pair, "tensor", across_core)
        full = jnp.zeros((zs, 2, 2) + by_zz.shape[1:], by_zz.dtype)
        for piece, place in ((pair, core), (other_core, 1 - core)):
            full = lax.dynamic_update_slice(full, piece[:, :, None], (0, 0, place, 0, 0))
        return full.reshape(-1, by_zz.shape[-1])

    def fold(value, axis, place, pairs):
        sent = lax.dynamic_index_in_dim(value, 1 - place, axis, keepdims=False)
        kept = lax.dynamic_index_in_dim(value, place, axis, keepdims=False)
        came = lax.ppermute(sent, "tensor", pairs)
        return (kept.astype(f32) + came.astype(f32)).astype(bf16)

    core_one = jnp.stack([core]).astype(jnp.int32)
    smem = pl.BlockSpec(memory_space=pltpu.SMEM)
    segment = group_len // 4

    def halves_of(w):
        return [pl.BlockSpec((2, 1, segment, w), lambda i, *s: (0, i, 0, 0))] * 2

    def halves_shape(w):
        return [shape((2, zs, segment, w), bf16)] * 2

    def add(one, two):
        return (one.astype(f32) + two.astype(f32)).astype(bf16)

    def sum_core(kept, sent):
        came = lax.ppermute(sent, "tensor", across_core)
        pick = lambda v, place: lax.dynamic_index_in_dim(v, place, 0, keepdims=False)
        return [add(pick(kept, place), pick(came, place)) for place in (1 - line, line)]

    def sum_line(sent, kept):
        return add(kept, lax.ppermute(sent, "tensor", across_line))

    def return_x(grad, parts=1):
        grad = grad.reshape(zs, xs, -1, grad.shape[1])
        halves = [grad[i * zs // parts : (i + 1) * zs // parts] for i in range(parts)]
        if xs != 2:
            came = [
                lax.psum_scatter(h.transpose(1, 0, 2, 3), "xx", scatter_dimension=0, tiled=False)
                for h in halves
            ]
            return halves, came, jnp.concatenate(came, axis=0)
        sent = [lax.dynamic_index_in_dim(h, 1 - xx, 1, keepdims=False) for h in halves]
        came = [shift(h, "xx", 1, 2) for h in sent]
        kept = lax.dynamic_index_in_dim(grad, xx, 1, keepdims=False)
        return sent, came, (kept.astype(f32) + jnp.concatenate(came, 0).astype(f32)).astype(bf16)

    packed = pl.pallas_call(
        pack_kernel,
        grid_spec=pltpu.PrefetchScalarGridSpec(
            num_scalar_prefetch=2,
            grid=(1,),
            in_specs=[
                pl.BlockSpec((rows, dim), lambda i, w, p: (0, 0)),
                pl.BlockSpec((rows, 2), lambda i, w, p: (w[0], 0)),
                pl.BlockSpec((rows, 2), lambda i, w, p: (w[0], 0)),
            ],
            out_specs=pl.BlockSpec((rows, wide_cols), lambda i, w, p: (0, 0)),
        ),
        out_shape=shape((rows, wide_cols), bf16),
        compiler_params=params(),
        name="pack",
    )(here, parents, tokens, att_route, ffn_route)

    group_tokens = lax.all_gather(packed, GROUP, axis=0, tiled=True)
    small = jnp.concatenate(
        [norm_gain1[None], norm_gain2[None], att_router.T, ffn_router.T], axis=0
    )
    devices = zs * xs * ts
    small = jnp.broadcast_to(small.reshape(1, -1), (devices, small.size))
    small = after(small, packed)
    small = lax.all_to_all(small, ALL, 0, 0, tiled=True)
    small = small.reshape(devices, 2 + 2 * EXPERTS, norm_gain1.shape[0])
    small = small.transpose(1, 0, 2).reshape(2 + 2 * EXPERTS, dim)
    gain1, gain2 = small[0:1], small[1:2]
    router1 = jnp.pad(small[2 : 2 + EXPERTS], ((0, 8 - EXPERTS), (0, 0)))
    router2 = jnp.pad(small[2 + EXPERTS :], ((0, 8 - EXPERTS), (0, 0)))
    parts1 = router_parts(small[2 : 2 + EXPERTS].T)
    parts2 = router_parts(small[2 + EXPERTS :].T)

    count = query_maps.shape[0] + kv_maps.shape[0] + out_maps.shape[0]
    part = query_maps.shape[1]
    zz_one = jnp.stack([zz]).astype(jnp.int32)
    vmem = pl.BlockSpec(memory_space=pltpu.VMEM)
    anywhere = pl.BlockSpec(memory_space=pl.ANY)
    cut, width = part // 2, ffn_maps.shape[2]
    by_head = pl.pallas_call(
        split_kernel,
        in_specs=[vmem, vmem, vmem, anywhere],
        out_specs=[vmem] * 2,
        out_shape=[shape((zs, cut, count * HS), bf16)] * 2,
        compiler_params=params(),
        name="split",
    )(query_maps, kv_maps, out_maps, small)
    att_first = exchange(by_head[0])
    att_half = exchange(after(by_head[1], att_first))
    w_att = assemble([att_first, att_half], [swap(att_first), swap(att_half)])

    cast = pl.pallas_call(
        cast_kernel,
        grid=(EXPERTS,),
        in_specs=[
            pl.BlockSpec((1, part, width), lambda i, kind=kind: (kind * EXPERTS + i, 0, 0))
            for kind in range(3)
        ]
        + [anywhere],
        out_specs=[pl.BlockSpec((1, cut, width), lambda i: (i, 0, 0))] * 6,
        out_shape=[shape((EXPERTS, cut, width), bf16)] * 6,
        compiler_params=params(),
        cost_estimate=cost(1e6, 6 * ffn_maps.size),
        name="cast",
    )(ffn_maps, ffn_maps, ffn_maps, by_head[0])
    chunks = []

    def chunk(n, *ready):
        value = exchange(after(cast[n], *ready))
        chunks.append(value)
        others.append(swap(value))

    others = []
    chunk(0, att_half)
    chunk(1, chunks[0])
    cot_zz, cot_line = gather_line(after(cotangent, chunks[0]))
    for n in range(2, 6):
        chunk(n, chunks[-1])
    w_gate, w_up = [assemble(chunks[n : n + 2], others[n : n + 2]) for n in (0, 2)]

    half = HS // 2
    frequency = rope_base ** (-2.0 * jnp.arange(half, dtype=f32) / HS)
    angles = jnp.arange(group_len, dtype=f32)[:, None] * frequency[None, :]
    cosines, sines = jnp.cos(angles), jnp.sin(angles)
    cos = jnp.concatenate([cosines, cosines], axis=1)
    sin = jnp.concatenate([-sines, sines], axis=1)

    trees = total // group_len
    block = lambda width: pl.BlockSpec((group_len, width), lambda i: (i, 0))
    kept_att, sent_att, x1, kept, gate1 = pl.pallas_call(
        att_fwd_kernel,
        grid=(trees,),
        in_specs=[
            smem, block(wide_cols), whole(w_att), whole(parts1), whole(gain1), whole(cos), whole(sin)
        ],
        out_specs=[*halves_of(dim), block(dim), block(6 * HS), block(SIDE)],
        out_shape=[
            *halves_shape(dim), shape((total, dim), bf16), shape((total, 6 * HS), bf16),
            shape((total, SIDE), f32),
        ],
        scratch_shapes=[pltpu.VMEM((group_len, EXPERTS * HS), bf16)],
        compiler_params=params(),
        cost_estimate=wall(),
        name="att_fwd",
    )(core_one, group_tokens, w_att, parts1, gain1, cos, sin)
    sent_att = after(sent_att, others[0], chunks[1])
    core_att = sum_core(kept_att, sent_att)
    line_att = after(sum_line(*core_att), cot_zz, others[1])
    sum_att = lax.psum_scatter(line_att, "zz", scatter_dimension=0, tiled=False)

    waited = [chunks[3], others[2], cot_line]
    packed2, middle, gate2 = pl.pallas_call(
        mid_kernel,
        in_specs=[vmem] * 4 + [pl.BlockSpec(memory_space=pl.ANY)] * len(waited),
        out_shape=[shape((rows, wide_cols), bf16), shape((rows, dim), f32), shape((rows, SIDE), f32)],
        compiler_params=params(),
        cost_estimate=wall(),
        name="mid",
    )(sum_att, packed, gain2, parts2, *waited)
    x2 = lax.all_gather(packed2, GROUP, axis=0, tiled=True)

    step = group_len
    steps = (total // step,)
    rows_of = lambda w: pl.BlockSpec((step, w), lambda i, *s: (i, 0))
    side_of = pl.BlockSpec((step, SIDE), lambda i, *s: (i, dim // SIDE))
    fixed = pl.BlockSpec(
        (dim, width), lambda i, *s: (0, 0), pipeline_mode=pl.Buffered(buffer_count=1)
    )
    gate_h, up_h, act = pl.pallas_call(
        ffn_fwd_kernel,
        grid_spec=pltpu.PrefetchScalarGridSpec(
            num_scalar_prefetch=1,
            grid=steps,
            in_specs=[rows_of(wide_cols), fixed, fixed],
            out_specs=[rows_of(width)] * 3,
        ),
        out_shape=[shape((total, width), bf16)] * 3,
        compiler_params=params(),
        cost_estimate=wall(),
        name="ffn_fwd",
    )(zz_one, x2, w_gate, w_up)
    group_cot = gather_core(cot_zz, cot_line)
    down_grad = dot_tn(group_cot, act).astype(bf16)
    down_sent, down_came, down_sum = return_x(down_grad, 2)
    w_down = assemble(chunks[4:], others[4:], act)
    gate_grad, up_grad, part2 = pl.pallas_call(
        ffn_act_kernel,
        grid_spec=pltpu.PrefetchScalarGridSpec(
            num_scalar_prefetch=1,
            grid=steps,
            in_specs=[
                side_of, rows_of(width), rows_of(width), rows_of(dim), fixed, anywhere
            ],
            out_specs=[rows_of(width)] * 2 + [rows_of(SIDE)],
        ),
        out_shape=[shape((total, width), bf16)] * 2 + [shape((total, SIDE), bf16)],
        compiler_params=params(),
        cost_estimate=wall(),
        name="ffn_act",
    )(zz_one, x2, gate_h, up_h, group_cot, w_down, down_grad)
    kept2, sent2 = pl.pallas_call(
        ffn_back_kernel,
        grid=steps,
        in_specs=[smem, rows_of(width), rows_of(width), rows_of(SIDE), fixed, fixed, anywhere],
        out_specs=halves_of(wide_cols),
        out_shape=halves_shape(wide_cols),
        compiler_params=params(),
        cost_estimate=wall(),
        name="ffn_back",
    )(core_one, gate_grad, up_grad, part2, w_gate, w_up, down_came[0])
    core2 = sum_core(kept2, after(sent2, down_came[1]))
    line2 = sum_line(*core2)
    sum_back2 = lax.psum_scatter(line2, "zz", scatter_dimension=0, tiled=False)

    x2_low = x2[:, :dim]
    gate_dw = dot_tn(x2_low, after(gate_grad, core2[0])).astype(bf16)
    up_dw = dot_tn(x2_low, after(up_grad, gate_dw)).astype(bf16)
    gate_sent, gate_came, gate_sum = return_x(gate_dw)
    up_sent, up_came, up_sum = return_x(up_dw)
    down_back = exchange(after(down_sum, core2[0]))
    gate_back = exchange(after(gate_sum, down_back))
    up_back = [exchange(after(up_sum[:, :cut], gate_back))]
    up_back.append(exchange(after(up_sum[:, cut:], up_back[0])))
    part_ffn = dot_nt(after(act, up_dw, line2), w_down).astype(bf16)
    core_ffn = fold(part_ffn.reshape(zs, 2, 2, rows, dim), 2, core, across_core)
    by_line = fold(after(core_ffn, gate_sum), 1, line, across_line)

    def norm_back(route_at, rsb, wide_rows, base, gain, router, gate, gate_at, outs, name, *waited):
        def pick(a):
            return pl.BlockSpec(a.shape, lambda i, w: (0,) * a.ndim)

        return pl.pallas_call(
            functools.partial(norm_back_kernel, route_at, 1 + len(outs)),
            grid_spec=pltpu.PrefetchScalarGridSpec(
                num_scalar_prefetch=1,
                grid=(1,),
                in_specs=[
                    pick(rsb), pl.BlockSpec((rows, dim), lambda i, w: (0, 0)), pick(base), pick(gain), pick(router),
                    pl.BlockSpec((rows, SIDE), lambda i, w: (w[0], 0)),
                    pl.BlockSpec((rows, SIDE), lambda i, w: (0, dim // SIDE)),
                ]
                + [anywhere] * len(waited),
                out_specs=[pl.BlockSpec((8, dim), lambda i, w: (0, 0))]
                + [pl.BlockSpec((rows, dim), lambda i, w: (0, 0)) for _ in outs],
            ),
            out_shape=[shape((8, dim), f32)] + [shape((rows, dim), d) for d in outs],
            compiler_params=params(),
            cost_estimate=wall(),
            name=name,
        )(gate_at, rsb, wide_rows, base, gain, router, gate, packed, *waited)

    zero = jnp.zeros((1,), jnp.int32)
    parts_ffn, middle_grad, att_cot = norm_back(
        7, sum_back2, middle, cotangent, gain2, router2, gate2, zero, [f32, bf16], "mid_back",
        down_back, gate_sum, part_ffn,
    )
    group_att_cot = lax.all_gather(att_cot, GROUP, axis=0, tiled=True)

    group_att_cot = after(group_att_cot, gate_back, up_sum, by_line)
    mixed_rows = lax.psum_scatter(
        after(by_line, group_att_cot), "zz", scatter_dimension=0, tiled=False
    )
    kept1, sent1, grad_qkv, z = pl.pallas_call(
        att_bwd_kernel,
        grid=(trees,),
        in_specs=[
            smem, block(dim), whole(w_att), block(6 * HS), block(SIDE),
            pl.BlockSpec((group_len, SIDE), lambda i: (i, dim // SIDE)), whole(cos), whole(sin),
        ],
        out_specs=[*halves_of(wide_cols), block(6 * HS), block(EXPERTS * HS)],
        out_shape=[
            *halves_shape(wide_cols), shape((total, 6 * HS), bf16),
            shape((total, EXPERTS * HS), bf16),
        ],
        scratch_shapes=[pltpu.VMEM((group_len, SIDE), bf16)],
        compiler_params=params(),
        cost_estimate=wall(),
        name="att_bwd",
    )(core_one, group_att_cot, w_att, kept, gate1, group_tokens, cos, sin)
    core1 = sum_core(kept1, after(sent1, up_back[0]))
    grad_att = pl.pallas_call(
        att_grad_kernel,
        grid=(zs,),
        in_specs=[
            pl.BlockSpec((total, dim // zs), lambda i: (0, i)),
            pl.BlockSpec((total, dim // zs), lambda i: (0, i)),
            whole(grad_qkv), whole(z), anywhere,
        ],
        out_specs=pl.BlockSpec((dim // zs, count * HS), lambda i: (i, 0)),
        out_shape=shape((dim, count * HS), bf16),
        compiler_params=params(),
        cost_estimate=cost(2 * total * dim * count * HS, 6 * total * dim),
        name="att_grad",
    )(x1, group_att_cot, grad_qkv, z, core1[0])
    att_sent, att_came, att_sum = return_x(grad_att, 2)
    line1 = sum_line(core1[0], after(core1[1], *att_sent, att_came[0], mixed_rows, up_back[1]))
    sum_back1 = lax.psum_scatter(line1, "zz", scatter_dimension=0, tiled=False)
    att_back = exchange(after(att_sum, up_back[1]))
    query_grad, kv_grad, out_grad = pl.pallas_call(
        join_kernel,
        in_specs=[vmem],
        out_specs=[vmem] * 3,
        out_shape=[shape(a.shape, f32) for a in (query_maps, kv_maps, out_maps)],
        compiler_params=params(),
        name="join",
    )(att_back)
    ffn_out = jnp.concatenate([v.astype(f32) for v in (gate_back, jnp.concatenate(up_back, axis=1), down_back)], axis=0)

    mixed = (middle + mixed_rows.astype(f32)).astype(bf16)

    parts_att, input_grad = norm_back(
        0, sum_back1, tokens, middle_grad, gain1, router1, gate1,
        (zz * ts + tt)[None].astype(jnp.int32), [bf16], "input_back",
    )

    used = EXPERTS + 1
    parts = jnp.concatenate([parts_ffn[:used], parts_att[:used]], axis=0)
    parts = parts.reshape(2 * used, devices, -1).transpose(1, 0, 2).reshape(devices, -1)
    parts = jnp.sum(lax.all_to_all(parts, ALL, 0, 0, tiled=True), axis=0).reshape(2, used, -1)
    ffn_router_grad, gain2_grad = parts[0, :EXPERTS].T, parts[0, EXPERTS]
    att_router_grad, gain1_grad = parts[1, :EXPERTS].T, parts[1, EXPERTS]
    return (
        mixed,
        input_grad,
        gain1_grad,
        gain2_grad,
        att_router_grad,
        query_grad,
        kv_grad,
        out_grad,
        ffn_router_grad,
        ffn_out,
    )


def solution(mesh):
    dp, tensor = mesh.shape["dp"], mesh.shape["tensor"]
    fine = Mesh(mesh.devices.reshape(EXPERTS, dp // EXPERTS, tensor), ALL)
    dps = ("zz", "xx")
    rows, flat, maps = P(ALL, None), P(ALL), P(None, dps, "tensor")
    placed = (
        rows, flat, flat, rows, maps, maps, maps, rows, maps, P(dps, None), P(dps, None), P(dps), rows
    )
    return jax.shard_map(
        local,
        mesh=fine,
        in_specs=placed,
        out_specs=(rows, rows, flat, flat, rows, maps, maps, maps, rows, maps),
        check_vma=False,
    )
```

```python
import functools

import jax
import jax.numpy as jnp
from jax import lax
from jax.experimental import pallas as pl
from jax.experimental.pallas import tpu as pltpu
from jax.sharding import Mesh, PartitionSpec as P

EXPERTS = 4
HS = 128
SEG = 128
SIDE = 128
epsilon = 1e-05
rope_base = 10000.0
f32 = jnp.float32
bf16 = jnp.bfloat16
ALL = ("zz", "xx", "tensor")
GROUP = ("zz", "tensor")
VMEM = 60 * 1024 * 1024


def dot(a, b):
    return lax.dot_general(a, b, (((1,), (0,)), ((), ())), preferred_element_type=f32)


def dot_nt(a, b):
    return lax.dot_general(a, b, (((1,), (1,)), ((), ())), preferred_element_type=f32)


def dot_tn(a, b):
    return lax.dot_general(a, b, (((0,), (0,)), ((), ())), preferred_element_type=f32)


def lanes(rows):
    return lax.broadcasted_iota(jnp.int32, (rows, SIDE), 1).astype(f32)


def put(columns, rows):
    lane = lanes(rows)
    out = jnp.zeros((rows, SIDE), f32)
    for place, column in columns.items():
        out = jnp.where(lane == place, column, out)
    return out


def norm_scale(rows):
    return lax.rsqrt(jnp.mean(rows * rows, axis=-1, keepdims=True) + epsilon)


def gate_probs(low, router_parts, route0, route1):
    rows = low.shape[0]
    parts = dot(low, router_parts)
    lane = lanes(rows)
    logits = (
        parts
        + pltpu.roll(parts, SIDE - EXPERTS, 1)
        + pltpu.roll(parts, SIDE - 2 * EXPERTS, 1)
    )
    c0 = jnp.sum(jnp.where(lane == route0, logits, 0.0), axis=1, keepdims=True)
    c1 = jnp.sum(jnp.where(lane == route1, logits, 0.0), axis=1, keepdims=True)
    top = jnp.maximum(c0, c1)
    e0 = jnp.exp(c0 - top)
    e1 = jnp.exp(c1 - top)
    total = e0 + e1
    return put({0: e0 / total, 1: e1 / total}, rows)


def choose(wide, route):
    out = wide[:, :HS]
    for e in range(1, EXPERTS):
        out = jnp.where(route == e, wide[:, e * HS : (e + 1) * HS], out)
    return out


def spread(slots, routes):
    blocks = []
    for e in range(EXPERTS):
        block = jnp.where(routes[0] == e, slots[0], 0.0)
        blocks.append(block + jnp.where(routes[1] == e, slots[1], 0.0))
    return blocks


def rope_rows(depth, table_ref):
    segments = table_ref.shape[0] // SEG
    out = table_ref[0:SEG, :]
    for d in range(1, segments):
        out = jnp.where(depth == d, table_ref[d * SEG : (d + 1) * SEG, :], out)
    return out


def allow_mask(side, seg):
    rows = side[seg * SEG : (seg + 1) * SEG]
    blocks = [jnp.broadcast_to(rows[:, 2 + b : 3 + b], (SEG, SEG)) for b in range(seg)]
    later = lax.broadcasted_iota(jnp.int32, (SEG, SEG), 1)
    here = lax.broadcasted_iota(jnp.int32, (SEG, SEG), 0)
    blocks.append((later <= here).astype(f32))
    mask = jnp.concatenate(blocks, axis=1) if seg else blocks[0]
    return jnp.concatenate([mask, mask], axis=0)


def weights_of(queries, keys, mask):
    scores = dot_nt(queries, keys) * (HS**-0.5)
    scores = jnp.where(mask > 0.5, scores, -1e30)
    top = jnp.max(scores, axis=-1, keepdims=True)
    exponent = jnp.exp(scores - top)
    return exponent / jnp.sum(exponent, axis=-1, keepdims=True)


def by_core(ref, core):
    half = ref.shape[0] // 4
    parts = []
    for other in range(2):
        for line in range(2):
            first = (2 * line + lax.rem(core + other, 2)) * half
            parts.append(ref[pl.ds(pl.multiple_of(first, half), half), :])
    return jnp.concatenate(parts, axis=0)


def split_rows(value, kept_ref, sent_ref, columns):
    half = value.shape[0] // 4
    for i, ref in enumerate((kept_ref, kept_ref, sent_ref, sent_ref)):
        ref[i % 2, 0, :, columns] = value[i * half : (i + 1) * half]


def pack_kernel(where_ref, parents_ref, tok_ref, att_ref, ffn_ref, out_ref):
    rows = tok_ref.shape[0]
    dim = tok_ref.shape[1]
    out_ref[:, :dim] = tok_ref[...]
    segments = parents_ref.shape[0]
    current = where_ref[0]
    reached = [current == b for b in range(segments)]
    for step in range(segments - 1):
        parent = parents_ref[jnp.maximum(current, 0)]
        current = jnp.where(current > 0, parent, 0)
        reached = [r | (current == b) for b, r in enumerate(reached)]
    flags = [jnp.where(r, 1.0, 0.0) for r in reached]
    depth = functools.reduce(lambda a, b: a + b, flags) - 1.0
    att = att_ref[...].astype(f32)
    ffn = ffn_ref[...].astype(f32)
    columns = {0: att[:, 0:1], 1: att[:, 1:2], 6: depth, 7: ffn[:, 0:1], 8: ffn[:, 1:2]}
    for b in range(segments):
        columns[2 + b] = flags[b]
    out_ref[:, dim:] = put(columns, rows).astype(bf16)


def att_fwd_kernel(
    core_ref, tok_ref, w_ref, router_ref, gain_ref, cos_ref, sin_ref, kept_ref, sent_ref, x_ref,
    keep_ref, gate_ref, z_ref
):
    dim = x_ref.shape[1]
    rows = x_ref.shape[0]
    side = tok_ref[:, dim:].astype(f32)
    wide = tok_ref[:, :dim].astype(f32)
    x = (wide * norm_scale(wide) * gain_ref[...]).astype(bf16)
    x_ref[...] = x
    qkv_width = (EXPERTS + 2) * HS
    qkv = dot(x, w_ref[:, :qkv_width])
    routes = (side[:, 0:1], side[:, 1:2])
    probs = gate_probs(x, router_ref[...], routes[0], routes[1])
    gate_ref[...] = probs
    gates = probs.astype(bf16).astype(f32)
    segments = rows // SEG
    cos, sin = [], []
    for a in range(segments):
        depth = side[a * SEG : (a + 1) * SEG, 6:7]
        cos.append(rope_rows(depth, cos_ref))
        sin.append(rope_rows(depth, sin_ref))
    cos = jnp.concatenate(cos, axis=0)
    sin = jnp.concatenate(sin, axis=0)

    def turn(v):
        return (v * cos + pltpu.roll(v, HS // 2, 1) * sin).astype(bf16)

    q = [turn(choose(qkv, r)) for r in routes]
    k = turn(qkv[:, EXPERTS * HS : (EXPERTS + 1) * HS])
    v = qkv[:, (EXPERTS + 1) * HS :].astype(bf16)
    heads = [[], []]
    for a in range(segments):
        here = slice(a * SEG, (a + 1) * SEG)
        upto = (a + 1) * SEG
        qa = jnp.concatenate([q[0][here], q[1][here]], axis=0)
        p = weights_of(qa, k[:upto], allow_mask(side, a))
        o = dot(p.astype(bf16), v[:upto]).astype(bf16)
        heads[0].append(o[:SEG])
        heads[1].append(o[SEG:])
    heads = [jnp.concatenate(h, axis=0) for h in heads]
    for i, piece in enumerate([q[0], q[1], k, v, heads[0], heads[1]]):
        keep_ref[:, i * HS : (i + 1) * HS] = piece
    gated = [gates[:, s : s + 1] * heads[s].astype(f32) for s in range(2)]
    z_ref[...] = jnp.concatenate([b.astype(bf16) for b in spread(gated, routes)], axis=1)
    part = dot_nt(by_core(z_ref, core_ref[0]), w_ref[:, qkv_width:]).astype(bf16)
    split_rows(part, kept_ref, sent_ref, slice(None))


def att_bwd_kernel(
    core_ref, c_ref, w_ref, keep_ref, gate_ref, side_ref, cos_ref, sin_ref, kept_ref, sent_ref,
    grad_ref, z_ref, part_ref
):
    dim = c_ref.shape[1]
    rows = c_ref.shape[0]
    qkv_width = (EXPERTS + 2) * HS
    side = side_ref[...].astype(f32)
    routes = (side[:, 0:1], side[:, 1:2])
    gates = gate_ref[...].astype(bf16).astype(f32)
    g = dot(c_ref[...], w_ref[:, qkv_width:])
    q = [keep_ref[:, :HS], keep_ref[:, HS : 2 * HS]]
    k = keep_ref[:, 2 * HS : 3 * HS]
    v = keep_ref[:, 3 * HS : 4 * HS]
    heads = [keep_ref[:, 4 * HS : 5 * HS].astype(f32), keep_ref[:, 5 * HS :].astype(f32)]
    chosen = [choose(g, r) for r in routes]
    parts = [jnp.sum(heads[s] * chosen[s], axis=1, keepdims=True) for s in range(2)]
    hg = [(gates[:, s : s + 1] * chosen[s]).astype(bf16) for s in range(2)]
    gated = [gates[:, s : s + 1] * heads[s] for s in range(2)]
    for e, block in enumerate(spread(gated, routes)):
        z_ref[:, e * HS : (e + 1) * HS] = block.astype(bf16)
    segments = rows // SEG
    dk = [jnp.zeros((SEG, HS), f32) for _ in range(segments)]
    dv = [jnp.zeros((SEG, HS), f32) for _ in range(segments)]
    dq = [[], []]
    for a in range(segments):
        here = slice(a * SEG, (a + 1) * SEG)
        upto = (a + 1) * SEG
        qa = jnp.concatenate([q[0][here], q[1][here]], axis=0)
        ha = jnp.concatenate([hg[0][here], hg[1][here]], axis=0)
        p = weights_of(qa, k[:upto], allow_mask(side, a))
        pg = dot_nt(ha, v[:upto])
        sg = (p * (pg - jnp.sum(p * pg, axis=-1, keepdims=True))).astype(bf16)
        dqa = dot(sg, k[:upto]) * (HS**-0.5)
        dq[0].append(dqa[:SEG])
        dq[1].append(dqa[SEG:])
        dka = dot_tn(sg, qa) * (HS**-0.5)
        dva = dot_tn(p.astype(bf16), ha)
        for b in range(a + 1):
            dk[b] = dk[b] + dka[b * SEG : (b + 1) * SEG]
            dv[b] = dv[b] + dva[b * SEG : (b + 1) * SEG]
    cos, sin = [], []
    for a in range(segments):
        depth = side[a * SEG : (a + 1) * SEG, 6:7]
        cos.append(rope_rows(depth, cos_ref))
        sin.append(rope_rows(depth, sin_ref))
    cos = jnp.concatenate(cos, axis=0)
    sin = jnp.concatenate(sin, axis=0)

    def unturn(v):
        return v * cos - pltpu.roll(v, HS // 2, 1) * sin

    dq = [unturn(jnp.concatenate(d, axis=0)) for d in dq]
    blocks = spread(dq, routes) + [unturn(jnp.concatenate(dk, axis=0)), jnp.concatenate(dv, axis=0)]
    grad = jnp.concatenate([b.astype(bf16) for b in blocks], axis=1)
    grad_ref[...] = grad
    part_ref[...] = put({0: parts[0], 1: parts[1]}, rows).astype(bf16)
    core = core_ref[0]
    back = dot_nt(by_core(grad_ref, core), w_ref[:, :qkv_width]).astype(bf16)
    split_rows(back, kept_ref, sent_ref, slice(0, dim))
    split_rows(by_core(part_ref, core), kept_ref, sent_ref, slice(dim, dim + SIDE))


def att_grad_kernel(x_ref, c_ref, grad_ref, z_ref, wait_ref, out_ref):
    width = grad_ref.shape[1]
    out_ref[:, :width] = dot_tn(x_ref[...], grad_ref[...]).astype(bf16)
    out_ref[:, width:] = dot_tn(c_ref[...], z_ref[...]).astype(bf16)


def mid_kernel(rs_ref, packed_ref, gain_ref, router_ref, *refs):
    out_ref, middle_ref, gate_ref = refs[-3:]
    rows, dim = rs_ref.shape
    side = packed_ref[:, dim:].astype(f32)
    middle = packed_ref[:, :dim].astype(f32) + rs_ref[...].astype(f32)
    middle_ref[...] = middle
    low = (middle * norm_scale(middle) * gain_ref[...]).astype(bf16)
    out_ref[:, :dim] = low
    probs = gate_probs(low, router_ref[...], side[:, 7:8], side[:, 8:9])
    gate_ref[...] = probs
    out_ref[:, dim:] = put(
        {0: probs[:, 0:1], 1: probs[:, 1:2], 2: side[:, 7:8], 3: side[:, 8:9]}, rows
    ).astype(bf16)


def norm_back_kernel(
    route_at, outs, where_ref, rsb_ref, rows_ref, base_ref, gain_ref, router_ref, gate_ref, side_ref,
    *refs
):
    out_refs = refs[-outs:]
    count, dim = rows_ref.shape
    grad = rsb_ref[:, :dim].astype(f32)
    gp = rsb_ref[:, dim:].astype(f32)
    side = side_ref[...].astype(f32)
    p0, p1 = gate_ref[:, 0:1], gate_ref[:, 1:2]
    q0, q1 = gp[:, 0:1], gp[:, 1:2]
    inner = p0 * q0 + p1 * q1
    i0, i1 = p0 * (q0 - inner), p1 * (q1 - inner)
    rows = rows_ref[...].astype(f32)
    scale = norm_scale(rows)
    normal = rows * scale
    gain = gain_ref[...]
    low = (normal * gain).astype(bf16).astype(f32)
    route0, route1 = side[:, route_at : route_at + 1], side[:, route_at + 1 : route_at + 2]
    parts = []
    for e in range(EXPERTS):
        logit_grad = jnp.where(route0 == e, i0, 0.0) + jnp.where(route1 == e, i1, 0.0)
        grad = grad + logit_grad * router_ref[e : e + 1, :]
        parts.append(jnp.sum(logit_grad * low, axis=0, keepdims=True))
    parts.append(jnp.sum(grad * normal, axis=0, keepdims=True))
    parts.append(jnp.zeros((8 - len(parts), dim), f32))
    out_refs[0][...] = jnp.concatenate(parts, axis=0)
    weighted = grad * gain
    total = base_ref[...].astype(f32) + scale * (
        weighted - normal * jnp.mean(weighted * normal, axis=-1, keepdims=True)
    )
    for ref in out_refs[1:]:
        ref[...] = total.astype(ref.dtype)


def ffn_coef(side, mine):
    in0, in1 = side[:, 2:3] == mine, side[:, 3:4] == mine
    return in0, in1, jnp.where(in0, side[:, 0:1], 0.0) + jnp.where(in1, side[:, 1:2], 0.0)


def column_chunks(width):
    return [slice(n, min(n + 256, width)) for n in range(0, width, 256)]


def sigmoid(v):
    return 0.5 * jnp.tanh(0.5 * v) + 0.5


def ffn_fwd_kernel(where_ref, x_ref, wg_ref, wu_ref, gate_ref, up_ref, a_ref):
    dim, width = wg_ref.shape
    side = x_ref[:, dim:].astype(f32)
    coef = ffn_coef(side, where_ref[0].astype(f32))[2]
    x = x_ref[:, :dim]
    for at in column_chunks(width):
        gate = dot(x, wg_ref[:, at])
        up = dot(x, wu_ref[:, at])
        gate_ref[:, at] = gate.astype(bf16)
        up_ref[:, at] = up.astype(bf16)
        a_ref[:, at] = (gate * sigmoid(gate) * up * coef).astype(bf16)


def ffn_act_kernel(
    where_ref, side_ref, gate_ref, up_ref, c_ref, wd_ref, wait_ref, gg_ref, ug_ref, part_ref
):
    rows = c_ref.shape[0]
    in0, in1, coef = ffn_coef(side_ref[...].astype(f32), where_ref[0].astype(f32))
    c = c_ref[...]
    part = jnp.zeros((rows, 1), f32)
    for at in column_chunks(wd_ref.shape[1]):
        gate = gate_ref[:, at].astype(f32)
        up = up_ref[:, at].astype(f32)
        act_grad = dot(c, wd_ref[:, at])
        sig = sigmoid(gate)
        silu = gate * sig
        part = part + jnp.sum(silu * up * act_grad, axis=-1, keepdims=True)
        act_grad = act_grad * coef
        gg_ref[:, at] = (act_grad * up * (sig + silu * (1.0 - sig))).astype(bf16)
        ug_ref[:, at] = (act_grad * silu).astype(bf16)
    part_ref[...] = put(
        {0: jnp.where(in0, part, 0.0), 1: jnp.where(in1, part, 0.0)}, rows
    ).astype(bf16)


def ffn_back_kernel(
    core_ref, gg_ref, ug_ref, part_ref, wg_ref, wu_ref, wait_ref, kept_ref, sent_ref
):
    dim = wg_ref.shape[0]
    core = core_ref[0]
    back = dot_nt(by_core(gg_ref, core), wg_ref[...]) + dot_nt(by_core(ug_ref, core), wu_ref[...])
    split_rows(back.astype(bf16), kept_ref, sent_ref, slice(0, dim))
    split_rows(by_core(part_ref, core), kept_ref, sent_ref, slice(dim, dim + SIDE))


def split_kernel(query_ref, kv_ref, out_ref, wait_ref, *piece_refs):
    cut = piece_refs[0].shape[1]
    for n, piece_ref in enumerate(piece_refs):
        for head in range(piece_ref.shape[0]):
            place = 0
            for ref in (query_ref, kv_ref, out_ref):
                for m in range(ref.shape[0]):
                    rows = ref[m, n * cut : (n + 1) * cut, head * HS : (head + 1) * HS]
                    piece_ref[head, :, place : place + HS] = rows.astype(bf16)
                    place += HS


def cast_kernel(*refs):
    kinds = (len(refs) - 1) // 3
    for kind in range(kinds):
        first, second = refs[kinds + 1 + 2 * kind : kinds + 3 + 2 * kind]
        cut = first.shape[1]
        first[...] = refs[kind][:, :cut].astype(bf16)
        second[...] = refs[kind][:, cut:].astype(bf16)


def join_kernel(piece_ref, wait_ref, *outs):
    for head in range(piece_ref.shape[0]):
        place = 0
        for ref in outs:
            for m in range(ref.shape[0]):
                rows = piece_ref[head, :, place : place + HS]
                ref[m, :, head * HS : (head + 1) * HS] = rows.astype(f32)
                place += HS


def after(value, *waited):
    def body(*refs):
        pass

    anywhere = pl.BlockSpec(memory_space=pl.ANY)
    return pl.pallas_call(
        body,
        in_specs=[anywhere] * (1 + len(waited)),
        out_specs=anywhere,
        out_shape=shape(value.shape, value.dtype),
        input_output_aliases={0: 0},
        cost_estimate=cost(1e6, 1e3),
        name="after",
    )(value, *waited)


def params():
    return pltpu.CompilerParams(vmem_limit_bytes=VMEM)


def cost(flops, nbytes):
    return pl.CostEstimate(flops=int(flops), bytes_accessed=int(nbytes), transcendentals=0)


def wall():
    return cost(2e11, 1e6)


def shape(dims, dtype):
    return jax.ShapeDtypeStruct(dims, dtype)


def whole(array):
    zeros = (0,) * array.ndim
    return pl.BlockSpec(array.shape, lambda *unused: zeros)


def router_parts(router):
    high = lax.reduce_precision(router, 8, 7)
    rest = router - high
    middle = lax.reduce_precision(rest, 8, 7)
    low = rest - middle
    parts = jnp.concatenate([high, middle, low], axis=1)
    return jnp.pad(parts, ((0, 0), (0, SIDE - parts.shape[1]))).astype(bf16)


def shift(value, axis, step, size):
    return lax.ppermute(value, axis, [(i, (i + step) % size) for i in range(size)])


def local(
    tokens, norm_gain1, norm_gain2, att_router, query_maps, kv_maps, out_maps, ffn_router,
    ffn_maps, att_route, ffn_route, parents, cotangent,
):
    rows, dim = tokens.shape
    group_len = att_route.shape[0]
    zz, xx, tt = lax.axis_index("zz"), lax.axis_index("xx"), lax.axis_index("tensor")
    zs, xs, ts = lax.axis_size("zz"), lax.axis_size("xx"), lax.axis_size("tensor")
    here = jnp.stack([tt]).astype(jnp.int32)
    total = rows * zs * ts
    wide_cols = dim + SIDE

    def exchange(value):
        return lax.all_to_all(value, "zz", 0, 0, tiled=True)

    def swap(half):
        return shift(half, "xx", 1, 2) if xs == 2 else half

    def assemble(halves, others, *ready):
        chunks = len(halves)
        part, width = halves[0].shape[1:]
        if xs == 2:
            full = jnp.zeros((zs, xs, chunks, part, width), bf16)
            for n in range(chunks):
                if ready and n == chunks - 1:
                    full = after(full, *ready)
                for piece, column in ((halves[n], xx), (others[n], 1 - xx)):
                    full = lax.dynamic_update_slice(
                        full, piece[:, None, None], (0, column, n, 0, 0)
                    )
        else:
            full = jnp.stack([lax.all_gather(h, "xx", axis=1) for h in halves], axis=2)
        return full.reshape(zs * xs * chunks * part, width)

    core, line = tt % 2, tt // 2
    across_core = [(i, i ^ 1) for i in range(ts)]
    across_line = [(i, i ^ 2) for i in range(ts)]

    def gather_line(mine):
        by_zz = lax.all_gather(mine, "zz", axis=0)
        return by_zz, lax.ppermute(by_zz, "tensor", across_line)

    def gather_core(by_zz, other_line):
        pair = jnp.zeros((zs, 2) + by_zz.shape[1:], by_zz.dtype)
        for piece, place in ((by_zz, line), (other_line, 1 - line)):
            pair = lax.dynamic_update_slice(pair, piece[:, None], (0, place, 0, 0))
        other_core = lax.ppermute(pair, "tensor", across_core)
        full = jnp.zeros((zs, 2, 2) + by_zz.shape[1:], by_zz.dtype)
        for piece, place in ((pair, core), (other_core, 1 - core)):
            full = lax.dynamic_update_slice(full, piece[:, :, None], (0, 0, place, 0, 0))
        return full.reshape(-1, by_zz.shape[-1])

    def fold(value, axis, place, pairs, sent=None):
        if sent is None:
            sent = lax.dynamic_index_in_dim(value, 1 - place, axis, keepdims=False)
        kept = lax.dynamic_index_in_dim(value, place, axis, keepdims=False)
        came = lax.ppermute(sent, "tensor", pairs)
        return (kept.astype(f32) + came.astype(f32)).astype(bf16)

    core_one = jnp.stack([core]).astype(jnp.int32)
    smem = pl.BlockSpec(memory_space=pltpu.SMEM)
    segment = group_len // 4

    def halves_of(w):
        return [pl.BlockSpec((2, 1, segment, w), lambda i, *s: (0, i, 0, 0))] * 2

    def halves_shape(w):
        return [shape((2, zs, segment, w), bf16)] * 2

    def add(one, two):
        return (one.astype(f32) + two.astype(f32)).astype(bf16)

    def sum_core(kept, sent):
        came = lax.ppermute(sent, "tensor", across_core)
        pick = lambda v, place: lax.dynamic_index_in_dim(v, place, 0, keepdims=False)
        return [add(pick(kept, place), pick(came, place)) for place in (1 - line, line)]

    def sum_line(sent, kept):
        return add(kept, lax.ppermute(sent, "tensor", across_line))

    def return_x(grad, parts=1):
        grad = grad.reshape(zs, xs, -1, grad.shape[1])
        halves = [grad[i * zs // parts : (i + 1) * zs // parts] for i in range(parts)]
        if xs != 2:
            came = [
                lax.psum_scatter(h.transpose(1, 0, 2, 3), "xx", scatter_dimension=0, tiled=False)
                for h in halves
            ]
            return halves, came, jnp.concatenate(came, axis=0)
        sent = [lax.dynamic_index_in_dim(h, 1 - xx, 1, keepdims=False) for h in halves]
        came = [shift(h, "xx", 1, 2) for h in sent]
        kept = lax.dynamic_index_in_dim(grad, xx, 1, keepdims=False)
        return sent, came, (kept.astype(f32) + jnp.concatenate(came, 0).astype(f32)).astype(bf16)

    packed = pl.pallas_call(
        pack_kernel,
        grid_spec=pltpu.PrefetchScalarGridSpec(
            num_scalar_prefetch=2,
            grid=(1,),
            in_specs=[
                pl.BlockSpec((rows, dim), lambda i, w, p: (0, 0)),
                pl.BlockSpec((rows, 2), lambda i, w, p: (w[0], 0)),
                pl.BlockSpec((rows, 2), lambda i, w, p: (w[0], 0)),
            ],
            out_specs=pl.BlockSpec((rows, wide_cols), lambda i, w, p: (0, 0)),
        ),
        out_shape=shape((rows, wide_cols), bf16),
        compiler_params=params(),
        name="pack",
    )(here, parents, tokens, att_route, ffn_route)

    group_tokens = lax.all_gather(packed, GROUP, axis=0, tiled=True)
    small = jnp.concatenate(
        [norm_gain1[None], norm_gain2[None], att_router.T, ffn_router.T], axis=0
    )
    devices = zs * xs * ts
    small = jnp.broadcast_to(small.reshape(1, -1), (devices, small.size))
    small = after(small, packed)
    small = lax.all_to_all(small, ALL, 0, 0, tiled=True)
    small = small.reshape(devices, 2 + 2 * EXPERTS, norm_gain1.shape[0])
    small = small.transpose(1, 0, 2).reshape(2 + 2 * EXPERTS, dim)
    gain1, gain2 = small[0:1], small[1:2]
    router1 = jnp.pad(small[2 : 2 + EXPERTS], ((0, 8 - EXPERTS), (0, 0)))
    router2 = jnp.pad(small[2 + EXPERTS :], ((0, 8 - EXPERTS), (0, 0)))
    parts1 = router_parts(small[2 : 2 + EXPERTS].T)
    parts2 = router_parts(small[2 + EXPERTS :].T)

    count = query_maps.shape[0] + kv_maps.shape[0] + out_maps.shape[0]
    part = query_maps.shape[1]
    zz_one = jnp.stack([zz]).astype(jnp.int32)
    vmem = pl.BlockSpec(memory_space=pltpu.VMEM)
    anywhere = pl.BlockSpec(memory_space=pl.ANY)
    cut, width = part // 2, ffn_maps.shape[2]
    by_head = pl.pallas_call(
        split_kernel,
        in_specs=[vmem, vmem, vmem, anywhere],
        out_specs=[vmem] * 2,
        out_shape=[shape((zs, cut, count * HS), bf16)] * 2,
        compiler_params=params(),
        name="split",
    )(query_maps, kv_maps, out_maps, small)
    att_first = exchange(by_head[0])
    att_half = exchange(after(by_head[1], att_first))
    w_att = assemble([att_first, att_half], [swap(att_first), swap(att_half)])

    cast = pl.pallas_call(
        cast_kernel,
        grid=(EXPERTS,),
        in_specs=[
            pl.BlockSpec((1, part, width), lambda i, kind=kind: (kind * EXPERTS + i, 0, 0))
            for kind in range(3)
        ]
        + [anywhere],
        out_specs=[pl.BlockSpec((1, cut, width), lambda i: (i, 0, 0))] * 6,
        out_shape=[shape((EXPERTS, cut, width), bf16)] * 6,
        compiler_params=params(),
        cost_estimate=cost(1e6, 6 * ffn_maps.size),
        name="cast",
    )(ffn_maps, ffn_maps, ffn_maps, by_head[0])
    chunks = []

    def chunk(n, *ready):
        value = exchange(after(cast[n], *ready))
        chunks.append(value)
        others.append(swap(value))

    others = []
    chunk(0, att_half)
    chunk(1, chunks[0])
    cot_zz, cot_line = gather_line(after(cotangent, chunks[0]))
    for n in range(2, 6):
        chunk(n, chunks[-1])
    w_gate, w_up = [assemble(chunks[n : n + 2], others[n : n + 2]) for n in (0, 2)]

    half = HS // 2
    frequency = rope_base ** (-2.0 * jnp.arange(half, dtype=f32) / HS)
    angles = jnp.arange(group_len, dtype=f32)[:, None] * frequency[None, :]
    cosines, sines = jnp.cos(angles), jnp.sin(angles)
    cos = jnp.concatenate([cosines, cosines], axis=1)
    sin = jnp.concatenate([-sines, sines], axis=1)

    trees = total // group_len
    block = lambda width: pl.BlockSpec((group_len, width), lambda i: (i, 0))
    kept_att, sent_att, x1, kept, gate1 = pl.pallas_call(
        att_fwd_kernel,
        grid=(trees,),
        in_specs=[
            smem, block(wide_cols), whole(w_att), whole(parts1), whole(gain1), whole(cos), whole(sin)
        ],
        out_specs=[*halves_of(dim), block(dim), block(6 * HS), block(SIDE)],
        out_shape=[
            *halves_shape(dim), shape((total, dim), bf16), shape((total, 6 * HS), bf16),
            shape((total, SIDE), f32),
        ],
        scratch_shapes=[pltpu.VMEM((group_len, EXPERTS * HS), bf16)],
        compiler_params=params(),
        cost_estimate=wall(),
        name="att_fwd",
    )(core_one, group_tokens, w_att, parts1, gain1, cos, sin)
    sent_att = after(sent_att, others[0], chunks[1])
    core_att = sum_core(kept_att, sent_att)
    line_att = after(sum_line(*core_att), cot_zz, others[1])
    sum_att = lax.psum_scatter(line_att, "zz", scatter_dimension=0, tiled=False)

    waited = [chunks[3], others[2], cot_line]
    packed2, middle, gate2 = pl.pallas_call(
        mid_kernel,
        in_specs=[vmem] * 4 + [pl.BlockSpec(memory_space=pl.ANY)] * len(waited),
        out_shape=[shape((rows, wide_cols), bf16), shape((rows, dim), f32), shape((rows, SIDE), f32)],
        compiler_params=params(),
        cost_estimate=wall(),
        name="mid",
    )(sum_att, packed, gain2, parts2, *waited)
    x2 = lax.all_gather(packed2, GROUP, axis=0, tiled=True)

    step = group_len
    steps = (total // step,)
    rows_of = lambda w: pl.BlockSpec((step, w), lambda i, *s: (i, 0))
    side_of = pl.BlockSpec((step, SIDE), lambda i, *s: (i, dim // SIDE))
    fixed = pl.BlockSpec(
        (dim, width), lambda i, *s: (0, 0), pipeline_mode=pl.Buffered(buffer_count=1)
    )
    gate_h, up_h, act = pl.pallas_call(
        ffn_fwd_kernel,
        grid_spec=pltpu.PrefetchScalarGridSpec(
            num_scalar_prefetch=1,
            grid=steps,
            in_specs=[rows_of(wide_cols), fixed, fixed],
            out_specs=[rows_of(width)] * 3,
        ),
        out_shape=[shape((total, width), bf16)] * 3,
        compiler_params=params(),
        cost_estimate=wall(),
        name="ffn_fwd",
    )(zz_one, x2, w_gate, w_up)
    group_cot = gather_core(cot_zz, cot_line)
    down_grad = dot_tn(group_cot, act).astype(bf16)
    down_sent, down_came, down_sum = return_x(down_grad, 2)
    w_down = assemble(chunks[4:], others[4:], act)
    gate_grad, up_grad, part2 = pl.pallas_call(
        ffn_act_kernel,
        grid_spec=pltpu.PrefetchScalarGridSpec(
            num_scalar_prefetch=1,
            grid=steps,
            in_specs=[
                side_of, rows_of(width), rows_of(width), rows_of(dim), fixed, anywhere
            ],
            out_specs=[rows_of(width)] * 2 + [rows_of(SIDE)],
        ),
        out_shape=[shape((total, width), bf16)] * 2 + [shape((total, SIDE), bf16)],
        compiler_params=params(),
        cost_estimate=wall(),
        name="ffn_act",
    )(zz_one, x2, gate_h, up_h, group_cot, w_down, down_grad)
    kept2, sent2 = pl.pallas_call(
        ffn_back_kernel,
        grid=steps,
        in_specs=[smem, rows_of(width), rows_of(width), rows_of(SIDE), fixed, fixed, anywhere],
        out_specs=halves_of(wide_cols),
        out_shape=halves_shape(wide_cols),
        compiler_params=params(),
        cost_estimate=wall(),
        name="ffn_back",
    )(core_one, gate_grad, up_grad, part2, w_gate, w_up, down_came[0])
    core2 = sum_core(kept2, after(sent2, down_came[1]))
    line2 = sum_line(*core2)
    sum_back2 = lax.psum_scatter(line2, "zz", scatter_dimension=0, tiled=False)

    x2_low = x2[:, :dim]
    gate_dw = dot_tn(x2_low, after(gate_grad, core2[0])).astype(bf16)
    up_dw = dot_tn(x2_low, after(up_grad, gate_dw)).astype(bf16)
    gate_sent, gate_came, gate_sum = return_x(gate_dw)
    up_sent, up_came, up_sum = return_x(up_dw)
    down_back = exchange(after(down_sum, core2[0]))
    gate_back = exchange(after(gate_sum, down_back))
    up_back = [exchange(after(up_sum[:, :cut], gate_back))]
    up_back.append(exchange(after(up_sum[:, cut:], up_back[0])))
    part_ffn = dot_nt(after(act, up_dw, line2), w_down).astype(bf16)
    by_rows = part_ffn.reshape(zs, 2, 2, rows, dim)
    sent_ffn = lax.dynamic_index_in_dim(by_rows, 1 - core, 2, keepdims=False)
    core_ffn = fold(by_rows, 2, core, across_core, sent_ffn)
    by_line = fold(after(core_ffn, gate_sum), 1, line, across_line)

    def norm_back(route_at, rsb, wide_rows, base, gain, router, gate, gate_at, outs, name, *waited):
        def pick(a):
            return pl.BlockSpec(a.shape, lambda i, w: (0,) * a.ndim)

        return pl.pallas_call(
            functools.partial(norm_back_kernel, route_at, 1 + len(outs)),
            grid_spec=pltpu.PrefetchScalarGridSpec(
                num_scalar_prefetch=1,
                grid=(1,),
                in_specs=[
                    pick(rsb), pl.BlockSpec((rows, dim), lambda i, w: (0, 0)), pick(base), pick(gain), pick(router),
                    pl.BlockSpec((rows, SIDE), lambda i, w: (w[0], 0)),
                    pl.BlockSpec((rows, SIDE), lambda i, w: (0, dim // SIDE)),
                ]
                + [anywhere] * len(waited),
                out_specs=[pl.BlockSpec((8, dim), lambda i, w: (0, 0))]
                + [pl.BlockSpec((rows, dim), lambda i, w: (0, 0)) for _ in outs],
            ),
            out_shape=[shape((8, dim), f32)] + [shape((rows, dim), d) for d in outs],
            compiler_params=params(),
            cost_estimate=wall(),
            name=name,
        )(gate_at, rsb, wide_rows, base, gain, router, gate, packed, *waited)

    zero = jnp.zeros((1,), jnp.int32)
    parts_ffn, middle_grad, att_cot = norm_back(
        7, sum_back2, middle, cotangent, gain2, router2, gate2, zero, [f32, bf16], "mid_back",
        down_back, gate_sum, sent_ffn,
    )
    group_att_cot = lax.all_gather(att_cot, GROUP, axis=0, tiled=True)

    group_att_cot = after(group_att_cot, gate_back, up_sum, by_line)
    mixed_rows = lax.psum_scatter(
        after(by_line, group_att_cot), "zz", scatter_dimension=0, tiled=False
    )
    kept1, sent1, grad_qkv, z = pl.pallas_call(
        att_bwd_kernel,
        grid=(trees,),
        in_specs=[
            smem, block(dim), whole(w_att), block(6 * HS), block(SIDE),
            pl.BlockSpec((group_len, SIDE), lambda i: (i, dim // SIDE)), whole(cos), whole(sin),
        ],
        out_specs=[*halves_of(wide_cols), block(6 * HS), block(EXPERTS * HS)],
        out_shape=[
            *halves_shape(wide_cols), shape((total, 6 * HS), bf16),
            shape((total, EXPERTS * HS), bf16),
        ],
        scratch_shapes=[pltpu.VMEM((group_len, SIDE), bf16)],
        compiler_params=params(),
        cost_estimate=wall(),
        name="att_bwd",
    )(core_one, group_att_cot, w_att, kept, gate1, group_tokens, cos, sin)
    core1 = sum_core(kept1, after(sent1, up_back[0]))
    grad_att = pl.pallas_call(
        att_grad_kernel,
        grid=(zs,),
        in_specs=[
            pl.BlockSpec((total, dim // zs), lambda i: (0, i)),
            pl.BlockSpec((total, dim // zs), lambda i: (0, i)),
            whole(grad_qkv), whole(z), anywhere,
        ],
        out_specs=pl.BlockSpec((dim // zs, count * HS), lambda i: (i, 0)),
        out_shape=shape((dim, count * HS), bf16),
        compiler_params=params(),
        cost_estimate=cost(2 * total * dim * count * HS, 6 * total * dim),
        name="att_grad",
    )(x1, group_att_cot, grad_qkv, z, core1[0])
    att_sent, att_came, att_sum = return_x(grad_att, 2)
    line1 = sum_line(core1[0], after(core1[1], *att_sent, att_came[0], mixed_rows, up_back[1]))
    sum_back1 = lax.psum_scatter(line1, "zz", scatter_dimension=0, tiled=False)
    att_back = exchange(after(att_sum, up_back[1]))
    ffn_out = jnp.concatenate([v.astype(f32) for v in (gate_back, jnp.concatenate(up_back, axis=1), down_back)], axis=0)

    mixed = (middle + mixed_rows.astype(f32)).astype(bf16)

    parts_att, input_grad = norm_back(
        0, sum_back1, tokens, middle_grad, gain1, router1, gate1,
        (zz * ts + tt)[None].astype(jnp.int32), [bf16], "input_back",
    )

    used = EXPERTS + 1
    parts = jnp.concatenate([parts_ffn[:used], parts_att[:used]], axis=0)
    parts = parts.reshape(2 * used, devices, -1).transpose(1, 0, 2).reshape(devices, -1)
    if xs == 2:
        parts = parts.reshape(zs, xs, 2, 2, -1)

        def halve(v, axis, place, move):
            pick = lambda at: lax.dynamic_index_in_dim(v, at, axis, keepdims=False)
            return pick(place) + move(pick(1 - place))

        parts = halve(parts, 3, core, lambda v: lax.ppermute(v, "tensor", across_core))
        parts = halve(parts, 2, line, lambda v: lax.ppermute(v, "tensor", across_line))
        parts = halve(parts, 1, xx, lambda v: shift(v, "xx", 1, 2))
        turn = lambda k: lax.dynamic_index_in_dim(parts, (zz + k) % zs, 0, keepdims=False)
        came = [shift(turn(k), "zz", k, zs) for k in range(1, zs)]
        parts = functools.reduce(lambda a, b: a + b, came, turn(0))
    else:
        parts = jnp.sum(lax.all_to_all(parts, ALL, 0, 0, tiled=True), axis=0)
    parts = parts.reshape(2, used, -1)
    ffn_router_grad, gain2_grad = parts[0, :EXPERTS].T, parts[0, EXPERTS]
    att_router_grad, gain1_grad = parts[1, :EXPERTS].T, parts[1, EXPERTS]
    query_grad, kv_grad, out_grad = pl.pallas_call(
        join_kernel,
        in_specs=[vmem, anywhere],
        out_specs=[vmem] * 3,
        out_shape=[shape(a.shape, f32) for a in (query_maps, kv_maps, out_maps)],
        compiler_params=params(),
        name="join",
    )(att_back, parts)
    return (
        mixed,
        input_grad,
        gain1_grad,
        gain2_grad,
        att_router_grad,
        query_grad,
        kv_grad,
        out_grad,
        ffn_router_grad,
        ffn_out,
    )


def solution(mesh):
    dp, tensor = mesh.shape["dp"], mesh.shape["tensor"]
    fine = Mesh(mesh.devices.reshape(EXPERTS, dp // EXPERTS, tensor), ALL)
    dps = ("zz", "xx")
    rows, flat, maps = P(ALL, None), P(ALL), P(None, dps, "tensor")
    placed = (
        rows, flat, flat, rows, maps, maps, maps, rows, maps, P(dps, None), P(dps, None), P(dps), rows
    )
    return jax.shard_map(
        local,
        mesh=fine,
        in_specs=placed,
        out_specs=(rows, rows, flat, flat, rows, maps, maps, maps, rows, maps),
        check_vma=False,
    )
```

```python
import functools

import jax
import jax.numpy as jnp
from jax import lax
from jax.experimental import pallas as pl
from jax.experimental.pallas import tpu as pltpu
from jax.sharding import Mesh, PartitionSpec as P

EXPERTS = 4
HS = 128
SEG = 128
SIDE = 128
epsilon = 1e-05
rope_base = 10000.0
f32 = jnp.float32
bf16 = jnp.bfloat16
ALL = ("zz", "xx", "tensor")
GROUP = ("zz", "tensor")
VMEM = 60 * 1024 * 1024


def dot(a, b):
    return lax.dot_general(a, b, (((1,), (0,)), ((), ())), preferred_element_type=f32)


def dot_nt(a, b):
    return lax.dot_general(a, b, (((1,), (1,)), ((), ())), preferred_element_type=f32)


def dot_tn(a, b):
    return lax.dot_general(a, b, (((0,), (0,)), ((), ())), preferred_element_type=f32)


def lanes(rows):
    return lax.broadcasted_iota(jnp.int32, (rows, SIDE), 1).astype(f32)


def put(columns, rows):
    lane = lanes(rows)
    out = jnp.zeros((rows, SIDE), f32)
    for place, column in columns.items():
        out = jnp.where(lane == place, column, out)
    return out


def norm_scale(rows):
    return lax.rsqrt(jnp.mean(rows * rows, axis=-1, keepdims=True) + epsilon)


def gate_probs(low, router_parts, route0, route1):
    rows = low.shape[0]
    parts = dot(low, router_parts)
    lane = lanes(rows)
    logits = (
        parts
        + pltpu.roll(parts, SIDE - EXPERTS, 1)
        + pltpu.roll(parts, SIDE - 2 * EXPERTS, 1)
    )
    c0 = jnp.sum(jnp.where(lane == route0, logits, 0.0), axis=1, keepdims=True)
    c1 = jnp.sum(jnp.where(lane == route1, logits, 0.0), axis=1, keepdims=True)
    top = jnp.maximum(c0, c1)
    e0 = jnp.exp(c0 - top)
    e1 = jnp.exp(c1 - top)
    total = e0 + e1
    return put({0: e0 / total, 1: e1 / total}, rows)


def choose(wide, route):
    out = wide[:, :HS]
    for e in range(1, EXPERTS):
        out = jnp.where(route == e, wide[:, e * HS : (e + 1) * HS], out)
    return out


def spread(slots, routes):
    blocks = []
    for e in range(EXPERTS):
        block = jnp.where(routes[0] == e, slots[0], 0.0)
        blocks.append(block + jnp.where(routes[1] == e, slots[1], 0.0))
    return blocks


def rope_rows(depth, table_ref):
    segments = table_ref.shape[0] // SEG
    out = table_ref[0:SEG, :]
    for d in range(1, segments):
        out = jnp.where(depth == d, table_ref[d * SEG : (d + 1) * SEG, :], out)
    return out


def allow_mask(side, seg):
    rows = side[seg * SEG : (seg + 1) * SEG]
    blocks = [jnp.broadcast_to(rows[:, 2 + b : 3 + b], (SEG, SEG)) for b in range(seg)]
    later = lax.broadcasted_iota(jnp.int32, (SEG, SEG), 1)
    here = lax.broadcasted_iota(jnp.int32, (SEG, SEG), 0)
    blocks.append((later <= here).astype(f32))
    mask = jnp.concatenate(blocks, axis=1) if seg else blocks[0]
    return jnp.concatenate([mask, mask], axis=0)


def weights_of(queries, keys, mask):
    scores = dot_nt(queries, keys) * (HS**-0.5)
    scores = jnp.where(mask > 0.5, scores, -1e30)
    top = jnp.max(scores, axis=-1, keepdims=True)
    exponent = jnp.exp(scores - top)
    return exponent / jnp.sum(exponent, axis=-1, keepdims=True)


def by_core(ref, core):
    half = ref.shape[0] // 4
    parts = []
    for other in range(2):
        for line in range(2):
            first = (2 * line + lax.rem(core + other, 2)) * half
            parts.append(ref[pl.ds(pl.multiple_of(first, half), half), :])
    return jnp.concatenate(parts, axis=0)


def split_rows(value, kept_ref, sent_ref, columns):
    half = value.shape[0] // 4
    for i, ref in enumerate((kept_ref, kept_ref, sent_ref, sent_ref)):
        ref[i % 2, 0, :, columns] = value[i * half : (i + 1) * half]


def pack_kernel(where_ref, parents_ref, tok_ref, att_ref, ffn_ref, out_ref):
    rows = tok_ref.shape[0]
    dim = tok_ref.shape[1]
    out_ref[:, :dim] = tok_ref[...]
    segments = parents_ref.shape[0]
    current = where_ref[0]
    reached = [current == b for b in range(segments)]
    for step in range(segments - 1):
        parent = parents_ref[jnp.maximum(current, 0)]
        current = jnp.where(current > 0, parent, 0)
        reached = [r | (current == b) for b, r in enumerate(reached)]
    flags = [jnp.where(r, 1.0, 0.0) for r in reached]
    depth = functools.reduce(lambda a, b: a + b, flags) - 1.0
    att = att_ref[...].astype(f32)
    ffn = ffn_ref[...].astype(f32)
    columns = {0: att[:, 0:1], 1: att[:, 1:2], 6: depth, 7: ffn[:, 0:1], 8: ffn[:, 1:2]}
    for b in range(segments):
        columns[2 + b] = flags[b]
    out_ref[:, dim:] = put(columns, rows).astype(bf16)


def att_fwd_kernel(
    core_ref, tok_ref, w_ref, router_ref, gain_ref, cos_ref, sin_ref, kept_ref, sent_ref, x_ref,
    keep_ref, gate_ref, z_ref
):
    dim = x_ref.shape[1]
    rows = x_ref.shape[0]
    side = tok_ref[:, dim:].astype(f32)
    wide = tok_ref[:, :dim].astype(f32)
    x = (wide * norm_scale(wide) * gain_ref[...]).astype(bf16)
    x_ref[...] = x
    qkv_width = (EXPERTS + 2) * HS
    qkv = dot(x, w_ref[:, :qkv_width])
    routes = (side[:, 0:1], side[:, 1:2])
    probs = gate_probs(x, router_ref[...], routes[0], routes[1])
    gate_ref[...] = probs
    gates = probs.astype(bf16).astype(f32)
    segments = rows // SEG
    cos, sin = [], []
    for a in range(segments):
        depth = side[a * SEG : (a + 1) * SEG, 6:7]
        cos.append(rope_rows(depth, cos_ref))
        sin.append(rope_rows(depth, sin_ref))
    cos = jnp.concatenate(cos, axis=0)
    sin = jnp.concatenate(sin, axis=0)

    def turn(v):
        return (v * cos + pltpu.roll(v, HS // 2, 1) * sin).astype(bf16)

    q = [turn(choose(qkv, r)) for r in routes]
    k = turn(qkv[:, EXPERTS * HS : (EXPERTS + 1) * HS])
    v = qkv[:, (EXPERTS + 1) * HS :].astype(bf16)
    heads = [[], []]
    for a in range(segments):
        here = slice(a * SEG, (a + 1) * SEG)
        upto = (a + 1) * SEG
        qa = jnp.concatenate([q[0][here], q[1][here]], axis=0)
        p = weights_of(qa, k[:upto], allow_mask(side, a))
        o = dot(p.astype(bf16), v[:upto]).astype(bf16)
        heads[0].append(o[:SEG])
        heads[1].append(o[SEG:])
    heads = [jnp.concatenate(h, axis=0) for h in heads]
    for i, piece in enumerate([q[0], q[1], k, v, heads[0], heads[1]]):
        keep_ref[:, i * HS : (i + 1) * HS] = piece
    gated = [gates[:, s : s + 1] * heads[s].astype(f32) for s in range(2)]
    z_ref[...] = jnp.concatenate([b.astype(bf16) for b in spread(gated, routes)], axis=1)
    part = dot_nt(by_core(z_ref, core_ref[0]), w_ref[:, qkv_width:]).astype(bf16)
    split_rows(part, kept_ref, sent_ref, slice(None))


def att_bwd_kernel(
    core_ref, c_ref, w_ref, keep_ref, gate_ref, side_ref, cos_ref, sin_ref, kept_ref, sent_ref,
    grad_ref, z_ref, part_ref
):
    dim = c_ref.shape[1]
    rows = c_ref.shape[0]
    qkv_width = (EXPERTS + 2) * HS
    side = side_ref[...].astype(f32)
    routes = (side[:, 0:1], side[:, 1:2])
    gates = gate_ref[...].astype(bf16).astype(f32)
    g = dot(c_ref[...], w_ref[:, qkv_width:])
    q = [keep_ref[:, :HS], keep_ref[:, HS : 2 * HS]]
    k = keep_ref[:, 2 * HS : 3 * HS]
    v = keep_ref[:, 3 * HS : 4 * HS]
    heads = [keep_ref[:, 4 * HS : 5 * HS].astype(f32), keep_ref[:, 5 * HS :].astype(f32)]
    chosen = [choose(g, r) for r in routes]
    parts = [jnp.sum(heads[s] * chosen[s], axis=1, keepdims=True) for s in range(2)]
    hg = [(gates[:, s : s + 1] * chosen[s]).astype(bf16) for s in range(2)]
    gated = [gates[:, s : s + 1] * heads[s] for s in range(2)]
    for e, block in enumerate(spread(gated, routes)):
        z_ref[:, e * HS : (e + 1) * HS] = block.astype(bf16)
    segments = rows // SEG
    dk = [jnp.zeros((SEG, HS), f32) for _ in range(segments)]
    dv = [jnp.zeros((SEG, HS), f32) for _ in range(segments)]
    dq = [[], []]
    for a in range(segments):
        here = slice(a * SEG, (a + 1) * SEG)
        upto = (a + 1) * SEG
        qa = jnp.concatenate([q[0][here], q[1][here]], axis=0)
        ha = jnp.concatenate([hg[0][here], hg[1][here]], axis=0)
        p = weights_of(qa, k[:upto], allow_mask(side, a))
        pg = dot_nt(ha, v[:upto])
        sg = (p * (pg - jnp.sum(p * pg, axis=-1, keepdims=True))).astype(bf16)
        dqa = dot(sg, k[:upto]) * (HS**-0.5)
        dq[0].append(dqa[:SEG])
        dq[1].append(dqa[SEG:])
        dka = dot_tn(sg, qa) * (HS**-0.5)
        dva = dot_tn(p.astype(bf16), ha)
        for b in range(a + 1):
            dk[b] = dk[b] + dka[b * SEG : (b + 1) * SEG]
            dv[b] = dv[b] + dva[b * SEG : (b + 1) * SEG]
    cos, sin = [], []
    for a in range(segments):
        depth = side[a * SEG : (a + 1) * SEG, 6:7]
        cos.append(rope_rows(depth, cos_ref))
        sin.append(rope_rows(depth, sin_ref))
    cos = jnp.concatenate(cos, axis=0)
    sin = jnp.concatenate(sin, axis=0)

    def unturn(v):
        return v * cos - pltpu.roll(v, HS // 2, 1) * sin

    dq = [unturn(jnp.concatenate(d, axis=0)) for d in dq]
    blocks = spread(dq, routes) + [unturn(jnp.concatenate(dk, axis=0)), jnp.concatenate(dv, axis=0)]
    grad = jnp.concatenate([b.astype(bf16) for b in blocks], axis=1)
    grad_ref[...] = grad
    part_ref[...] = put({0: parts[0], 1: parts[1]}, rows).astype(bf16)
    core = core_ref[0]
    back = dot_nt(by_core(grad_ref, core), w_ref[:, :qkv_width]).astype(bf16)
    split_rows(back, kept_ref, sent_ref, slice(0, dim))
    split_rows(by_core(part_ref, core), kept_ref, sent_ref, slice(dim, dim + SIDE))


def att_grad_kernel(x_ref, c_ref, grad_ref, z_ref, wait_ref, out_ref):
    width = grad_ref.shape[1]
    out_ref[:, :width] = dot_tn(x_ref[...], grad_ref[...]).astype(bf16)
    out_ref[:, width:] = dot_tn(c_ref[...], z_ref[...]).astype(bf16)


def mid_kernel(rs_ref, packed_ref, gain_ref, router_ref, *refs):
    out_ref, middle_ref, gate_ref = refs[-3:]
    rows, dim = rs_ref.shape
    side = packed_ref[:, dim:].astype(f32)
    middle = packed_ref[:, :dim].astype(f32) + rs_ref[...].astype(f32)
    middle_ref[...] = middle
    low = (middle * norm_scale(middle) * gain_ref[...]).astype(bf16)
    out_ref[:, :dim] = low
    probs = gate_probs(low, router_ref[...], side[:, 7:8], side[:, 8:9])
    gate_ref[...] = probs
    out_ref[:, dim:] = put(
        {0: probs[:, 0:1], 1: probs[:, 1:2], 2: side[:, 7:8], 3: side[:, 8:9]}, rows
    ).astype(bf16)


def norm_back_kernel(
    route_at, outs, where_ref, rsb_ref, rows_ref, base_ref, gain_ref, router_ref, gate_ref, side_ref,
    *refs
):
    out_refs = refs[-outs:]
    count, dim = rows_ref.shape
    grad = rsb_ref[:, :dim].astype(f32)
    gp = rsb_ref[:, dim:].astype(f32)
    side = side_ref[...].astype(f32)
    p0, p1 = gate_ref[:, 0:1], gate_ref[:, 1:2]
    q0, q1 = gp[:, 0:1], gp[:, 1:2]
    inner = p0 * q0 + p1 * q1
    i0, i1 = p0 * (q0 - inner), p1 * (q1 - inner)
    rows = rows_ref[...].astype(f32)
    scale = norm_scale(rows)
    normal = rows * scale
    gain = gain_ref[...]
    low = (normal * gain).astype(bf16).astype(f32)
    route0, route1 = side[:, route_at : route_at + 1], side[:, route_at + 1 : route_at + 2]
    parts = []
    for e in range(EXPERTS):
        logit_grad = jnp.where(route0 == e, i0, 0.0) + jnp.where(route1 == e, i1, 0.0)
        grad = grad + logit_grad * router_ref[e : e + 1, :]
        parts.append(jnp.sum(logit_grad * low, axis=0, keepdims=True))
    parts.append(jnp.sum(grad * normal, axis=0, keepdims=True))
    parts.append(jnp.zeros((8 - len(parts), dim), f32))
    out_refs[0][...] = jnp.concatenate(parts, axis=0)
    weighted = grad * gain
    total = base_ref[...].astype(f32) + scale * (
        weighted - normal * jnp.mean(weighted * normal, axis=-1, keepdims=True)
    )
    for ref in out_refs[1:]:
        ref[...] = total.astype(ref.dtype)


def ffn_coef(side, mine):
    in0, in1 = side[:, 2:3] == mine, side[:, 3:4] == mine
    return in0, in1, jnp.where(in0, side[:, 0:1], 0.0) + jnp.where(in1, side[:, 1:2], 0.0)


def column_chunks(width):
    return [slice(0, width)]


def sigmoid(v):
    return 0.5 * jnp.tanh(0.5 * v) + 0.5


def ffn_fwd_kernel(where_ref, x_ref, wg_ref, wu_ref, gate_ref, up_ref, a_ref):
    dim, width = wg_ref.shape
    side = x_ref[:, dim:].astype(f32)
    coef = ffn_coef(side, where_ref[0].astype(f32))[2]
    x = x_ref[:, :dim]
    for at in column_chunks(width):
        gate = dot(x, wg_ref[:, at])
        up = dot(x, wu_ref[:, at])
        gate_ref[:, at] = gate.astype(bf16)
        up_ref[:, at] = up.astype(bf16)
        a_ref[:, at] = (gate * sigmoid(gate) * up * coef).astype(bf16)


def ffn_act_kernel(
    where_ref, side_ref, gate_ref, up_ref, c_ref, wd_ref, wait_ref, gg_ref, ug_ref, part_ref
):
    rows = c_ref.shape[0]
    in0, in1, coef = ffn_coef(side_ref[...].astype(f32), where_ref[0].astype(f32))
    c = c_ref[...]
    part = jnp.zeros((rows, 1), f32)
    for at in column_chunks(wd_ref.shape[1]):
        gate = gate_ref[:, at].astype(f32)
        up = up_ref[:, at].astype(f32)
        act_grad = dot(c, wd_ref[:, at])
        sig = sigmoid(gate)
        silu = gate * sig
        part = part + jnp.sum(silu * up * act_grad, axis=-1, keepdims=True)
        act_grad = act_grad * coef
        gg_ref[:, at] = (act_grad * up * (sig + silu * (1.0 - sig))).astype(bf16)
        ug_ref[:, at] = (act_grad * silu).astype(bf16)
    part_ref[...] = put(
        {0: jnp.where(in0, part, 0.0), 1: jnp.where(in1, part, 0.0)}, rows
    ).astype(bf16)


def ffn_back_kernel(
    core_ref, gg_ref, ug_ref, part_ref, wg_ref, wu_ref, wait_ref, kept_ref, sent_ref
):
    dim = wg_ref.shape[0]
    core = core_ref[0]
    back = dot_nt(by_core(gg_ref, core), wg_ref[...]) + dot_nt(by_core(ug_ref, core), wu_ref[...])
    split_rows(back.astype(bf16), kept_ref, sent_ref, slice(0, dim))
    split_rows(by_core(part_ref, core), kept_ref, sent_ref, slice(dim, dim + SIDE))


def split_kernel(query_ref, kv_ref, out_ref, *piece_refs):
    cut = piece_refs[0].shape[1]
    for n, piece_ref in enumerate(piece_refs):
        for head in range(piece_ref.shape[0]):
            place = 0
            for ref in (query_ref, kv_ref, out_ref):
                for m in range(ref.shape[0]):
                    rows = ref[m, n * cut : (n + 1) * cut, head * HS : (head + 1) * HS]
                    piece_ref[head, :, place : place + HS] = rows.astype(bf16)
                    place += HS


def cast_kernel(*refs):
    kinds = (len(refs) - 1) // 3
    for kind in range(kinds):
        first, second = refs[kinds + 1 + 2 * kind : kinds + 3 + 2 * kind]
        cut = first.shape[1]
        first[...] = refs[kind][:, :cut].astype(bf16)
        second[...] = refs[kind][:, cut:].astype(bf16)


def join_kernel(piece_ref, wait_ref, *outs):
    for head in range(piece_ref.shape[0]):
        place = 0
        for ref in outs:
            for m in range(ref.shape[0]):
                rows = piece_ref[head, :, place : place + HS]
                ref[m, :, head * HS : (head + 1) * HS] = rows.astype(f32)
                place += HS


def after(value, *waited):
    def body(*refs):
        pass

    anywhere = pl.BlockSpec(memory_space=pl.ANY)
    return pl.pallas_call(
        body,
        in_specs=[anywhere] * (1 + len(waited)),
        out_specs=anywhere,
        out_shape=shape(value.shape, value.dtype),
        input_output_aliases={0: 0},
        cost_estimate=cost(1e6, 1e3),
        name="after",
    )(value, *waited)


def params():
    return pltpu.CompilerParams(vmem_limit_bytes=VMEM)


def cost(flops, nbytes):
    return pl.CostEstimate(flops=int(flops), bytes_accessed=int(nbytes), transcendentals=0)


def wall():
    return cost(2e11, 1e6)


def shape(dims, dtype):
    return jax.ShapeDtypeStruct(dims, dtype)


def whole(array):
    zeros = (0,) * array.ndim
    return pl.BlockSpec(array.shape, lambda *unused: zeros)


def router_parts(router):
    high = lax.reduce_precision(router, 8, 7)
    rest = router - high
    middle = lax.reduce_precision(rest, 8, 7)
    low = rest - middle
    parts = jnp.concatenate([high, middle, low], axis=1)
    return jnp.pad(parts, ((0, 0), (0, SIDE - parts.shape[1]))).astype(bf16)


def shift(value, axis, step, size):
    return lax.ppermute(value, axis, [(i, (i + step) % size) for i in range(size)])


def local(
    tokens, norm_gain1, norm_gain2, att_router, query_maps, kv_maps, out_maps, ffn_router,
    ffn_maps, att_route, ffn_route, parents, cotangent,
):
    rows, dim = tokens.shape
    group_len = att_route.shape[0]
    zz, xx, tt = lax.axis_index("zz"), lax.axis_index("xx"), lax.axis_index("tensor")
    zs, xs, ts = lax.axis_size("zz"), lax.axis_size("xx"), lax.axis_size("tensor")
    here = jnp.stack([tt]).astype(jnp.int32)
    total = rows * zs * ts
    wide_cols = dim + SIDE

    def exchange(value):
        return lax.all_to_all(value, "zz", 0, 0, tiled=True)

    def swap(half):
        return shift(half, "xx", 1, 2) if xs == 2 else half

    def assemble(halves, others, *ready):
        chunks = len(halves)
        part, width = halves[0].shape[1:]
        if xs == 2:
            full = jnp.zeros((zs, xs, chunks, part, width), bf16)
            for n in range(chunks):
                if ready and n == chunks - 1:
                    full = after(full, *ready)
                for piece, column in ((halves[n], xx), (others[n], 1 - xx)):
                    full = lax.dynamic_update_slice(
                        full, piece[:, None, None], (0, column, n, 0, 0)
                    )
        else:
            full = jnp.stack([lax.all_gather(h, "xx", axis=1) for h in halves], axis=2)
        return full.reshape(zs * xs * chunks * part, width)

    core, line = tt % 2, tt // 2
    across_core = [(i, i ^ 1) for i in range(ts)]
    across_line = [(i, i ^ 2) for i in range(ts)]

    def gather_line(mine):
        by_zz = lax.all_gather(mine, "zz", axis=0)
        return by_zz, lax.ppermute(by_zz, "tensor", across_line)

    def gather_core(by_zz, other_line):
        pair = jnp.zeros((zs, 2) + by_zz.shape[1:], by_zz.dtype)
        for piece, place in ((by_zz, line), (other_line, 1 - line)):
            pair = lax.dynamic_update_slice(pair, piece[:, None], (0, place, 0, 0))
        other_core = lax.ppermute(pair, "tensor", across_core)
        full = jnp.zeros((zs, 2, 2) + by_zz.shape[1:], by_zz.dtype)
        for piece, place in ((pair, core), (other_core, 1 - core)):
            full = lax.dynamic_update_slice(full, piece[:, :, None], (0, 0, place, 0, 0))
        return full.reshape(-1, by_zz.shape[-1])

    def fold(value, axis, place, pairs, sent=None):
        if sent is None:
            sent = lax.dynamic_index_in_dim(value, 1 - place, axis, keepdims=False)
        kept = lax.dynamic_index_in_dim(value, place, axis, keepdims=False)
        came = lax.ppermute(sent, "tensor", pairs)
        return (kept.astype(f32) + came.astype(f32)).astype(bf16)

    core_one = jnp.stack([core]).astype(jnp.int32)
    smem = pl.BlockSpec(memory_space=pltpu.SMEM)
    segment = group_len // 4

    def halves_of(w):
        return [pl.BlockSpec((2, 1, segment, w), lambda i, *s: (0, i, 0, 0))] * 2

    def halves_shape(w):
        return [shape((2, zs, segment, w), bf16)] * 2

    def add(one, two):
        return (one.astype(f32) + two.astype(f32)).astype(bf16)

    def sum_core(kept, sent):
        came = lax.ppermute(sent, "tensor", across_core)
        pick = lambda v, place: lax.dynamic_index_in_dim(v, place, 0, keepdims=False)
        return [add(pick(kept, place), pick(came, place)) for place in (1 - line, line)]

    def sum_line(sent, kept):
        return add(kept, lax.ppermute(sent, "tensor", across_line))

    def return_x(grad, parts=1):
        grad = grad.reshape(zs, xs, -1, grad.shape[1])
        halves = [grad[i * zs // parts : (i + 1) * zs // parts] for i in range(parts)]
        if xs != 2:
            came = [
                lax.psum_scatter(h.transpose(1, 0, 2, 3), "xx", scatter_dimension=0, tiled=False)
                for h in halves
            ]
            return halves, came, jnp.concatenate(came, axis=0)
        sent = [lax.dynamic_index_in_dim(h, 1 - xx, 1, keepdims=False) for h in halves]
        came = [shift(h, "xx", 1, 2) for h in sent]
        kept = lax.dynamic_index_in_dim(grad, xx, 1, keepdims=False)
        return sent, came, (kept.astype(f32) + jnp.concatenate(came, 0).astype(f32)).astype(bf16)

    packed = pl.pallas_call(
        pack_kernel,
        grid_spec=pltpu.PrefetchScalarGridSpec(
            num_scalar_prefetch=2,
            grid=(1,),
            in_specs=[
                pl.BlockSpec((rows, dim), lambda i, w, p: (0, 0)),
                pl.BlockSpec((rows, 2), lambda i, w, p: (w[0], 0)),
                pl.BlockSpec((rows, 2), lambda i, w, p: (w[0], 0)),
            ],
            out_specs=pl.BlockSpec((rows, wide_cols), lambda i, w, p: (0, 0)),
        ),
        out_shape=shape((rows, wide_cols), bf16),
        compiler_params=params(),
        name="pack",
    )(here, parents, tokens, att_route, ffn_route)

    group_tokens = lax.all_gather(packed, GROUP, axis=0, tiled=True)
    small = jnp.concatenate(
        [norm_gain1[None], norm_gain2[None], att_router.T, ffn_router.T], axis=0
    )
    devices = zs * xs * ts
    small = jnp.broadcast_to(small.reshape(1, -1), (devices, small.size))
    small = after(small, packed)
    small = lax.all_to_all(small, ALL, 0, 0, tiled=True)
    small = small.reshape(devices, 2 + 2 * EXPERTS, norm_gain1.shape[0])
    small = small.transpose(1, 0, 2).reshape(2 + 2 * EXPERTS, dim)
    gain1, gain2 = small[0:1], small[1:2]
    router1 = jnp.pad(small[2 : 2 + EXPERTS], ((0, 8 - EXPERTS), (0, 0)))
    router2 = jnp.pad(small[2 + EXPERTS :], ((0, 8 - EXPERTS), (0, 0)))
    parts1 = router_parts(small[2 : 2 + EXPERTS].T)
    parts2 = router_parts(small[2 + EXPERTS :].T)

    count = query_maps.shape[0] + kv_maps.shape[0] + out_maps.shape[0]
    part = query_maps.shape[1]
    zz_one = jnp.stack([zz]).astype(jnp.int32)
    vmem = pl.BlockSpec(memory_space=pltpu.VMEM)
    anywhere = pl.BlockSpec(memory_space=pl.ANY)
    cut, width = part // 2, ffn_maps.shape[2]
    by_head = pl.pallas_call(
        split_kernel,
        in_specs=[vmem, vmem, vmem],
        out_specs=[vmem] * 2,
        out_shape=[shape((zs, cut, count * HS), bf16)] * 2,
        compiler_params=params(),
        name="split",
    )(query_maps, kv_maps, out_maps)
    att_first = exchange(after(by_head[0], small))
    att_half = exchange(after(by_head[1], att_first))
    w_att = assemble([att_first, att_half], [swap(att_first), swap(att_half)])

    cast = pl.pallas_call(
        cast_kernel,
        grid=(EXPERTS,),
        in_specs=[
            pl.BlockSpec((1, part, width), lambda i, kind=kind: (kind * EXPERTS + i, 0, 0))
            for kind in range(3)
        ]
        + [anywhere],
        out_specs=[pl.BlockSpec((1, cut, width), lambda i: (i, 0, 0))] * 6,
        out_shape=[shape((EXPERTS, cut, width), bf16)] * 6,
        compiler_params=params(),
        cost_estimate=cost(1e6, 6 * ffn_maps.size),
        name="cast",
    )(ffn_maps, ffn_maps, ffn_maps, by_head[0])
    chunks = []

    def chunk(n, *ready):
        value = exchange(after(cast[n], *ready))
        chunks.append(value)
        others.append(swap(value))

    others = []
    chunk(0, att_half)
    chunk(1, chunks[0])
    cot_zz, cot_line = gather_line(after(cotangent, chunks[0]))
    for n in range(2, 6):
        chunk(n, chunks[-1])
    w_gate, w_up = [assemble(chunks[n : n + 2], others[n : n + 2]) for n in (0, 2)]

    half = HS // 2
    frequency = rope_base ** (-2.0 * jnp.arange(half, dtype=f32) / HS)
    angles = jnp.arange(group_len, dtype=f32)[:, None] * frequency[None, :]
    cosines, sines = jnp.cos(angles), jnp.sin(angles)
    cos = jnp.concatenate([cosines, cosines], axis=1)
    sin = jnp.concatenate([-sines, sines], axis=1)

    trees = total // group_len
    block = lambda width: pl.BlockSpec((group_len, width), lambda i: (i, 0))
    kept_att, sent_att, x1, kept, gate1 = pl.pallas_call(
        att_fwd_kernel,
        grid=(trees,),
        in_specs=[
            smem, block(wide_cols), whole(w_att), whole(parts1), whole(gain1), whole(cos), whole(sin)
        ],
        out_specs=[*halves_of(dim), block(dim), block(6 * HS), block(SIDE)],
        out_shape=[
            *halves_shape(dim), shape((total, dim), bf16), shape((total, 6 * HS), bf16),
            shape((total, SIDE), f32),
        ],
        scratch_shapes=[pltpu.VMEM((group_len, EXPERTS * HS), bf16)],
        compiler_params=params(),
        cost_estimate=wall(),
        name="att_fwd",
    )(core_one, group_tokens, w_att, parts1, gain1, cos, sin)
    sent_att = after(sent_att, others[0], chunks[1])
    core_att = sum_core(kept_att, sent_att)
    line_att = after(sum_line(*core_att), cot_zz, others[1])
    sum_att = lax.psum_scatter(line_att, "zz", scatter_dimension=0, tiled=False)

    waited = [chunks[3], others[2], cot_line]
    packed2, middle, gate2 = pl.pallas_call(
        mid_kernel,
        in_specs=[vmem] * 4 + [pl.BlockSpec(memory_space=pl.ANY)] * len(waited),
        out_shape=[shape((rows, wide_cols), bf16), shape((rows, dim), f32), shape((rows, SIDE), f32)],
        compiler_params=params(),
        cost_estimate=wall(),
        name="mid",
    )(sum_att, packed, gain2, parts2, *waited)
    x2 = lax.all_gather(packed2, GROUP, axis=0, tiled=True)

    step = group_len
    steps = (total // step,)
    rows_of = lambda w: pl.BlockSpec((step, w), lambda i, *s: (i, 0))
    side_of = pl.BlockSpec((step, SIDE), lambda i, *s: (i, dim // SIDE))
    fixed = pl.BlockSpec(
        (dim, width), lambda i, *s: (0, 0), pipeline_mode=pl.Buffered(buffer_count=1)
    )
    gate_h, up_h, act = pl.pallas_call(
        ffn_fwd_kernel,
        grid_spec=pltpu.PrefetchScalarGridSpec(
            num_scalar_prefetch=1,
            grid=steps,
            in_specs=[rows_of(wide_cols), fixed, fixed],
            out_specs=[rows_of(width)] * 3,
        ),
        out_shape=[shape((total, width), bf16)] * 3,
        compiler_params=params(),
        cost_estimate=wall(),
        name="ffn_fwd",
    )(zz_one, x2, w_gate, w_up)
    group_cot = gather_core(cot_zz, cot_line)
    down_grad = dot_tn(group_cot, act).astype(bf16)
    down_sent, down_came, down_sum = return_x(down_grad, 2)
    w_down = assemble(chunks[4:], others[4:], act)
    gate_grad, up_grad, part2 = pl.pallas_call(
        ffn_act_kernel,
        grid_spec=pltpu.PrefetchScalarGridSpec(
            num_scalar_prefetch=1,
            grid=steps,
            in_specs=[
                side_of, rows_of(width), rows_of(width), rows_of(dim), fixed, anywhere
            ],
            out_specs=[rows_of(width)] * 2 + [rows_of(SIDE)],
        ),
        out_shape=[shape((total, width), bf16)] * 2 + [shape((total, SIDE), bf16)],
        compiler_params=params(),
        cost_estimate=wall(),
        name="ffn_act",
    )(zz_one, x2, gate_h, up_h, group_cot, w_down, down_grad)
    kept2, sent2 = pl.pallas_call(
        ffn_back_kernel,
        grid=steps,
        in_specs=[smem, rows_of(width), rows_of(width), rows_of(SIDE), fixed, fixed, anywhere],
        out_specs=halves_of(wide_cols),
        out_shape=halves_shape(wide_cols),
        compiler_params=params(),
        cost_estimate=wall(),
        name="ffn_back",
    )(core_one, gate_grad, up_grad, part2, w_gate, w_up, down_came[0])
    core2 = sum_core(kept2, after(sent2, down_came[1]))
    line2 = sum_line(*core2)
    sum_back2 = lax.psum_scatter(line2, "zz", scatter_dimension=0, tiled=False)

    x2_low = x2[:, :dim]
    gate_dw = dot_tn(x2_low, after(gate_grad, core2[0])).astype(bf16)
    up_dw = dot_tn(x2_low, after(up_grad, gate_dw)).astype(bf16)
    gate_sent, gate_came, gate_sum = return_x(gate_dw)
    up_sent, up_came, up_sum = return_x(up_dw)
    down_back = exchange(after(down_sum, core2[0]))
    gate_back = exchange(after(gate_sum, down_back))
    up_back = [exchange(after(up_sum[:, :cut], gate_back))]
    up_back.append(exchange(after(up_sum[:, cut:], up_back[0])))
    part_ffn = dot_nt(after(act, up_dw, line2), w_down).astype(bf16)
    by_rows = part_ffn.reshape(zs, 2, 2, rows, dim)
    sent_ffn = lax.dynamic_index_in_dim(by_rows, 1 - core, 2, keepdims=False)
    core_ffn = fold(by_rows, 2, core, across_core, sent_ffn)
    by_line = fold(after(core_ffn, gate_sum), 1, line, across_line)

    def norm_back(route_at, rsb, wide_rows, base, gain, router, gate, gate_at, outs, name, *waited):
        def pick(a):
            return pl.BlockSpec(a.shape, lambda i, w: (0,) * a.ndim)

        return pl.pallas_call(
            functools.partial(norm_back_kernel, route_at, 1 + len(outs)),
            grid_spec=pltpu.PrefetchScalarGridSpec(
                num_scalar_prefetch=1,
                grid=(1,),
                in_specs=[
                    pick(rsb), pl.BlockSpec((rows, dim), lambda i, w: (0, 0)), pick(base), pick(gain), pick(router),
                    pl.BlockSpec((rows, SIDE), lambda i, w: (w[0], 0)),
                    pl.BlockSpec((rows, SIDE), lambda i, w: (0, dim // SIDE)),
                ]
                + [anywhere] * len(waited),
                out_specs=[pl.BlockSpec((8, dim), lambda i, w: (0, 0))]
                + [pl.BlockSpec((rows, dim), lambda i, w: (0, 0)) for _ in outs],
            ),
            out_shape=[shape((8, dim), f32)] + [shape((rows, dim), d) for d in outs],
            compiler_params=params(),
            cost_estimate=wall(),
            name=name,
        )(gate_at, rsb, wide_rows, base, gain, router, gate, packed, *waited)

    zero = jnp.zeros((1,), jnp.int32)
    parts_ffn, middle_grad, att_cot = norm_back(
        7, sum_back2, middle, cotangent, gain2, router2, gate2, zero, [f32, bf16], "mid_back",
        down_back, gate_sum, sent_ffn,
    )
    group_att_cot = lax.all_gather(att_cot, GROUP, axis=0, tiled=True)

    group_att_cot = after(group_att_cot, gate_back, up_sum, by_line)
    mixed_rows = lax.psum_scatter(
        after(by_line, group_att_cot), "zz", scatter_dimension=0, tiled=False
    )
    kept1, sent1, grad_qkv, z = pl.pallas_call(
        att_bwd_kernel,
        grid=(trees,),
        in_specs=[
            smem, block(dim), whole(w_att), block(6 * HS), block(SIDE),
            pl.BlockSpec((group_len, SIDE), lambda i: (i, dim // SIDE)), whole(cos), whole(sin),
        ],
        out_specs=[*halves_of(wide_cols), block(6 * HS), block(EXPERTS * HS)],
        out_shape=[
            *halves_shape(wide_cols), shape((total, 6 * HS), bf16),
            shape((total, EXPERTS * HS), bf16),
        ],
        scratch_shapes=[pltpu.VMEM((group_len, SIDE), bf16)],
        compiler_params=params(),
        cost_estimate=wall(),
        name="att_bwd",
    )(core_one, group_att_cot, w_att, kept, gate1, group_tokens, cos, sin)
    core1 = sum_core(kept1, after(sent1, up_back[0]))
    grad_att = pl.pallas_call(
        att_grad_kernel,
        grid=(zs,),
        in_specs=[
            pl.BlockSpec((total, dim // zs), lambda i: (0, i)),
            pl.BlockSpec((total, dim // zs), lambda i: (0, i)),
            whole(grad_qkv), whole(z), anywhere,
        ],
        out_specs=pl.BlockSpec((dim // zs, count * HS), lambda i: (i, 0)),
        out_shape=shape((dim, count * HS), bf16),
        compiler_params=params(),
        cost_estimate=cost(2 * total * dim * count * HS, 6 * total * dim),
        name="att_grad",
    )(x1, group_att_cot, grad_qkv, z, core1[0])
    att_sent, att_came, att_sum = return_x(grad_att, 2)
    line1 = sum_line(core1[0], after(core1[1], *att_sent, att_came[0], mixed_rows, up_back[1]))
    sum_back1 = lax.psum_scatter(line1, "zz", scatter_dimension=0, tiled=False)
    att_back = exchange(after(att_sum, up_back[1]))
    ffn_out = jnp.concatenate([v.astype(f32) for v in (gate_back, jnp.concatenate(up_back, axis=1), down_back)], axis=0)

    mixed = (middle + mixed_rows.astype(f32)).astype(bf16)

    parts_att, input_grad = norm_back(
        0, sum_back1, tokens, middle_grad, gain1, router1, gate1,
        (zz * ts + tt)[None].astype(jnp.int32), [bf16], "input_back",
    )

    used = EXPERTS + 1
    parts = jnp.concatenate([parts_ffn[:used], parts_att[:used]], axis=0)
    parts = parts.reshape(2 * used, devices, -1).transpose(1, 0, 2).reshape(devices, -1)
    if xs == 2:
        parts = parts.reshape(zs, xs, 2, 2, -1)

        def halve(v, axis, place, move):
            pick = lambda at: lax.dynamic_index_in_dim(v, at, axis, keepdims=False)
            return pick(place) + move(pick(1 - place))

        parts = halve(parts, 3, core, lambda v: lax.ppermute(v, "tensor", across_core))
        parts = halve(parts, 2, line, lambda v: lax.ppermute(v, "tensor", across_line))
        parts = halve(parts, 1, xx, lambda v: shift(v, "xx", 1, 2))
        turn = lambda k: lax.dynamic_index_in_dim(parts, (zz + k) % zs, 0, keepdims=False)
        came = [shift(turn(k), "zz", k, zs) for k in range(1, zs)]
        parts = functools.reduce(lambda a, b: a + b, came, turn(0))
    else:
        parts = jnp.sum(lax.all_to_all(parts, ALL, 0, 0, tiled=True), axis=0)
    parts = parts.reshape(2, used, -1)
    ffn_router_grad, gain2_grad = parts[0, :EXPERTS].T, parts[0, EXPERTS]
    att_router_grad, gain1_grad = parts[1, :EXPERTS].T, parts[1, EXPERTS]
    query_grad, kv_grad, out_grad = pl.pallas_call(
        join_kernel,
        in_specs=[vmem, anywhere],
        out_specs=[vmem] * 3,
        out_shape=[shape(a.shape, f32) for a in (query_maps, kv_maps, out_maps)],
        compiler_params=params(),
        name="join",
    )(att_back, parts)
    return (
        mixed,
        input_grad,
        gain1_grad,
        gain2_grad,
        att_router_grad,
        query_grad,
        kv_grad,
        out_grad,
        ffn_router_grad,
        ffn_out,
    )


def solution(mesh):
    dp, tensor = mesh.shape["dp"], mesh.shape["tensor"]
    fine = Mesh(mesh.devices.reshape(EXPERTS, dp // EXPERTS, tensor), ALL)
    dps = ("zz", "xx")
    rows, flat, maps = P(ALL, None), P(ALL), P(None, dps, "tensor")
    placed = (
        rows, flat, flat, rows, maps, maps, maps, rows, maps, P(dps, None), P(dps, None), P(dps), rows
    )
    return jax.shard_map(
        local,
        mesh=fine,
        in_specs=placed,
        out_specs=(rows, rows, flat, flat, rows, maps, maps, maps, rows, maps),
        check_vma=False,
    )
```
